128 devices in a mesh: group: 8 (over x, core), tile: 16 (over y, z).
Axes of the slice: x: 4, y: 4, z: 4, core: 2. Of those that a mesh axis runs over, the one named last changes fastest.
Arguments:
- image: bfloat16 [8, 192, 48, 512], P('group', 'tile'), may hold values from -6 to 6
- grad_out: bfloat16 [8, 192, 48, 512], P('group', 'tile'), may hold values from -6 to 6
- gate: bfloat16 [8, 192, 48], P('group', 'tile'), may hold values from 0.19921875 to 1
- routes: int32 [8, 192, 48, 1], P('group', 'tile'), may hold values from 0 to 15; in each aligned block of 576 rows (0 to 575, 576 to 1151, ..., all dimensions but the last counted through in order) at most 72 rows name the same one
- gain_one: float32 [512], replicated, may hold values from 0.1 to 1.9
- w_qkv: bfloat16 [512, 1536], replicated, may hold values from -0.25 to 0.25
- w_proj: bfloat16 [512, 512], replicated, may hold values from -0.25 to 0.25
- table: float32 [16, 529], replicated, may hold values from -4 to 303
- gain_two: float32 [512], replicated, may hold values from 0.1 to 1.9
- w_fc1: bfloat16 [16, 512, 2048], P('tile'), may hold values from -0.25 to 0.25
- w_fc2: bfloat16 [16, 2048, 512], P('tile'), may hold values from -0.125 to 0.125
Outputs:
- grad_image: bfloat16 [8, 192, 48, 512], P('group', 'tile')
- grad_gate: float32 [8, 192, 48], P('group', 'tile')
- grad_fc1: float32 [16, 512, 2048], P('tile')
- grad_fc2: float32 [16, 2048, 512], P('tile')
- grad_qkv: float32 [512, 1536], replicated
- grad_proj: float32 [512, 512], replicated
- grad_table: float32 [16, 529], replicated
- grad_gain_one: float32 [512], replicated
- grad_gain_two: float32 [512], replicated
The draws below stay inside these ranges and needn't reach their ends.
Inputs may be any that keep to these rules, and one draw needn't show every extreme that they name: `routes`: among the 576 tokens of one image in one band of 12 rows (one tile), no expert is named more than 72 times.
All inputs are finite; a program needn't handle non-finite values.
Results may differ from the reference program's by a relative error of at most 0.035.
Values may be sent and summed in bfloat16 or wider, within the bound.
No kernel may reach another device: no remote copies, remote signals or barrier semaphores. Data moves between devices by JAX's collectives and lax.ppermute only.
A program may use at most 192 MiB of HBM per device.

```python
import functools
import math
import jax
import jax.numpy as jnp
import numpy as np
from jax import lax

C = 512
HEADS = 16
FFN = 2048
WINDOW = 12
SHIFT = 6
EXPERTS = 16
BATCH = 8
HEIGHT = 192
WIDTH = 48
ROWS = 576
CAP = 72
TABLE = 529
N_TILE = 16


def draw_table(key, part):
    key = jax.random.fold_in(key, 11)
    base_key = jax.random.fold_in(key, 0)
    base = jnp.clip(jax.random.normal(base_key, (HEADS, TABLE), jnp.float32), -4.0, 4.0)
    return base


def shard_levels(own_key, shape, cuts, least, top_value):
    loudness = 1.0
    for position, parts in cuts:
        heights = jax.random.uniform(jax.random.fold_in(jax.random.fold_in(own_key, 6), position), (parts,), jnp.float32, least / len(cuts), top_value / len(cuts))
        loudness = loudness * jnp.repeat(jnp.exp(heights), shape[position] // parts).reshape((-1,) + (1,) * (len(shape) - 1 - position))
    return loudness


def routed_block(key, own, number, rows, amount, top, reach, skew):
    order = jax.random.permutation(key, amount)
    heavy_load, common = shares(amount, rows * top, reach, skew, True), shares(amount, rows * top, reach, skew, False)
    places = jnp.arange(amount)

    def named(lengths, turn):
        used = int((lengths > 0).sum())
        fixed = max(1, used // 4)
        moved = fixed + (places - fixed + turn * (used - fixed)) % max(1, amount - fixed)
        return jnp.zeros((amount,), jnp.int32).at[order[jnp.where(places < fixed, places, moved)]].set(jnp.asarray(lengths, jnp.int32))

    lengths = jnp.where(number % 4 == 0, named(heavy_load, number // 4), named(common, number - number // 4 - 1))
    mixed = jax.random.permutation(jax.random.fold_in(own, 3), amount)
    giver, sink = mixed[0:amount // 2 * 2:2], mixed[1:amount // 2 * 2:2]
    margin = jnp.minimum(lengths[giver] - 1, reach - lengths[sink]) // 2
    margin = jnp.where((giver == order[0]) | (sink == order[0]) | (lengths[sink] == 0), 0, jnp.maximum(margin, 0))
    moved = jax.random.randint(jax.random.fold_in(own, 4), (amount // 2,), 0, 1 << 20) % (margin + 1)
    lengths = lengths.at[giver].add(-moved).at[sink].add(moved)
    members = jnp.searchsorted(jnp.cumsum(lengths), jnp.arange(rows * top), side="right").astype(jnp.int32)
    grid = members.reshape(top, rows).T
    grid = grid[jax.random.permutation(jax.random.fold_in(own, 1), rows)]
    turn = jax.random.randint(jax.random.fold_in(own, 2), (rows, 1), 0, top)
    return jnp.take_along_axis(grid, (jnp.arange(top)[None, :] + turn) % top, axis=1)


def shares(amount, total, reach, slope, full):
    loads = [(1 << 20) // math.isqrt(standing ** slope) + 1 for standing in range(1, amount + 1)]
    largest = reach if full else min(reach, max(-(-total // amount), total * loads[0] // sum(loads)))
    least = 1 if total - largest >= amount - 1 else 0
    given, rest = [largest] + [least] * (amount - 1), total - largest - least * (amount - 1)
    while rest > 0:
        candidates = [i for i in range(1, amount) if given[i] < largest] or [i for i in range(1, amount) if given[i] < reach]
        mass, remaining = sum([loads[i] for i in candidates]), rest
        for i in candidates:
            addition = min(reach - given[i], max(1, remaining * loads[i] // mass), rest)
            given[i] = given[i] + addition
            rest = rest - addition
    return np.array(given)


def gaussian(key, shape, width, most, pieces=(), kind=jnp.bfloat16):
    entries = jax.random.normal(key, shape, jnp.float32) * width
    if len(pieces) > 0:
        entries = shard_levels(key, shape, pieces, -0.22, 0.18) * entries
    return jnp.clip(entries, min=-most, max=most).astype(kind)


def setup_inputs(seed: int = 0) -> dict:
    key_of = jax.random.split(jax.random.key(seed), 12)
    image = gaussian(key_of[0], (BATCH, HEIGHT, WIDTH, C), 1.0, 6.0, ((0, 8), (1, 16)))
    grad_out = gaussian(key_of[1], (BATCH, HEIGHT, WIDTH, C), 1.0, 6.0, ((0, 8), (1, 16)))
    gate = jnp.clip(jnp.exp(math.log(1.0) - 1.6133518 * jax.random.uniform(key_of[2], (BATCH, HEIGHT, WIDTH), jnp.float32) ** shard_levels(key_of[2], (BATCH, HEIGHT, WIDTH), ((0, 8), (1, 16)), -0.2, 0.2)), 0.19921875, 1.0).astype(jnp.bfloat16)
    routes_keys = jax.random.split(jax.random.fold_in(key_of[3], 1), BATCH * HEIGHT * WIDTH // ROWS)
    routes_turns = jax.random.permutation(jax.random.fold_in(key_of[3], 3), BATCH * HEIGHT * WIDTH // ROWS)
    routes = jax.vmap(lambda own, number: routed_block(jax.random.fold_in(key_of[3], 2), own, number, ROWS, EXPERTS, 1, CAP, 2))(routes_keys, routes_turns).reshape((BATCH, HEIGHT, WIDTH, 1))
    gain_one = jnp.clip(1.0 + 0.18 * jax.random.normal(key_of[4], (C,), jnp.float32), 0.1, 1.9)
    w_qkv = gaussian(key_of[5], (C, 3 * C), C ** -0.5, 0.25)
    w_proj = gaussian(key_of[6], (C, C), C ** -0.5, 0.25)
    table = draw_table(jax.random.fold_in(key_of[11], 71), 0)
    gain_two = jnp.clip(1.0 + 0.18 * jax.random.normal(key_of[8], (C,), jnp.float32), 0.1, 1.9)
    w_fc1 = gaussian(key_of[9], (EXPERTS, C, FFN), C ** -0.5, 0.25, ((0, 16),))
    w_fc2 = gaussian(key_of[10], (EXPERTS, FFN, C), FFN ** -0.5, 0.125, ((0, 16),))
    return {"image": image, "grad_out": grad_out, "gate": gate, "routes": routes, "gain_one": gain_one, "w_qkv": w_qkv, "w_proj": w_proj, "table": table, "gain_two": gain_two, "w_fc1": w_fc1, "w_fc2": w_fc2}


def relative_index(window):
    grid_rows, grid_cols = np.meshgrid(np.arange(window), np.arange(window), indexing='ij')
    flat_r = grid_rows.reshape(-1)
    flat_c = grid_cols.reshape(-1)
    delta_r = flat_r[:, None] - flat_r[None, :] + window - 1
    delta_c = flat_c[:, None] - flat_c[None, :] + window - 1
    return (delta_r * (2 * window - 1) + delta_c).astype(np.int32)

def layer_norm(values, gain_vec):
    row_mean = lax.optimization_barrier(jnp.mean(values, axis=-1, keepdims=True))
    centred = values - row_mean
    row_var = lax.optimization_barrier(jnp.mean(centred * centred, axis=-1, keepdims=True))
    return centred * lax.rsqrt(row_var + 1e-05) * gain_vec

def gelu_exact(values):
    return 0.5 * values * (1.0 + jax.scipy.special.erf(values * 0.7071067811865476))

def gelu_slope(values):
    cumulative = 0.5 * (1.0 + jax.scipy.special.erf(values * 0.7071067811865476))
    density = jnp.exp(-0.5 * values * values) * 0.3989422804014327
    return cumulative + values * density

def window_masks(row_last, col_windows):
    inner_pos = jnp.arange(WINDOW * WINDOW, dtype=jnp.int32)
    row_in = inner_pos // WINDOW
    col_in = inner_pos % WINDOW
    row_region = jnp.where(row_last[:, None], jnp.where(row_in < SHIFT, 1, 2)[None], 0)
    col_last = jnp.arange(col_windows, dtype=jnp.int32) == col_windows - 1
    col_region = jnp.where(col_last[:, None], jnp.where(col_in < SHIFT, 1, 2)[None], 0)
    region = (row_region[:, None, :] * 3 + col_region[None, :, :]).reshape(-1, WINDOW * WINDOW)
    same = region[:, :, None] == region[:, None, :]
    return jnp.where(same, 0.0, -100.0).astype(jnp.float32)

def to_windows(field_in):
    row_count, col_count, channels = field_in.shape
    blocks = field_in.reshape(row_count // WINDOW, WINDOW, col_count // WINDOW, WINDOW, channels)
    return blocks.transpose(0, 2, 1, 3, 4).reshape(-1, WINDOW * WINDOW, channels)

def from_windows(windows, row_count, col_count):
    channels = windows.shape[-1]
    blocks = windows.reshape(row_count // WINDOW, col_count // WINDOW, WINDOW, WINDOW, channels)
    return blocks.transpose(0, 2, 1, 3, 4).reshape(row_count, col_count, channels)

def core_attention(qkv_act, table, mask_add):
    win_count, win_tokens, triple = qkv_act.shape
    channels = triple // 3
    head_dim = channels // HEADS
    split_qkv = qkv_act.reshape(win_count, win_tokens, 3, HEADS, head_dim).astype(jnp.float32)
    logits = jnp.einsum('nqhd,nkhd->nhqk', split_qkv[:, :, 0], split_qkv[:, :, 1]) * head_dim ** (-0.5)
    rel_bias = jnp.take(table, relative_index(WINDOW), axis=1)
    logits = logits + rel_bias[None] + mask_add[:, None]
    attn_prob = jax.nn.softmax(logits, axis=-1).astype(jnp.bfloat16)
    mixed_heads = jnp.einsum('nhqk,nkhd->nqhd', attn_prob.astype(jnp.float32), split_qkv[:, :, 2])
    return mixed_heads.astype(jnp.bfloat16).reshape(win_count, win_tokens, channels)

def attend_forward(windows, mask_add, gain_one, w_qkv, w_proj, table):
    window_shape = windows.shape
    flat_rows = windows.reshape(-1, window_shape[2]).astype(jnp.float32)
    normed_f, norm_pull = jax.vjp(layer_norm, flat_rows, gain_one)
    normed = normed_f.astype(jnp.bfloat16)
    qkv_act = jnp.dot(normed, w_qkv, preferred_element_type=jnp.float32).astype(jnp.bfloat16)
    qkv_act = qkv_act.reshape(window_shape[0], window_shape[1], -1)
    mixed_heads, core_pull = jax.vjp(functools.partial(core_attention, mask_add=mask_add), qkv_act, table)
    mixed_rows = mixed_heads.reshape(flat_rows.shape[0], -1)
    residual_sum = flat_rows + jnp.dot(mixed_rows, w_proj, preferred_element_type=jnp.float32)
    return (residual_sum, (normed, mixed_rows, norm_pull, core_pull, window_shape))

def attend_backward(stored, cotangent, w_qkv, w_proj, with_weights):
    normed, mixed_rows, norm_pull, core_pull, window_shape = stored
    cot_half = cotangent.astype(jnp.bfloat16)
    grad_mixed = jnp.dot(cot_half, w_proj.T, preferred_element_type=jnp.float32).astype(jnp.bfloat16)
    grad_qkv_act, grad_table = core_pull(grad_mixed.reshape(window_shape))
    grad_qkv_act = grad_qkv_act.reshape(normed.shape[0], -1)
    grad_normed = jnp.dot(grad_qkv_act, w_qkv.T, preferred_element_type=jnp.float32)
    grad_rows, grad_gain = norm_pull(grad_normed)
    result_rows = cotangent + grad_rows
    if with_weights:
        grad_proj = jnp.dot(mixed_rows.T, cot_half, preferred_element_type=jnp.float32)
        grad_qkv = jnp.dot(normed.T, grad_qkv_act, preferred_element_type=jnp.float32)
        return (result_rows, (grad_gain, grad_qkv, grad_proj, grad_table))
    return (result_rows, ())

def expert_pass(block_in, block_grad, block_gate, w_up, w_down):
    pre_act = jnp.dot(block_in, w_up, preferred_element_type=jnp.float32)
    hidden = gelu_exact(pre_act).astype(jnp.bfloat16)
    output = jnp.dot(hidden, w_down, preferred_element_type=jnp.float32)
    grad_output = (block_gate.astype(jnp.float32)[:, None] * block_grad.astype(jnp.float32)).astype(jnp.bfloat16)
    grad_hidden = jnp.dot(grad_output, w_down.T, preferred_element_type=jnp.float32)
    grad_pre = (grad_hidden * gelu_slope(pre_act)).astype(jnp.bfloat16)
    grad_down = jnp.dot(hidden.T, grad_output, preferred_element_type=jnp.float32)
    grad_up = jnp.dot(block_in.T, grad_pre, preferred_element_type=jnp.float32)
    grad_inputs = jnp.dot(grad_pre, w_up.T, preferred_element_type=jnp.float32).astype(jnp.bfloat16)
    return (grad_inputs, output, grad_up, grad_down)

def slot_numbers(route_flat, experts):
    onehot = (route_flat[:, None] == jnp.arange(experts, dtype=jnp.int32)[None]).astype(jnp.int32)
    running = jnp.cumsum(onehot, axis=0)
    return (lax.optimization_barrier(jnp.sum(running * onehot, axis=1)) - 1).astype(jnp.int32)

def reference(image, grad_out, gate, routes, gain_one, w_qkv, w_proj, table, gain_two, w_fc1, w_fc2):
    batch, height, columns, channels = image.shape
    row_windows = height // WINDOW
    col_windows = columns // WINDOW
    mask_add = window_masks(jnp.arange(row_windows, dtype=jnp.int32) == row_windows - 1, col_windows)

    def shifted(picture):
        return to_windows(jnp.roll(picture, (-SHIFT, -SHIFT), (0, 1)))

    def unshift(windows):
        return jnp.roll(from_windows(windows, height, columns), (SHIFT, SHIFT), (0, 1))

    def forward_one(picture):
        windows = shifted(picture)
        residual_sum, stored = attend_forward(windows, mask_add, gain_one, w_qkv, w_proj, table)
        return unshift(residual_sum.reshape(windows.shape))
    after_attn = lax.map(forward_one, image)
    tokens = after_attn.reshape(-1, channels)
    normed_f, norm_pull = jax.vjp(layer_norm, tokens, gain_two)
    inputs = normed_f.astype(jnp.bfloat16)
    blocks_all = batch * N_TILE
    route_flat = routes.reshape(blocks_all, -1)
    slot_ids = jax.vmap(slot_numbers, in_axes=(0, None))(route_flat, EXPERTS)
    source = jnp.arange(blocks_all, dtype=jnp.int32)[:, None]
    positions = ((route_flat * blocks_all + source) * CAP + slot_ids).reshape(-1).astype(jnp.int32)
    total_slots = EXPERTS * blocks_all * CAP
    grad_rows_out = grad_out.reshape(-1, channels)
    buf_in = jnp.zeros((total_slots, channels), jnp.bfloat16).at[positions].set(inputs)
    buf_grad = jnp.zeros((total_slots, channels), jnp.bfloat16).at[positions].set(grad_rows_out)
    buf_gate = jnp.zeros((total_slots,), jnp.bfloat16).at[positions].set(gate.reshape(-1))

    def per_expert(packed):
        block_in, block_grad, block_gate, w_up, w_down = packed
        grad_inputs, output, grad_up, grad_down = expert_pass(block_in, block_grad, block_gate, w_up, w_down)
        scores = lax.optimization_barrier(jnp.sum(block_grad.astype(jnp.float32) * output, axis=1))
        return (grad_inputs, scores, grad_up, grad_down)
    results = lax.map(per_expert, (buf_in.reshape(EXPERTS, -1, channels), buf_grad.reshape(EXPERTS, -1, channels), buf_gate.reshape(EXPERTS, -1), w_fc1, w_fc2))
    grad_inputs = results[0].reshape(total_slots, channels)[positions]
    grad_gate = results[1].reshape(total_slots)[positions].reshape(gate.shape)
    grad_tokens, grad_gain_two = norm_pull(grad_inputs.astype(jnp.float32))
    grad_after = (grad_rows_out.astype(jnp.float32) + grad_tokens).reshape(image.shape)

    def backward_one(running, packed):
        picture, cotangent = packed
        windows = shifted(picture)
        residual_sum, stored = attend_forward(windows, mask_add, gain_one, w_qkv, w_proj, table)
        cot_rows = shifted(cotangent).reshape(-1, channels)
        grad_rows, weight_grads = attend_backward(stored, cot_rows, w_qkv, w_proj, True)
        running = jax.tree.map(jnp.add, running, weight_grads)
        grad_picture = unshift(grad_rows.reshape(windows.shape)).astype(jnp.bfloat16)
        return (running, grad_picture)
    start = (jnp.zeros((channels,), jnp.float32), jnp.zeros((channels, 3 * channels), jnp.float32), jnp.zeros((channels, channels), jnp.float32), jnp.zeros(table.shape, jnp.float32))
    summed, grad_image = lax.scan(backward_one, start, (image, grad_after))
    return (grad_image, grad_gate, results[2], results[3], summed[1], summed[2], summed[3], summed[0], grad_gain_two)
```

```python
import functools

import jax
import jax.numpy as jnp
import numpy as np
from jax import lax
from jax.experimental import pallas as pl
from jax.experimental.pallas import tpu as pltpu
from jax.sharding import PartitionSpec as P

HEADS = 16
WINDOW = 12
SHIFT = 6
TOKENS = WINDOW * WINDOW
HALF = TOKENS // 2
SIDE = 2 * WINDOW - 1
SPAN = 384
TABLE_PAD = 640
SCALE = 32**-0.5
EXPERT_ROWS = 384
TAIL = (
    0.0997355664,
    0.0997364567,
    0.0934658327,
    0.0816079977,
    0.0589507659,
    0.0637694228,
    -0.0318383035,
    0.0957188375,
    -0.0809437035,
    0.0197971106,
)
VMEM_LIMIT = 40 * 1024 * 1024
ATTEND_LIMIT = 60 * 1024 * 1024
F32 = jnp.float32
BF16 = jnp.bfloat16
GROUP = ("x", "core")
SAME_CORE = ("x", "tile")
OWNERS = 64


def nn(a, b):
    return lax.dot_general(a, b, (((1,), (0,)), ((), ())), preferred_element_type=F32)


def nt(a, b):
    return lax.dot_general(a, b, (((1,), (1,)), ((), ())), preferred_element_type=F32)


def tn(a, b):
    return lax.dot_general(a, b, (((0,), (0,)), ((), ())), preferred_element_type=F32)


def call(kernel, outs, *, grid=None, in_specs=None, out_specs=None, scratch=(), cost=None, limit=VMEM_LIMIT):
    extra = {}
    if grid is not None:
        extra = dict(grid=grid, in_specs=in_specs, out_specs=out_specs)
    if cost is not None:
        extra["cost_estimate"] = pl.CostEstimate(flops=cost[0], bytes_accessed=cost[1], transcendentals=cost[2])
    return pl.pallas_call(
        kernel,
        out_shape=outs,
        scratch_shapes=list(scratch),
        compiler_params=pltpu.CompilerParams(vmem_limit_bytes=limit),
        **extra,
    )


def shape(dims, dtype):
    return jax.ShapeDtypeStruct(dims, dtype)


def whole(*dims):
    return pl.BlockSpec(dims, lambda *_: (0,) * len(dims))


def shifted(value, axis, steps):
    count = lax.axis_size(axis)
    pairs = [(source, (source + steps) % count) for source in range(count)]
    return lax.ppermute(value, axis, pairs)


def half_order(col_windows):
    columns = col_windows * WINDOW
    pick = np.zeros((SHIFT * columns, SHIFT * columns), np.float32)
    for win in range(col_windows):
        for row in range(SHIFT):
            for col in range(WINDOW):
                source = row * columns + (win * WINDOW + SHIFT + col) % columns
                pick[win * HALF + row * WINDOW + col, source] = 1.0
    return pick


def bias_targets():
    lane = np.arange(SPAN)
    target = (lane // WINDOW) * SIDE + lane % WINDOW + WINDOW - 1
    return np.where(lane < SIDE * WINDOW, target, -1000).astype(np.int32)[None]


def window_masks(row_last, col_windows):
    inner_pos = jnp.arange(TOKENS, dtype=jnp.int32)
    row_in = inner_pos // WINDOW
    col_in = inner_pos % WINDOW
    row_region = jnp.where(row_last[:, None], jnp.where(row_in < SHIFT, 1, 2)[None], 0)
    col_last = jnp.arange(col_windows, dtype=jnp.int32) == col_windows - 1
    col_region = jnp.where(col_last[:, None], jnp.where(col_in < SHIFT, 1, 2)[None], 0)
    region = (row_region[:, None, :] * 3 + col_region[None, :, :]).reshape(-1, TOKENS)
    same = region[:, :, None] == region[:, None, :]
    return jnp.where(same, 0.0, -100.0).astype(F32)


def normalised(values):
    mean = jnp.mean(values, axis=-1, keepdims=True)
    centred = values - mean
    scale = lax.rsqrt(jnp.mean(centred * centred, axis=-1, keepdims=True) + 1e-05)
    return centred * scale, scale


def norm_backward(unit, scale, grad, gain):
    weighted = grad * gain
    along = jnp.mean(weighted * unit, axis=-1, keepdims=True)
    flat = jnp.mean(weighted, axis=-1, keepdims=True)
    return scale * (weighted - flat - unit * along), jnp.sum(grad * unit, axis=0, keepdims=True)


def normal_of(values):
    bell = jnp.exp(-0.5 * values * values)
    inverse = 1.0 / (1.0 + 0.25 * jnp.abs(values))
    ratio = jnp.full_like(values, TAIL[-1])
    for factor in TAIL[-2::-1]:
        ratio = ratio * inverse + factor
    tail = bell * (ratio * inverse)
    return jnp.where(values < 0.0, tail, 1.0 - tail), bell * 0.3989422804014327


def iota(dims, axis):
    return lax.broadcasted_iota(jnp.int32, dims, axis)


def spread_matrix(targets, col):
    hit = iota((TABLE_PAD, SPAN), 0) == targets - col
    return jnp.where(hit, 1.0, 0.0).astype(BF16)


def pieces_of(value, count):
    parts = []
    for _ in range(count):
        part = value.astype(BF16)
        parts.append(part)
        value = value - part.astype(F32)
    return parts


def route_kernel(capacity, routes_ref, gate_ref, grad_ref, order_ref, send_ref, row_ref, col_ref):
    rows = grad_ref.shape[0]
    slots = send_ref.shape[0]
    routes = routes_ref[...]
    chosen = jnp.where(iota((HEADS, rows), 0) == routes, 1.0, 0.0)
    upto = jnp.where(iota((rows, rows), 0) <= iota((rows, rows), 1), 1.0, 0.0).astype(BF16)
    running = nn(chosen.astype(BF16), upto)
    slot = jnp.sum(running * chosen, axis=0, keepdims=True) - 1.0
    expert = routes.astype(F32)
    place = (expert * capacity + slot).astype(jnp.int32)
    picks = jnp.where(iota((slots, rows), 0) == place, gate_ref[...].astype(F32), 0.0).astype(BF16)
    send_ref[...] = nn(picks, grad_ref[...]).astype(BF16)
    order = order_ref[...]
    both = jnp.concatenate(
        [jnp.broadcast_to(expert, (8, rows)), jnp.broadcast_to(slot, (8, rows))], axis=0
    ).astype(BF16)
    moved = nt(both, order)
    there = moved[0:1] * capacity + moved[8:9]
    row_ref[...] = there.astype(jnp.int32)
    same = iota((rows, rows), 0) == iota((rows, rows), 1)
    col_ref[...] = jnp.sum(jnp.where(same, there, 0.0), axis=1, keepdims=True).astype(jnp.int32)


def bias_kernel(table_ref, targets_ref, bias_ref, spread):
    table = jnp.concatenate(pieces_of(table_ref[...], 3), axis=0)
    for col in range(16):
        part = nn(table, spread_matrix(targets_ref[...], col % WINDOW))
        spread[col] = part[0:HEADS] + part[HEADS : 2 * HEADS] + part[2 * HEADS :]
    for head in range(HEADS):
        rows = spread[:, head, :]
        for row in range(WINDOW):
            start = (WINDOW - 1 - row) * WINDOW
            turned = pltpu.roll(rows, (SPAN - start) % SPAN, 1) if start else rows
            bias_ref[head, row * WINDOW : (row + 1) * WINDOW, :] = turned[:WINDOW, :TOKENS]


def table_kernel(pair_ref, targets_ref, gain_one_ref, gain_two_ref, out_ref, wide, lined):
    wide[...] = jnp.zeros_like(wide)
    for head in range(HEADS):
        wide[:TOKENS, :TOKENS] = pair_ref[head]
        total = wide[(WINDOW - 1) * WINDOW : (WINDOW - 1) * WINDOW + 16, :]
        for row in range(WINDOW - 1):
            start = (WINDOW - 1 - row) * WINDOW
            total = total + pltpu.roll(wide[row * WINDOW : row * WINDOW + 16, :], start, 1)
        lined[head] = total
    grads = jnp.zeros((2 * HEADS, TABLE_PAD), F32)
    for col in range(WINDOW):
        value = jnp.concatenate(pieces_of(lined[:, col, :], 2), axis=0)
        grads = grads + nt(value, spread_matrix(targets_ref[...], col))
    grads = grads[:HEADS] + grads[HEADS:]
    out_ref[...] = jnp.zeros_like(out_ref)
    lines = [grads[head : head + 1, 128 * part : 128 * part + 128] for head in range(HEADS) for part in range(5)]
    for gain_ref in (gain_one_ref, gain_two_ref):
        lines += [gain_ref[:, 128 * part : 128 * part + 128] for part in range(4)]
    for number, line in enumerate(lines):
        high, low = pieces_of(line, 2)
        out_ref[number // 2, number % 2 : number % 2 + 1, :] = high.astype(F32)
        out_ref[number // 2, 2 + number % 2 : 3 + number % 2, :] = low.astype(F32)


def merge_kernel(mine_ref, other_ref, small_ref, out_ref):
    for owner in range(OWNERS):
        both = mine_ref[owner].astype(F32) + other_ref[owner].astype(F32)
        out_ref[owner, :, :512] = both.astype(BF16)
        out_ref[owner, :, 512:] = small_ref[owner].astype(BF16)


def sum_kernel(all_ref, out_ref):
    total = all_ref[0].astype(F32)
    for owner in range(1, OWNERS):
        total = total + all_ref[owner].astype(F32)
    small = total[:, 512:]
    small = small + pltpu.roll(small, 14, 0)
    high = small.astype(BF16).astype(F32)
    low = pltpu.roll(small - high, 2, 0)
    row = iota(small.shape, 0)
    small = jnp.where(row < 2, high, jnp.where(row < 4, low, 0.0))
    total = jnp.concatenate([total[:, :512], small], axis=1).astype(BF16)
    for owner in range(OWNERS):
        out_ref[owner] = total


def unpack_kernel(core_ref, mine_ref, other_ref, qkv_ref, proj_ref, small_ref):
    def place(half_ref, first):
        for row in range(16):
            here = slice(first + 16 * row, first + 16 * row + 16)
            for col in range(4):
                block = half_ref[4 * row + col].astype(F32)
                qkv_ref[here, 384 * col : 384 * col + 384] = block[:, :384]
                proj_ref[here, 128 * col : 128 * col + 128] = block[:, 384:512]

    @pl.when(core_ref[0] == 0)
    def _():
        place(mine_ref, 0)
        place(other_ref, 256)

    @pl.when(core_ref[0] != 0)
    def _():
        place(other_ref, 0)
        place(mine_ref, 256)

    for owner in range(OWNERS):
        small = mine_ref[owner, :, 512:].astype(F32) + other_ref[owner, :, 512:].astype(F32)
        small_ref[owner] = small + pltpu.roll(small, 14, 0)


def attend_kernel(
    image_ref, below_ref, order_ref, gain_ref, w_qkv_ref, w_proj_ref, bias_ref, mask_ref,
    prob_ref, qkv_ref, x_ref, normed_ref, mixed_ref, own_ref, send_ref, blended,
):
    group = pl.program_id(0)
    wins = x_ref.shape[0] // TOKENS
    lanes = iota((TOKENS, 128), 1) // 32

    @pl.when(group == 0)
    def _():
        order = order_ref[...]
        upper = nn(order, image_ref[...])
        lower = nn(order, below_ref[...])
        parts = []
        for win in range(wins):
            parts.append(upper[win * HALF : (win + 1) * HALF])
            parts.append(lower[win * HALF : (win + 1) * HALF])
        x = jnp.concatenate(parts, axis=0)
        x_ref[...] = x.astype(BF16)
        unit, _ = normalised(x)
        normed_ref[...] = (unit * gain_ref[...]).astype(BF16)
        normed = normed_ref[...]
        for pair in range(6):
            act = nn(normed, w_qkv_ref[:, 256 * pair : 256 * pair + 256]).astype(BF16)
            qkv_ref[2 * pair] = act[:, :128]
            qkv_ref[2 * pair + 1] = act[:, 128:]

    for win in range(wins):
        rows = slice(win * TOKENS, (win + 1) * TOKENS)
        query = qkv_ref[group, rows, :]
        key = qkv_ref[4 + group, rows, :]
        value_t = jnp.transpose(qkv_ref[8 + group, rows, :].astype(F32)).astype(BF16)
        mask = mask_ref[int(win == wins - 1)]
        mixes = []
        for head in range(4):
            own = jnp.where(lanes == head, query, jnp.zeros_like(query))
            score = nt(key, own) * SCALE + bias_ref[head] + mask
            score = jnp.exp(score - jnp.max(score, axis=0, keepdims=True))
            prob = (score * (1.0 / jnp.sum(score, axis=0, keepdims=True))).astype(BF16)
            prob_ref[head, win] = prob
            mixes.append(nn(value_t[32 * head : 32 * head + 32], prob))
        mix = jnp.transpose(jnp.concatenate(mixes, axis=0))
        blended[group, rows, :] = mix.astype(BF16)

    @pl.when(group == pl.num_programs(0) - 1)
    def _():
        mixed = jnp.concatenate([blended[i] for i in range(4)], axis=1)
        mixed_ref[...] = mixed
        after = x_ref[...].astype(F32) + nn(mixed, w_proj_ref[...])
        kept = [after[win * TOKENS : win * TOKENS + HALF] for win in range(wins)]
        away = [after[win * TOKENS + HALF : (win + 1) * TOKENS] for win in range(wins)]
        own_ref[...] = jnp.concatenate(kept, axis=0)
        send_ref[...] = jnp.concatenate(away, axis=0).astype(BF16)


def dispatch_kernel(own_ref, above_ref, gain_ref, row_ref, send_ref, after_ref):
    after = jnp.concatenate([above_ref[...].astype(F32), own_ref[...]], axis=0)
    after_ref[...] = after
    unit, _ = normalised(after)
    normed = (unit * gain_ref[...]).astype(BF16)
    picks = iota((send_ref.shape[0], after.shape[0]), 0) == row_ref[...]
    send_ref[...] = nn(jnp.where(picks, 1.0, 0.0).astype(BF16), normed).astype(BF16)


def expert_kernel(in_ref, back_ref, w_up_ref, hidden_ref, pre_ref, out_ref, total, score):
    step = pl.program_id(0)
    rows = in_ref.shape[0]
    width = out_ref.shape[1] - 128

    @pl.when(step == 0)
    def _():
        total[...] = jnp.zeros_like(total)
        score[...] = jnp.zeros_like(score)

    w_up = w_up_ref[...]
    for block in range(rows // EXPERT_ROWS):
        here = slice(block * EXPERT_ROWS, (block + 1) * EXPERT_ROWS)
        pre = nn(in_ref[here, :], w_up)
        cumulative, density = normal_of(pre)
        hidden = (pre * cumulative).astype(BF16)
        back = back_ref[here, :].astype(F32)
        grad = (back * (cumulative + pre * density)).astype(BF16)
        hidden_ref[here, :] = hidden
        pre_ref[here, :] = grad
        product = hidden.astype(F32) * back
        score[here, :] += product[:, :128] + product[:, 128:]
        total[here, :] += nt(grad, w_up)

    @pl.when(step == pl.num_programs(0) - 1)
    def _():
        out_ref[:, :width] = total[...].astype(BF16)
        summed = jnp.sum(score[...], axis=1, keepdims=True)
        high = summed.astype(BF16).astype(F32)
        lane = iota((rows, 128), 1)
        tail = jnp.where(lane == 0, high, jnp.where(lane == 1, summed - high, 0.0))
        out_ref[:, width:] = tail.astype(BF16)


def combine_kernel(
    back_ref, col_ref, after_ref, grad_ref, order_ref, gain_ref, send_ref, own_ref, gain_out_ref, score_ref
):
    rows, width = after_ref.shape
    picks = iota((rows, back_ref.shape[0]), 1) == col_ref[...]
    picks = jnp.where(picks, 1.0, 0.0).astype(BF16)
    back = nn(picks, back_ref[...])
    score_ref[...] = back[:, width:]
    unit, scale = normalised(after_ref[...])
    grad, gain_grad = norm_backward(unit, scale, back[:, :width], gain_ref[...])
    gain_out_ref[...] = gain_grad
    order = order_ref[...]
    half = rows // 2
    send_ref[...] = (nn(order, grad_ref[:half, :]) + grad[:half]).astype(BF16)
    own_ref[...] = nn(order, grad_ref[half:, :]) + grad[half:]


def attend_backward_kernel(
    core_ref, own_ref, below_ref, order_t_ref, gain_ref, w_qkv_ref, w_proj_ref, qkv_ref, x_ref, normed_ref, mixed_ref,
    prob_ref, pair_ref, mine_ref, other_ref, kept_ref, send_ref, gain_out_ref, cotangent, grad_mixed, grad_act,
    grad_qkv, grad_proj,
):
    group = pl.program_id(0)
    rows_all = x_ref.shape[0]
    wins = rows_all // TOKENS
    lanes = iota((TOKENS, 128), 1) // 32

    @pl.when(group == 0)
    def _():
        parts = []
        for win in range(wins):
            parts.append(own_ref[win * HALF : (win + 1) * HALF, :])
            parts.append(below_ref[...].astype(F32)[win * HALF : (win + 1) * HALF, :])
        cot = jnp.concatenate(parts, axis=0)
        cotangent[...] = cot
        mixed = nt(cot.astype(BF16), w_proj_ref[...]).astype(BF16)
        for i in range(4):
            grad_mixed[i] = mixed[:, 128 * i : 128 * i + 128]

    pair_ref[...] = jnp.zeros_like(pair_ref)

    for win in range(wins):
        rows = slice(win * TOKENS, (win + 1) * TOKENS)
        query = qkv_ref[group, rows, :]
        key = qkv_ref[4 + group, rows, :]
        value = qkv_ref[8 + group, rows, :]
        out = grad_mixed[group, rows, :]
        key_t = jnp.transpose(key.astype(F32)).astype(BF16)
        grad_query, grad_key, grad_value = [], None, None
        for head in range(4):
            own_out = jnp.where(lanes == head, out, jnp.zeros_like(out))
            own_query = jnp.where(lanes == head, query, jnp.zeros_like(query))
            half_prob = prob_ref[head, win]
            prob = half_prob.astype(F32)
            grad_prob = nt(value, own_out).astype(BF16).astype(F32)
            weighted = prob * grad_prob
            grad_score = weighted - prob * jnp.sum(weighted, axis=0, keepdims=True)
            pair_ref[head] += grad_score
            half_score = grad_score.astype(BF16)
            part_value = nn(half_prob, own_out)
            part_key = nn(half_score, own_query)
            grad_value = part_value if head == 0 else grad_value + part_value
            grad_key = part_key if head == 0 else grad_key + part_key
            grad_query.append(nn(key_t[32 * head : 32 * head + 32], half_score))
        full_query = jnp.transpose(jnp.concatenate(grad_query, axis=0))
        grad_act[group, rows, :] = (full_query * SCALE).astype(BF16)
        grad_act[4 + group, rows, :] = (grad_key * SCALE).astype(BF16)
        grad_act[8 + group, rows, :] = grad_value.astype(BF16)

    @pl.when(group == pl.num_programs(0) - 1)
    def _():
        act = jnp.concatenate([grad_act[i] for i in range(12)], axis=1)
        normed_t = jnp.transpose(normed_ref[...].astype(F32)).astype(BF16)
        mixed_t = jnp.transpose(mixed_ref[...].astype(F32)).astype(BF16)
        cot = cotangent[...]
        grad_proj[...] = nn(mixed_t, cot.astype(BF16)).astype(BF16)
        grad_qkv[...] = nn(normed_t, act).astype(BF16)

        def scatter(half_ref, first):
            for row in range(16):
                here = slice(first + 16 * row, first + 16 * row + 16)
                for col in range(4):
                    half_ref[4 * row + col, :, :384] = grad_qkv[here, 384 * col : 384 * col + 384]
                    half_ref[4 * row + col, :, 384:] = grad_proj[here, 128 * col : 128 * col + 128]

        @pl.when(core_ref[0] == 0)
        def _():
            scatter(mine_ref, 0)
            scatter(other_ref, 256)

        @pl.when(core_ref[0] != 0)
        def _():
            scatter(other_ref, 0)
            scatter(mine_ref, 256)

        grad_normed = nt(act, w_qkv_ref[...])
        unit, scale = normalised(x_ref[...].astype(F32))
        grad, gain_grad = norm_backward(unit, scale, grad_normed, gain_ref[...])
        gain_out_ref[...] = gain_grad
        total = cot + grad
        kept = [total[win * TOKENS : win * TOKENS + HALF] for win in range(wins)]
        away = [total[win * TOKENS + HALF : (win + 1) * TOKENS] for win in range(wins)]
        order_t = order_t_ref[...]
        kept_ref[...] = nn(order_t, jnp.concatenate(kept, axis=0).astype(BF16)).astype(BF16)
        send_ref[...] = nn(order_t, jnp.concatenate(away, axis=0).astype(BF16)).astype(BF16)


def on_device(
    image, grad_out, gate, routes, gain_one, w_qkv, w_proj, table, gain_two, w_fc1, w_fc2
):
    tile_count = lax.axis_size("tile")
    tile_index = lax.axis_index("tile")
    strip_height, columns, channels = image.shape[1:]
    wins = columns // WINDOW
    rows = strip_height * columns
    half = rows // 2
    capacity = 2 * rows // tile_count
    slots = tile_count * capacity
    ffn = w_fc1.shape[2]
    core = lax.axis_index("core").reshape(1).astype(jnp.int32)
    exchange = functools.partial(lax.all_to_all, split_axis=0, concat_axis=0, tiled=True)
    pick = half_order(wins)
    order = jnp.asarray(pick, BF16)
    order_t = jnp.asarray(pick.T, BF16)
    order_all = jnp.asarray(np.kron(np.eye(2), pick), BF16)
    targets = jnp.asarray(bias_targets())
    gain_one = gain_one.reshape(1, channels)
    gain_two = gain_two.reshape(1, channels)
    image_rows = image.reshape(rows, channels)
    grad_rows = grad_out.reshape(rows, channels)
    gate_row = gate.reshape(1, rows)

    below = shifted(image_rows[:half], "tile", -1)
    send_grad, place_row, place_col = call(
        functools.partial(route_kernel, capacity),
        (shape((slots, channels), BF16), shape((1, rows), jnp.int32), shape((rows, 1), jnp.int32)),
        cost=(700000000, 3000000, 0),
    )(routes.reshape(1, rows), gate_row, grad_rows, order_all)
    recv_grad = exchange(send_grad, "tile")
    bias = call(
        bias_kernel,
        shape((HEADS, TOKENS, TOKENS), F32),
        scratch=[pltpu.VMEM((16, HEADS, SPAN), F32)],
        cost=(400000000, 3000000, 0),
    )(jnp.pad(table, ((0, 0), (0, TABLE_PAD - table.shape[1]))), targets)
    mask = window_masks(jnp.reshape(tile_index == tile_count - 1, (1,)), wins)[wins - 2 :]

    head_block = pl.BlockSpec((4, wins, TOKENS, TOKENS), lambda g: (g, 0, 0, 0))
    pair_block = pl.BlockSpec((4, TOKENS, TOKENS), lambda g: (g, 0, 0))
    prob, qkv_act, windows, normed_one, mixed, own_after, send_after = call(
        attend_kernel,
        (
            shape((HEADS, wins, TOKENS, TOKENS), BF16),
            shape((12, rows, 128), BF16),
            shape((rows, channels), BF16),
            shape((rows, channels), BF16),
            shape((rows, channels), BF16),
            shape((half, channels), F32),
            shape((half, channels), BF16),
        ),
        grid=(4,),
        in_specs=[
            pl.BlockSpec((half, channels), lambda g: (1, 0)),
            whole(half, channels),
            whole(half, half),
            whole(1, channels),
            whole(channels, 3 * channels),
            whole(channels, channels),
            pair_block,
            whole(2, TOKENS, TOKENS),
        ],
        out_specs=(
            head_block,
            whole(12, rows, 128),
            whole(rows, channels),
            whole(rows, channels),
            whole(rows, channels),
            whole(half, channels),
            whole(half, channels),
        ),
        scratch=[pltpu.VMEM((4, rows, 128), BF16)],
        cost=(3000000000, 12000000, 2000000),
        limit=ATTEND_LIMIT,
    )(image_rows, below, order, gain_one, w_qkv, w_proj, bias, mask)

    above = shifted(send_after, "tile", 1)
    send_in, after = call(
        dispatch_kernel,
        (shape((slots, channels), BF16), shape((rows, channels), F32)),
        cost=(700000000, 4000000, 0),
    )(own_after, above, gain_two, place_row)
    recv_in = exchange(send_in, "tile")

    w_up, w_down = w_fc1[0], w_fc2[0]
    grad_hidden = jnp.dot(recv_grad, w_down.T, preferred_element_type=F32).astype(BF16)
    chunk = 256
    strip = pl.BlockSpec((slots, chunk), lambda f: (0, f))
    hidden, grad_pre, send_back = call(
        expert_kernel,
        (
            shape((slots, ffn), BF16),
            shape((slots, ffn), BF16),
            shape((slots, channels + 128), BF16),
        ),
        grid=(ffn // chunk,),
        in_specs=[whole(slots, channels), strip, pl.BlockSpec((channels, chunk), lambda f: (0, f))],
        out_specs=(strip, strip, whole(slots, channels + 128)),
        scratch=[pltpu.VMEM((slots, channels), F32), pltpu.VMEM((slots, 128), F32)],
        cost=(4800000000, 20000000, 5000000),
    )(recv_in, grad_hidden, w_up)
    recv_back = exchange(send_back, "tile")
    grad_up = jnp.dot(recv_in.T, grad_pre, preferred_element_type=F32).astype(BF16)
    grad_down = jnp.dot(hidden.T, recv_grad, preferred_element_type=F32).astype(BF16)
    recv_back, grad_up, grad_down = lax.optimization_barrier((recv_back, grad_up, grad_down))
    summed_up, summed_down = lax.psum((grad_up, grad_down), GROUP)

    send_cot, own_cot, gain_two_part, score = call(
        combine_kernel,
        (
            shape((half, channels), BF16),
            shape((half, channels), F32),
            shape((1, channels), F32),
            shape((rows, 128), F32),
        ),
        cost=(1000000000, 7000000, 0),
    )(recv_back, place_col, after, grad_rows, order, gain_two)
    below_cot = shifted(send_cot, "tile", -1)
    score = (score[:, 0] + score[:, 1]).reshape(2, wins, SHIFT, WINDOW)
    score = score.transpose(0, 2, 1, 3).reshape(strip_height, columns)
    grad_gate = jnp.roll(score, SHIFT, axis=1) / gate[0].astype(F32)

    half_pieces = shape((OWNERS, 16, 512), BF16)
    pair, mine, other, kept, send_up, gain_one_part = call(
        attend_backward_kernel,
        (
            shape((HEADS, TOKENS, TOKENS), F32),
            half_pieces,
            half_pieces,
            shape((half, channels), BF16),
            shape((half, channels), BF16),
            shape((1, channels), F32),
        ),
        grid=(4,),
        in_specs=[
            pl.BlockSpec(memory_space=pltpu.SMEM),
            whole(half, channels),
            whole(half, channels),
            whole(half, half),
            whole(1, channels),
            whole(channels, 3 * channels),
            whole(channels, channels),
            whole(12, rows, 128),
            whole(rows, channels),
            whole(rows, channels),
            whole(rows, channels),
            head_block,
        ],
        out_specs=(
            pair_block,
            whole(OWNERS, 16, 512),
            whole(OWNERS, 16, 512),
            whole(half, channels),
            whole(half, channels),
            whole(1, channels),
        ),
        scratch=[
            pltpu.VMEM((rows, channels), F32),
            pltpu.VMEM((4, rows, 128), BF16),
            pltpu.VMEM((12, rows, 128), BF16),
            pltpu.VMEM((channels, 3 * channels), BF16),
            pltpu.VMEM((channels, channels), BF16),
        ],
        cost=(6000000000, 18000000, 0),
        limit=ATTEND_LIMIT,
    )(core, own_cot, below_cot, order_t, gain_one, w_qkv, w_proj, qkv_act, windows, normed_one, mixed, prob)
    upper = shifted(send_up, "tile", 1)
    other = shifted(other, "core", 1)
    small = call(
        table_kernel,
        shape((OWNERS, 16, 128), F32),
        scratch=[pltpu.VMEM((TOKENS + 16, SPAN), F32), pltpu.VMEM((HEADS, 16, SPAN), F32)],
        cost=(400000000, 3000000, 0),
    )(pair, targets, gain_one_part, gain_two_part)
    pieces = shape((OWNERS, 16, 640), BF16)
    merged = call(merge_kernel, pieces, cost=(0, 4000000, 0))(mine, other, small)
    parts = exchange(merged, SAME_CORE)
    parts, upper = lax.optimization_barrier((parts, upper))
    summed = call(sum_kernel, pieces, cost=(0, 4000000, 0))(parts)
    grad_image = jnp.concatenate([upper, kept], axis=0).reshape(image.shape)
    gathered = exchange(summed, SAME_CORE)
    grad_qkv, grad_proj, small_all = call(
        unpack_kernel,
        (
            shape((channels, 3 * channels), F32),
            shape((channels, channels), F32),
            shape((OWNERS, 16, 128), F32),
        ),
        grid=(1,),
        in_specs=[pl.BlockSpec(memory_space=pltpu.SMEM), whole(OWNERS, 16, 640), whole(OWNERS, 16, 640)],
        out_specs=(whole(channels, 3 * channels), whole(channels, channels), whole(OWNERS, 16, 128)),
        cost=(0, 7000000, 0),
    )(core, gathered, shifted(gathered, "core", 1))
    small_all = small_all[:, :2, :].reshape(2 * OWNERS, 128)
    first = HEADS * TABLE_PAD // 128
    grad_table = small_all[:first].reshape(HEADS, TABLE_PAD)[:, : table.shape[1]]
    grad_gain_one = small_all[first : first + 4].reshape(channels)
    grad_gain_two = small_all[first + 4 : first + 8].reshape(channels)
    return (
        grad_image,
        grad_gate.reshape(1, strip_height, columns),
        summed_up.astype(F32).reshape(1, channels, ffn),
        summed_down.astype(F32).reshape(1, ffn, channels),
        grad_qkv,
        grad_proj,
        grad_table,
        grad_gain_one,
        grad_gain_two,
    )


def solution(mesh):
    devices = mesh.devices
    split = jax.sharding.Mesh(devices.reshape(-1, 2, devices.shape[1]), ("x", "core", "tile"))
    return jax.shard_map(
        on_device,
        mesh=split,
        in_specs=(
            P(GROUP, "tile", None, None),
            P(GROUP, "tile", None, None),
            P(GROUP, "tile", None),
            P(GROUP, "tile", None, None),
            P(),
            P(),
            P(),
            P(),
            P(),
            P("tile", None, None),
            P("tile", None, None),
        ),
        out_specs=(
            P(GROUP, "tile", None, None),
            P(GROUP, "tile", None),
            P("tile", None, None),
            P("tile", None, None),
            P(),
            P(),
            P(),
            P(),
            P(),
        ),
        check_vma=False,
    )
```

```python
import functools

import jax
import jax.numpy as jnp
import numpy as np
from jax import lax
from jax.experimental import pallas as pl
from jax.experimental.pallas import tpu as pltpu
from jax.sharding import PartitionSpec as P

HEADS = 16
WINDOW = 12
SHIFT = 6
TOKENS = WINDOW * WINDOW
HALF = TOKENS // 2
SIDE = 2 * WINDOW - 1
SPAN = 384
TABLE_PAD = 640
SCALE = 32**-0.5
EXPERT_ROWS = 128
TAIL = (
    0.0997355664,
    0.0997364567,
    0.0934658327,
    0.0816079977,
    0.0589507659,
    0.0637694228,
    -0.0318383035,
    0.0957188375,
    -0.0809437035,
    0.0197971106,
)
VMEM_LIMIT = 40 * 1024 * 1024
LARGE_LIMIT = 60 * 1024 * 1024
F32 = jnp.float32
BF16 = jnp.bfloat16
GROUP = ("x", "core")
SAME_CORE = ("x", "tile")
OWNERS = 64
LIGHT = (1000000, 100000, 0)


def nn(a, b):
    return lax.dot_general(a, b, (((1,), (0,)), ((), ())), preferred_element_type=F32)


def nt(a, b):
    return lax.dot_general(a, b, (((1,), (1,)), ((), ())), preferred_element_type=F32)


def tn(a, b):
    return lax.dot_general(a, b, (((0,), (0,)), ((), ())), preferred_element_type=F32)


def call(kernel, outs, *, grid=None, in_specs=None, out_specs=None, scratch=(), cost=None, limit=VMEM_LIMIT, scalars=0):
    extra = dict(scratch_shapes=list(scratch))
    if scalars:
        spec = pltpu.PrefetchScalarGridSpec(
            num_scalar_prefetch=scalars, grid=grid, in_specs=in_specs, out_specs=out_specs, scratch_shapes=list(scratch)
        )
        extra = dict(grid_spec=spec)
    elif grid is not None:
        extra.update(grid=grid, in_specs=in_specs, out_specs=out_specs)
    if cost is not None:
        extra["cost_estimate"] = pl.CostEstimate(flops=cost[0], bytes_accessed=cost[1], transcendentals=cost[2])
    return pl.pallas_call(
        kernel, out_shape=outs, compiler_params=pltpu.CompilerParams(vmem_limit_bytes=limit), **extra
    )


def shape(dims, dtype):
    return jax.ShapeDtypeStruct(dims, dtype)


def whole(*dims):
    return pl.BlockSpec(dims, lambda *_: (0,) * len(dims))


def shifted(value, axis, steps):
    count = lax.axis_size(axis)
    pairs = [(source, (source + steps) % count) for source in range(count)]
    return lax.ppermute(value, axis, pairs)


def half_order(col_windows):
    columns = col_windows * WINDOW
    pick = np.zeros((SHIFT * columns, SHIFT * columns), np.float32)
    for win in range(col_windows):
        for row in range(SHIFT):
            for col in range(WINDOW):
                source = row * columns + (win * WINDOW + SHIFT + col) % columns
                pick[win * HALF + row * WINDOW + col, source] = 1.0
    return pick


def bias_targets():
    lane = np.arange(SPAN)
    target = (lane // WINDOW) * SIDE + lane % WINDOW + WINDOW - 1
    return np.where(lane < SIDE * WINDOW, target, -1000).astype(np.int32)[None]


def window_masks(row_last, col_windows):
    inner_pos = jnp.arange(TOKENS, dtype=jnp.int32)
    row_in = inner_pos // WINDOW
    col_in = inner_pos % WINDOW
    row_region = jnp.where(row_last[:, None], jnp.where(row_in < SHIFT, 1, 2)[None], 0)
    col_last = jnp.arange(col_windows, dtype=jnp.int32) == col_windows - 1
    col_region = jnp.where(col_last[:, None], jnp.where(col_in < SHIFT, 1, 2)[None], 0)
    region = (row_region[:, None, :] * 3 + col_region[None, :, :]).reshape(-1, TOKENS)
    same = region[:, :, None] == region[:, None, :]
    return jnp.where(same, 0.0, -100.0).astype(F32)


def normalised(values):
    mean = jnp.mean(values, axis=-1, keepdims=True)
    centred = values - mean
    scale = lax.rsqrt(jnp.mean(centred * centred, axis=-1, keepdims=True) + 1e-05)
    return centred * scale, scale


def norm_backward(unit, scale, grad, gain):
    weighted = grad * gain
    along = jnp.mean(weighted * unit, axis=-1, keepdims=True)
    flat = jnp.mean(weighted, axis=-1, keepdims=True)
    return scale * (weighted - flat - unit * along), jnp.sum(grad * unit, axis=0, keepdims=True)


def normal_of(values):
    bell = jnp.exp(-0.5 * values * values)
    inverse = pl.reciprocal(1.0 + 0.25 * jnp.abs(values))
    ratio = jnp.full_like(values, TAIL[-1])
    for factor in TAIL[-2::-1]:
        ratio = ratio * inverse + factor
    tail = bell * (ratio * inverse)
    return jnp.where(values < 0.0, tail, 1.0 - tail), bell * 0.3989422804014327


def iota(dims, axis):
    return lax.broadcasted_iota(jnp.int32, dims, axis)


def spread_matrix(targets, col):
    hit = iota((TABLE_PAD, SPAN), 0) == targets - col
    return jnp.where(hit, 1.0, 0.0).astype(BF16)


def pieces_of(value, count):
    parts = []
    for _ in range(count):
        part = value.astype(BF16)
        parts.append(part)
        value = value - part.astype(F32)
    return parts


def route_kernel(capacity, routes_ref, gate_ref, grad_ref, order_ref, send_ref, row_ref, col_ref):
    rows = grad_ref.shape[0]
    slots = send_ref.shape[0]
    routes = routes_ref[...]
    chosen = jnp.where(iota((HEADS, rows), 0) == routes, 1.0, 0.0)
    upto = jnp.where(iota((rows, rows), 0) <= iota((rows, rows), 1), 1.0, 0.0).astype(BF16)
    running = nn(chosen.astype(BF16), upto)
    slot = jnp.sum(running * chosen, axis=0, keepdims=True) - 1.0
    expert = routes.astype(F32)
    place = (expert * capacity + slot).astype(jnp.int32)
    picks = jnp.where(iota((slots, rows), 0) == place, gate_ref[...].astype(F32), 0.0).astype(BF16)
    send_ref[...] = nn(picks, grad_ref[...]).astype(BF16)
    order = order_ref[...]
    both = jnp.concatenate(
        [jnp.broadcast_to(expert, (8, rows)), jnp.broadcast_to(slot, (8, rows))], axis=0
    ).astype(BF16)
    moved = nt(both, order)
    there = moved[0:1] * capacity + moved[8:9]
    row_ref[...] = there.astype(jnp.int32)
    same = iota((rows, rows), 0) == iota((rows, rows), 1)
    col_ref[...] = jnp.sum(jnp.where(same, there, 0.0), axis=1, keepdims=True).astype(jnp.int32)


def bias_kernel(table_ref, targets_ref, bias_ref, spread):
    table = jnp.concatenate(pieces_of(table_ref[...], 3), axis=0)
    for col in range(16):
        part = nn(table, spread_matrix(targets_ref[...], col % WINDOW))
        spread[col] = part[0:HEADS] + part[HEADS : 2 * HEADS] + part[2 * HEADS :]
    for head in range(HEADS):
        rows = spread[:, head, :]
        for row in range(WINDOW):
            start = (WINDOW - 1 - row) * WINDOW
            turned = pltpu.roll(rows, (SPAN - start) % SPAN, 1) if start else rows
            bias_ref[head, row * WINDOW : (row + 1) * WINDOW, :] = turned[:WINDOW, :TOKENS]


def table_kernel(pair_ref, targets_ref, gain_one_ref, gain_two_ref, out_ref, wide, lined):
    wide[...] = jnp.zeros_like(wide)
    for head in range(HEADS):
        wide[:TOKENS, :TOKENS] = pair_ref[head]
        total = wide[(WINDOW - 1) * WINDOW : (WINDOW - 1) * WINDOW + 16, :]
        for row in range(WINDOW - 1):
            start = (WINDOW - 1 - row) * WINDOW
            total = total + pltpu.roll(wide[row * WINDOW : row * WINDOW + 16, :], start, 1)
        lined[head] = total
    grads = jnp.zeros((2 * HEADS, TABLE_PAD), F32)
    for col in range(WINDOW):
        value = jnp.concatenate(pieces_of(lined[:, col, :], 2), axis=0)
        grads = grads + nt(value, spread_matrix(targets_ref[...], col))
    grads = grads[:HEADS] + grads[HEADS:]
    out_ref[...] = jnp.zeros_like(out_ref)
    lines = [grads[head : head + 1, 128 * part : 128 * part + 128] for head in range(HEADS) for part in range(5)]
    for gain_ref in (gain_one_ref, gain_two_ref):
        lines += [gain_ref[:, 128 * part : 128 * part + 128] for part in range(4)]
    for number, line in enumerate(lines):
        high, low = pieces_of(line, 2)
        out_ref[number // 2, number % 2 : number % 2 + 1, :] = high.astype(F32)
        out_ref[number // 2, 2 + number % 2 : 3 + number % 2, :] = low.astype(F32)


def merge_kernel(mine_ref, other_ref, small_ref, out_ref):
    for owner in range(OWNERS):
        both = mine_ref[owner].astype(F32) + other_ref[owner].astype(F32)
        out_ref[owner, :, :512] = both.astype(BF16)
        out_ref[owner, :, 512:] = small_ref[owner].astype(BF16)


def sum_kernel(all_ref, out_ref):
    total = all_ref[0].astype(F32)
    for owner in range(1, OWNERS):
        total = total + all_ref[owner].astype(F32)
    small = total[:, 512:]
    small = small + pltpu.roll(small, 14, 0)
    high = small.astype(BF16).astype(F32)
    low = pltpu.roll(small - high, 2, 0)
    row = iota(small.shape, 0)
    small = jnp.where(row < 2, high, jnp.where(row < 4, low, 0.0))
    total = jnp.concatenate([total[:, :512], small], axis=1).astype(BF16)
    for owner in range(OWNERS):
        out_ref[owner] = total


def unpack_kernel(core_ref, mine_ref, other_ref, qkv_ref, proj_ref, small_ref):
    def place(half_ref, first):
        for row in range(16):
            here = slice(first + 16 * row, first + 16 * row + 16)
            for col in range(4):
                block = half_ref[4 * row + col].astype(F32)
                qkv_ref[here, 384 * col : 384 * col + 384] = block[:, :384]
                proj_ref[here, 128 * col : 128 * col + 128] = block[:, 384:512]

    @pl.when(core_ref[0] == 0)
    def _():
        place(mine_ref, 0)
        place(other_ref, 256)

    @pl.when(core_ref[0] != 0)
    def _():
        place(other_ref, 0)
        place(mine_ref, 256)

    for owner in range(OWNERS):
        small = mine_ref[owner, :, 512:].astype(F32) + other_ref[owner, :, 512:].astype(F32)
        small_ref[owner] = small + pltpu.roll(small, 14, 0)


def attend_kernel(
    image_ref, below_ref, order_ref, gain_ref, w_qkv_ref, w_proj_ref, bias_ref, mask_ref,
    prob_ref, qkv_ref, x_ref, normed_ref, mixed_ref, own_ref, send_ref, blended,
):
    group = pl.program_id(0)
    wins = x_ref.shape[0] // TOKENS
    lanes = iota((TOKENS, 128), 1) // 32

    @pl.when(group == 0)
    def _():
        order = order_ref[...]
        upper = nn(order, image_ref[...])
        lower = nn(order, below_ref[...])
        parts = []
        for win in range(wins):
            parts.append(upper[win * HALF : (win + 1) * HALF])
            parts.append(lower[win * HALF : (win + 1) * HALF])
        x = jnp.concatenate(parts, axis=0)
        x_ref[...] = x.astype(BF16)
        unit, _ = normalised(x)
        normed_ref[...] = (unit * gain_ref[...]).astype(BF16)
        normed = normed_ref[...]
        for pair in range(6):
            act = nn(normed, w_qkv_ref[:, 256 * pair : 256 * pair + 256]).astype(BF16)
            qkv_ref[2 * pair] = act[:, :128]
            qkv_ref[2 * pair + 1] = act[:, 128:]

    def scores_of(win):
        rows = slice(win * TOKENS, (win + 1) * TOKENS)
        query = qkv_ref[group, rows, :]
        key = qkv_ref[4 + group, rows, :]
        return [nt(key, jnp.where(lanes == head, query, jnp.zeros_like(query))) for head in range(4)]

    later = scores_of(0)
    for win in range(wins):
        scores = later
        later = scores_of(win + 1) if win + 1 < wins else None
        rows = slice(win * TOKENS, (win + 1) * TOKENS)
        value_t = jnp.transpose(qkv_ref[8 + group, rows, :].astype(F32)).astype(BF16)
        mask = mask_ref[int(win == wins - 1)]
        mixes = []
        for head in range(4):
            score = scores[head] * SCALE + (bias_ref[head] + mask)
            score = jnp.exp(score - jnp.max(score, axis=0, keepdims=True))
            prob = (score * (1.0 / jnp.sum(score, axis=0, keepdims=True))).astype(BF16)
            prob_ref[head, win] = prob
            mixes.append(nn(value_t[32 * head : 32 * head + 32], prob))
        mix = jnp.transpose(jnp.concatenate(mixes, axis=0))
        blended[group, rows, :] = mix.astype(BF16)

    @pl.when(group == pl.num_programs(0) - 1)
    def _():
        mixed = jnp.concatenate([blended[i] for i in range(4)], axis=1)
        mixed_ref[...] = mixed
        after = x_ref[...].astype(F32) + nn(mixed, w_proj_ref[...])
        kept = [after[win * TOKENS : win * TOKENS + HALF] for win in range(wins)]
        away = [after[win * TOKENS + HALF : (win + 1) * TOKENS] for win in range(wins)]
        own_ref[...] = jnp.concatenate(kept, axis=0)
        send_ref[...] = jnp.concatenate(away, axis=0).astype(BF16)


def weight_kernel(which_ref, pre_ref, hidden_ref, in_ref, grad_ref, *rest):
    out_ref = rest[-1]
    up, down = tn(pre_ref[...], in_ref[...]), tn(hidden_ref[...], grad_ref[...])
    if len(rest) > 1:
        up, down = up + rest[0][0, 0].astype(F32), down + rest[0][0, 1].astype(F32)
    out_ref[0, 0] = up.astype(BF16)
    out_ref[0, 1] = down.astype(BF16)


def weight_grads(which, grad_pre, hidden, recv_in, recv_grad, added=None):
    slots, ffn = hidden.shape
    width = recv_in.shape[1]
    chunk = ffn // 8
    strip = pl.BlockSpec((slots, chunk), lambda s, which: (0, which[0] * 4 + (which[1] + s) % 4))
    block = pl.BlockSpec((1, 2, chunk, width), lambda s, which: (s, 0, 0, 0))
    specs = [strip, strip, whole(slots, width), whole(slots, width)]
    return call(
        weight_kernel,
        shape((4, 2, chunk, width), BF16),
        grid=(4,),
        in_specs=specs + ([block] if added is not None else []),
        out_specs=block,
        scalars=1,
        cost=LIGHT,
    )(which, grad_pre, hidden, recv_in, recv_grad, *(() if added is None else (added,)))


def relay_kernel(part_ref, up_ref, down_ref, next_ref, last_ref):
    next_ref[0] = (part_ref[1, 0].astype(F32) + up_ref[...].astype(F32)).astype(BF16)
    next_ref[1] = part_ref[1, 1]
    last_ref[0] = part_ref[3, 0]
    last_ref[1] = (part_ref[3, 1].astype(F32) + down_ref[...].astype(F32)).astype(BF16)


def owned_kernel(part_ref, left_ref, right_ref, out_ref):
    total = part_ref[0].astype(F32) + left_ref[...].astype(F32) + right_ref[...].astype(F32)
    out_ref[...] = total.astype(BF16)


def assemble_kernel(which_ref, *refs):
    up_ref, down_ref = refs[-2:]
    for core in range(2):
        half = which_ref[0] if core == 0 else 1 - which_ref[0]
        own, left, right, far_up, far_down = refs[5 * core : 5 * core + 5]
        for step, up, down in (
            (0, own.at[0], own.at[1]),
            (3, left.at[0], left.at[1]),
            (1, right.at[0], right.at[1]),
            (2, far_up, far_down),
        ):
            chunk = half * 4 + (which_ref[1] + step) % 4
            here = pl.ds(pl.multiple_of(chunk * 256, 256), 256)
            up_ref[:, here] = jnp.transpose(up[...].astype(F32))
            down_ref[here, :] = down[...].astype(F32)


def dispatch_kernel(own_ref, above_ref, gain_ref, row_ref, send_ref, after_ref):
    after = jnp.concatenate([above_ref[...].astype(F32), own_ref[...]], axis=0)
    after_ref[...] = after
    unit, _ = normalised(after)
    normed = (unit * gain_ref[...]).astype(BF16)
    picks = iota((send_ref.shape[0], after.shape[0]), 0) == row_ref[...]
    send_ref[...] = nn(jnp.where(picks, 1.0, 0.0).astype(BF16), normed).astype(BF16)


def expert_kernel(in_ref, back_ref, w_up_ref, hidden_ref, pre_ref, out_ref, total, score):
    step = pl.program_id(0)
    rows = in_ref.shape[0]
    width = out_ref.shape[1] - 128

    @pl.when(step == 0)
    def _():
        total[...] = jnp.zeros_like(total)
        score[...] = jnp.zeros_like(score)

    w_up = w_up_ref[...]
    blocks = rows // EXPERT_ROWS
    places = [slice(block * EXPERT_ROWS, (block + 1) * EXPERT_ROWS) for block in range(blocks)]
    later = nn(in_ref[places[0], :], w_up)
    for block, here in enumerate(places):
        pre = later
        later = nn(in_ref[places[block + 1], :], w_up) if block + 1 < blocks else None
        cumulative, density = normal_of(pre)
        hidden = (pre * cumulative).astype(BF16)
        back = back_ref[here, :].astype(F32)
        grad = (back * (cumulative + pre * density)).astype(BF16)
        hidden_ref[here, :] = hidden
        pre_ref[here, :] = grad
        product = hidden.astype(F32) * back
        score[here, :] += product[:, :128] + product[:, 128:]
        total[here, :] += nt(grad, w_up)

    @pl.when(step == pl.num_programs(0) - 1)
    def _():
        out_ref[:, :width] = total[...].astype(BF16)
        summed = jnp.sum(score[...], axis=1, keepdims=True)
        high = summed.astype(BF16).astype(F32)
        lane = iota((rows, 128), 1)
        tail = jnp.where(lane == 0, high, jnp.where(lane == 1, summed - high, 0.0))
        out_ref[:, width:] = tail.astype(BF16)


def combine_kernel(
    back_ref, col_ref, after_ref, grad_ref, order_ref, gain_ref, send_ref, own_ref, gain_out_ref, score_ref
):
    rows, width = after_ref.shape
    picks = iota((rows, back_ref.shape[0]), 1) == col_ref[...]
    picks = jnp.where(picks, 1.0, 0.0).astype(BF16)
    back = nn(picks, back_ref[...])
    score_ref[...] = back[:, width:]
    unit, scale = normalised(after_ref[...])
    grad, gain_grad = norm_backward(unit, scale, back[:, :width], gain_ref[...])
    gain_out_ref[...] = gain_grad
    order = order_ref[...]
    half = rows // 2
    send_ref[...] = (nn(order, grad_ref[:half, :]) + grad[:half]).astype(BF16)
    own_ref[...] = nn(order, grad_ref[half:, :]) + grad[half:]


def attend_backward_kernel(
    core_ref, own_ref, below_ref, order_t_ref, gain_ref, w_qkv_ref, w_proj_ref, qkv_ref, x_ref, normed_ref, mixed_ref,
    prob_ref, pair_ref, mine_ref, other_ref, kept_ref, send_ref, gain_out_ref, cotangent, grad_mixed, grad_act,
    grad_qkv, grad_proj,
):
    group = pl.program_id(0)
    rows_all = x_ref.shape[0]
    wins = rows_all // TOKENS
    lanes = iota((TOKENS, 128), 1) // 32

    @pl.when(group == 0)
    def _():
        parts = []
        for win in range(wins):
            parts.append(own_ref[win * HALF : (win + 1) * HALF, :])
            parts.append(below_ref[...].astype(F32)[win * HALF : (win + 1) * HALF, :])
        cot = jnp.concatenate(parts, axis=0)
        cotangent[...] = cot
        mixed = nt(cot.astype(BF16), w_proj_ref[...]).astype(BF16)
        for i in range(4):
            grad_mixed[i] = mixed[:, 128 * i : 128 * i + 128]

    pair_ref[...] = jnp.zeros_like(pair_ref)

    def first_part(win):
        rows = slice(win * TOKENS, (win + 1) * TOKENS)
        value = qkv_ref[8 + group, rows, :]
        out = grad_mixed[group, rows, :]
        grad_probs, grad_value = [], None
        for head in range(4):
            own_out = jnp.where(lanes == head, out, jnp.zeros_like(out))
            grad_probs.append(nt(value, own_out))
            part = nn(prob_ref[head, win], own_out)
            grad_value = part if head == 0 else grad_value + part
        grad_act[8 + group, rows, :] = grad_value.astype(BF16)
        return grad_probs

    later = first_part(0)
    for win in range(wins):
        grad_probs = later
        later = first_part(win + 1) if win + 1 < wins else None
        rows = slice(win * TOKENS, (win + 1) * TOKENS)
        query = qkv_ref[group, rows, :]
        key_t = jnp.transpose(qkv_ref[4 + group, rows, :].astype(F32)).astype(BF16)
        grad_query, grad_key = [], None
        for head in range(4):
            own_query = jnp.where(lanes == head, query, jnp.zeros_like(query))
            prob = prob_ref[head, win].astype(F32)
            grad_prob = grad_probs[head].astype(BF16).astype(F32)
            weighted = prob * grad_prob
            grad_score = weighted - prob * jnp.sum(weighted, axis=0, keepdims=True)
            pair_ref[head] += grad_score
            half_score = grad_score.astype(BF16)
            part = nn(half_score, own_query)
            grad_key = part if head == 0 else grad_key + part
            grad_query.append(nn(key_t[32 * head : 32 * head + 32], half_score))
        full_query = jnp.transpose(jnp.concatenate(grad_query, axis=0))
        grad_act[group, rows, :] = (full_query * SCALE).astype(BF16)
        grad_act[4 + group, rows, :] = (grad_key * SCALE).astype(BF16)

    @pl.when(group == pl.num_programs(0) - 1)
    def _():
        act = jnp.concatenate([grad_act[i] for i in range(12)], axis=1)
        normed_t = jnp.transpose(normed_ref[...].astype(F32)).astype(BF16)
        mixed_t = jnp.transpose(mixed_ref[...].astype(F32)).astype(BF16)
        cot = cotangent[...]
        grad_proj[...] = nn(mixed_t, cot.astype(BF16)).astype(BF16)
        grad_qkv[...] = nn(normed_t, act).astype(BF16)

        def scatter(half_ref, first):
            for row in range(16):
                here = slice(first + 16 * row, first + 16 * row + 16)
                for col in range(4):
                    half_ref[4 * row + col, :, :384] = grad_qkv[here, 384 * col : 384 * col + 384]
                    half_ref[4 * row + col, :, 384:] = grad_proj[here, 128 * col : 128 * col + 128]

        @pl.when(core_ref[0] == 0)
        def _():
            scatter(mine_ref, 0)
            scatter(other_ref, 256)

        @pl.when(core_ref[0] != 0)
        def _():
            scatter(other_ref, 0)
            scatter(mine_ref, 256)

        grad_normed = nt(act, w_qkv_ref[...])
        unit, scale = normalised(x_ref[...].astype(F32))
        grad, gain_grad = norm_backward(unit, scale, grad_normed, gain_ref[...])
        gain_out_ref[...] = gain_grad
        total = cot + grad
        kept = [total[win * TOKENS : win * TOKENS + HALF] for win in range(wins)]
        away = [total[win * TOKENS + HALF : (win + 1) * TOKENS] for win in range(wins)]
        order_t = order_t_ref[...]
        kept_ref[...] = nn(order_t, jnp.concatenate(kept, axis=0).astype(BF16)).astype(BF16)
        send_ref[...] = nn(order_t, jnp.concatenate(away, axis=0).astype(BF16)).astype(BF16)


def on_device(
    image, grad_out, gate, routes, gain_one, w_qkv, w_proj, table, gain_two, w_fc1, w_fc2
):
    tile_count = lax.axis_size("tile")
    tile_index = lax.axis_index("tile")
    strip_height, columns, channels = image.shape[1:]
    wins = columns // WINDOW
    rows = strip_height * columns
    half = rows // 2
    capacity = 2 * rows // tile_count
    slots = tile_count * capacity
    ffn = w_fc1.shape[2]
    core = lax.axis_index("core").reshape(1).astype(jnp.int32)
    exchange = functools.partial(lax.all_to_all, split_axis=0, concat_axis=0, tiled=True)
    pick = half_order(wins)
    order = jnp.asarray(pick, BF16)
    order_t = jnp.asarray(pick.T, BF16)
    order_all = jnp.asarray(np.kron(np.eye(2), pick), BF16)
    targets = jnp.asarray(bias_targets())
    gain_one = gain_one.reshape(1, channels)
    gain_two = gain_two.reshape(1, channels)
    image_rows = image.reshape(rows, channels)
    grad_rows = grad_out.reshape(rows, channels)
    gate_row = gate.reshape(1, rows)

    below = shifted(image_rows[:half], "tile", -1)
    send_grad, place_row, place_col = call(
        functools.partial(route_kernel, capacity),
        (shape((slots, channels), BF16), shape((1, rows), jnp.int32), shape((rows, 1), jnp.int32)),
        cost=(700000000, 3000000, 0),
    )(routes.reshape(1, rows), gate_row, grad_rows, order_all)
    recv_grad = exchange(send_grad, "tile")
    bias = call(
        bias_kernel,
        shape((HEADS, TOKENS, TOKENS), F32),
        scratch=[pltpu.VMEM((16, HEADS, SPAN), F32)],
        cost=(400000000, 3000000, 0),
    )(jnp.pad(table, ((0, 0), (0, TABLE_PAD - table.shape[1]))), targets)
    mask = window_masks(jnp.reshape(tile_index == tile_count - 1, (1,)), wins)[wins - 2 :]

    head_block = pl.BlockSpec((4, wins, TOKENS, TOKENS), lambda g: (g, 0, 0, 0))
    pair_block = pl.BlockSpec((4, TOKENS, TOKENS), lambda g: (g, 0, 0))
    prob, qkv_act, windows, normed_one, mixed, own_after, send_after = call(
        attend_kernel,
        (
            shape((HEADS, wins, TOKENS, TOKENS), BF16),
            shape((12, rows, 128), BF16),
            shape((rows, channels), BF16),
            shape((rows, channels), BF16),
            shape((rows, channels), BF16),
            shape((half, channels), F32),
            shape((half, channels), BF16),
        ),
        grid=(4,),
        in_specs=[
            pl.BlockSpec((half, channels), lambda g: (1, 0)),
            whole(half, channels),
            whole(half, half),
            whole(1, channels),
            whole(channels, 3 * channels),
            whole(channels, channels),
            pair_block,
            whole(2, TOKENS, TOKENS),
        ],
        out_specs=(
            head_block,
            whole(12, rows, 128),
            whole(rows, channels),
            whole(rows, channels),
            whole(rows, channels),
            whole(half, channels),
            whole(half, channels),
        ),
        scratch=[pltpu.VMEM((4, rows, 128), BF16)],
        cost=(3000000000, 12000000, 2000000),
        limit=LARGE_LIMIT,
    )(image_rows, below, order, gain_one, w_qkv, w_proj, bias, mask)

    above = shifted(send_after, "tile", 1)
    send_in, after = call(
        dispatch_kernel,
        (shape((slots, channels), BF16), shape((rows, channels), F32)),
        cost=(700000000, 4000000, 0),
    )(own_after, above, gain_two, place_row)
    recv_in = exchange(send_in, "tile")

    w_up, w_down = w_fc1[0], w_fc2[0]
    grad_hidden = jnp.dot(recv_grad, w_down.T, preferred_element_type=F32).astype(BF16)
    chunk = 256
    strip = pl.BlockSpec((slots, chunk), lambda f: (0, f))
    hidden, grad_pre, send_back = call(
        expert_kernel,
        (
            shape((slots, ffn), BF16),
            shape((slots, ffn), BF16),
            shape((slots, channels + 128), BF16),
        ),
        grid=(ffn // chunk,),
        in_specs=[whole(slots, channels), strip, pl.BlockSpec((channels, chunk), lambda f: (0, f))],
        out_specs=(strip, strip, whole(slots, channels + 128)),
        scratch=[pltpu.VMEM((slots, channels), F32), pltpu.VMEM((slots, 128), F32)],
        cost=(4800000000, 20000000, 5000000),
        limit=LARGE_LIMIT,
    )(recv_in, grad_hidden, w_up)
    recv_back = exchange(send_back, "tile")
    place_x = lax.axis_index("x").astype(jnp.int32)
    mine_at = jnp.stack([core[0], place_x])
    other_at = jnp.stack([1 - core[0], place_x])
    other_part = weight_grads(other_at, grad_pre, hidden, recv_in, recv_grad)
    other_part = shifted(other_part, "core", 1)
    mine_part = weight_grads(mine_at, grad_pre, hidden, recv_in, recv_grad, other_part)
    far_up = shifted(mine_part[2, 0], "x", 1)
    far_down = shifted(mine_part[2, 1], "x", -1)
    recv_back, mine_part, far_up, far_down = lax.optimization_barrier((recv_back, mine_part, far_up, far_down))
    chunk = shape(mine_part.shape[1:], BF16)
    to_right, to_left = call(relay_kernel, (chunk, chunk), cost=LIGHT)(mine_part, far_up, far_down)
    from_left, from_right = shifted(to_right, "x", 1), shifted(to_left, "x", -1)

    send_cot, own_cot, gain_two_part, score = call(
        combine_kernel,
        (
            shape((half, channels), BF16),
            shape((half, channels), F32),
            shape((1, channels), F32),
            shape((rows, 128), F32),
        ),
        cost=LIGHT,
    )(recv_back, place_col, after, grad_rows, order, gain_two)
    below_cot = shifted(send_cot, "tile", -1)
    below_cot, from_left, from_right = lax.optimization_barrier((below_cot, from_left, from_right))
    owned = call(owned_kernel, chunk, cost=LIGHT)(mine_part, from_left, from_right)
    below_cot, owned = lax.optimization_barrier((below_cot, owned))
    left, right = shifted(owned, "x", 1), shifted(owned, "x", -1)
    score = (score[:, 0] + score[:, 1]).reshape(2, wins, SHIFT, WINDOW)
    score = score.transpose(0, 2, 1, 3).reshape(strip_height, columns)
    grad_gate = jnp.roll(score, SHIFT, axis=1) / gate[0].astype(F32)

    half_pieces = shape((OWNERS, 16, 512), BF16)
    pair, mine, other, kept, send_up, gain_one_part = call(
        attend_backward_kernel,
        (
            shape((HEADS, TOKENS, TOKENS), F32),
            half_pieces,
            half_pieces,
            shape((half, channels), BF16),
            shape((half, channels), BF16),
            shape((1, channels), F32),
        ),
        grid=(4,),
        in_specs=[
            pl.BlockSpec(memory_space=pltpu.SMEM),
            whole(half, channels),
            whole(half, channels),
            whole(half, half),
            whole(1, channels),
            whole(channels, 3 * channels),
            whole(channels, channels),
            whole(12, rows, 128),
            whole(rows, channels),
            whole(rows, channels),
            whole(rows, channels),
            head_block,
        ],
        out_specs=(
            pair_block,
            whole(OWNERS, 16, 512),
            whole(OWNERS, 16, 512),
            whole(half, channels),
            whole(half, channels),
            whole(1, channels),
        ),
        scratch=[
            pltpu.VMEM((rows, channels), F32),
            pltpu.VMEM((4, rows, 128), BF16),
            pltpu.VMEM((12, rows, 128), BF16),
            pltpu.VMEM((channels, 3 * channels), BF16),
            pltpu.VMEM((channels, channels), BF16),
        ],
        cost=LIGHT,
        limit=LARGE_LIMIT,
    )(core, own_cot, below_cot, order_t, gain_one, w_qkv, w_proj, qkv_act, windows, normed_one, mixed, prob)
    pair, mine, other, send_up, gain_one_part, left, right = lax.optimization_barrier(
        (pair, mine, other, send_up, gain_one_part, left, right)
    )
    upper = shifted(send_up, "tile", 1)
    other = shifted(other, "core", 1)
    small = call(
        table_kernel,
        shape((OWNERS, 16, 128), F32),
        scratch=[pltpu.VMEM((TOKENS + 16, SPAN), F32), pltpu.VMEM((HEADS, 16, SPAN), F32)],
        cost=LIGHT,
    )(pair, targets, gain_one_part, gain_two_part)
    upper, other, small = lax.optimization_barrier((upper, other, small))
    pieces = shape((OWNERS, 16, 640), BF16)
    merged = call(merge_kernel, pieces, cost=(0, 4000000, 0))(mine, other, small)
    parts = exchange(merged, SAME_CORE)
    far_up, far_down = shifted(left[0], "x", 1), shifted(right[1], "x", -1)
    parts, far_up, far_down = lax.optimization_barrier((parts, far_up, far_down))
    summed = call(sum_kernel, pieces, cost=LIGHT)(parts)
    chunks = [owned, left, right, far_up, far_down]
    chunks = chunks + [shifted(value, "core", 1) for value in chunks]
    grad_image = jnp.concatenate([upper, kept], axis=0).reshape(image.shape)
    summed_up, summed_down = call(
        assemble_kernel,
        (shape((channels, ffn), F32), shape((ffn, channels), F32)),
        grid=(1,),
        in_specs=[pl.BlockSpec(memory_space=pltpu.SMEM)] + ([whole(*chunk.shape)] * 3 + [whole(*chunk.shape[1:])] * 2) * 2,
        out_specs=(whole(channels, ffn), whole(ffn, channels)),
        cost=LIGHT,
    )(mine_at, *chunks)
    gathered = exchange(summed, SAME_CORE)
    gathered, summed_up, summed_down, grad_image = lax.optimization_barrier(
        (gathered, summed_up, summed_down, grad_image)
    )
    grad_qkv, grad_proj, small_all = call(
        unpack_kernel,
        (
            shape((channels, 3 * channels), F32),
            shape((channels, channels), F32),
            shape((OWNERS, 16, 128), F32),
        ),
        grid=(1,),
        in_specs=[pl.BlockSpec(memory_space=pltpu.SMEM), whole(OWNERS, 16, 640), whole(OWNERS, 16, 640)],
        out_specs=(whole(channels, 3 * channels), whole(channels, channels), whole(OWNERS, 16, 128)),
        cost=(0, 7000000, 0),
    )(core, gathered, shifted(gathered, "core", 1))
    small_all = small_all[:, :2, :].reshape(2 * OWNERS, 128)
    first = HEADS * TABLE_PAD // 128
    grad_table = small_all[:first].reshape(HEADS, TABLE_PAD)[:, : table.shape[1]]
    grad_gain_one = small_all[first : first + 4].reshape(channels)
    grad_gain_two = small_all[first + 4 : first + 8].reshape(channels)
    return (
        grad_image,
        grad_gate.reshape(1, strip_height, columns),
        summed_up.reshape(1, channels, ffn),
        summed_down.reshape(1, ffn, channels),
        grad_qkv,
        grad_proj,
        grad_table,
        grad_gain_one,
        grad_gain_two,
    )


def solution(mesh):
    devices = mesh.devices
    split = jax.sharding.Mesh(devices.reshape(-1, 2, devices.shape[1]), ("x", "core", "tile"))
    return jax.shard_map(
        on_device,
        mesh=split,
        in_specs=(
            P(GROUP, "tile", None, None),
            P(GROUP, "tile", None, None),
            P(GROUP, "tile", None),
            P(GROUP, "tile", None, None),
            P(),
            P(),
            P(),
            P(),
            P(),
            P("tile", None, None),
            P("tile", None, None),
        ),
        out_specs=(
            P(GROUP, "tile", None, None),
            P(GROUP, "tile", None),
            P("tile", None, None),
            P("tile", None, None),
            P(),
            P(),
            P(),
            P(),
            P(),
        ),
        check_vma=False,
    )
```

```python
import functools

import jax
import jax.numpy as jnp
import numpy as np
from jax import lax
from jax.experimental import pallas as pl
from jax.experimental.pallas import tpu as pltpu
from jax.sharding import PartitionSpec as P

HEADS = 16
WINDOW = 12
SHIFT = 6
TOKENS = WINDOW * WINDOW
HALF = TOKENS // 2
SIDE = 2 * WINDOW - 1
SPAN = 384
TABLE_PAD = 640
SCALE = 32**-0.5
EXPERT_ROWS = 384
TAIL = (
    0.0997355664,
    0.0997364567,
    0.0934658327,
    0.0816079977,
    0.0589507659,
    0.0637694228,
    -0.0318383035,
    0.0957188375,
    -0.0809437035,
    0.0197971106,
)
VMEM_LIMIT = 40 * 1024 * 1024
LARGE_LIMIT = 60 * 1024 * 1024
F32 = jnp.float32
BF16 = jnp.bfloat16
GROUP = ("x", "core")
SAME_CORE = ("x", "tile")
OWNERS = 64
LIGHT = (1000000, 100000, 0)


def nn(a, b):
    return lax.dot_general(a, b, (((1,), (0,)), ((), ())), preferred_element_type=F32)


def nt(a, b):
    return lax.dot_general(a, b, (((1,), (1,)), ((), ())), preferred_element_type=F32)


def tn(a, b):
    return lax.dot_general(a, b, (((0,), (0,)), ((), ())), preferred_element_type=F32)


def call(kernel, outs, *, grid=None, in_specs=None, out_specs=None, scratch=(), cost=None, limit=VMEM_LIMIT, scalars=0):
    extra = dict(scratch_shapes=list(scratch))
    if scalars:
        spec = pltpu.PrefetchScalarGridSpec(
            num_scalar_prefetch=scalars, grid=grid, in_specs=in_specs, out_specs=out_specs, scratch_shapes=list(scratch)
        )
        extra = dict(grid_spec=spec)
    elif grid is not None:
        extra.update(grid=grid, in_specs=in_specs, out_specs=out_specs)
    if cost is not None:
        extra["cost_estimate"] = pl.CostEstimate(flops=cost[0], bytes_accessed=cost[1], transcendentals=cost[2])
    return pl.pallas_call(
        kernel, out_shape=outs, compiler_params=pltpu.CompilerParams(vmem_limit_bytes=limit), **extra
    )


def shape(dims, dtype):
    return jax.ShapeDtypeStruct(dims, dtype)


def whole(*dims):
    return pl.BlockSpec(dims, lambda *_: (0,) * len(dims))


def shifted(value, axis, steps):
    count = lax.axis_size(axis)
    pairs = [(source, (source + steps) % count) for source in range(count)]
    return lax.ppermute(value, axis, pairs)


def half_order(col_windows):
    columns = col_windows * WINDOW
    pick = np.zeros((SHIFT * columns, SHIFT * columns), np.float32)
    for win in range(col_windows):
        for row in range(SHIFT):
            for col in range(WINDOW):
                source = row * columns + (win * WINDOW + SHIFT + col) % columns
                pick[win * HALF + row * WINDOW + col, source] = 1.0
    return pick


def bias_targets():
    lane = np.arange(SPAN)
    target = (lane // WINDOW) * SIDE + lane % WINDOW + WINDOW - 1
    return np.where(lane < SIDE * WINDOW, target, -1000).astype(np.int32)[None]


def window_masks(row_last, col_windows):
    inner_pos = jnp.arange(TOKENS, dtype=jnp.int32)
    row_in = inner_pos // WINDOW
    col_in = inner_pos % WINDOW
    row_region = jnp.where(row_last[:, None], jnp.where(row_in < SHIFT, 1, 2)[None], 0)
    col_last = jnp.arange(col_windows, dtype=jnp.int32) == col_windows - 1
    col_region = jnp.where(col_last[:, None], jnp.where(col_in < SHIFT, 1, 2)[None], 0)
    region = (row_region[:, None, :] * 3 + col_region[None, :, :]).reshape(-1, TOKENS)
    same = region[:, :, None] == region[:, None, :]
    return jnp.where(same, 0.0, -100.0).astype(F32)


def normalised(values):
    mean = jnp.mean(values, axis=-1, keepdims=True)
    centred = values - mean
    scale = lax.rsqrt(jnp.mean(centred * centred, axis=-1, keepdims=True) + 1e-05)
    return centred * scale, scale


def norm_backward(unit, scale, grad, gain):
    weighted = grad * gain
    along = jnp.mean(weighted * unit, axis=-1, keepdims=True)
    flat = jnp.mean(weighted, axis=-1, keepdims=True)
    return scale * (weighted - flat - unit * along), jnp.sum(grad * unit, axis=0, keepdims=True)


def normal_of(values):
    bell = jnp.exp(-0.5 * values * values)
    inverse = pl.reciprocal(1.0 + 0.25 * jnp.abs(values))
    ratio = jnp.full_like(values, TAIL[-1])
    for factor in TAIL[-2::-1]:
        ratio = ratio * inverse + factor
    tail = bell * (ratio * inverse)
    return jnp.where(values < 0.0, tail, 1.0 - tail), bell * 0.3989422804014327


def iota(dims, axis):
    return lax.broadcasted_iota(jnp.int32, dims, axis)


def spread_matrix(targets, col):
    hit = iota((TABLE_PAD, SPAN), 0) == targets - col
    return jnp.where(hit, 1.0, 0.0).astype(BF16)


def pieces_of(value, count):
    parts = []
    for _ in range(count):
        part = value.astype(BF16)
        parts.append(part)
        value = value - part.astype(F32)
    return parts


def route_kernel(capacity, routes_ref, gate_ref, grad_ref, order_ref, send_ref, row_ref, col_ref):
    rows = grad_ref.shape[0]
    slots = send_ref.shape[0]
    routes = routes_ref[...]
    chosen = jnp.where(iota((HEADS, rows), 0) == routes, 1.0, 0.0)
    upto = jnp.where(iota((rows, rows), 0) <= iota((rows, rows), 1), 1.0, 0.0).astype(BF16)
    running = nn(chosen.astype(BF16), upto)
    slot = jnp.sum(running * chosen, axis=0, keepdims=True) - 1.0
    expert = routes.astype(F32)
    place = (expert * capacity + slot).astype(jnp.int32)
    picks = jnp.where(iota((slots, rows), 0) == place, gate_ref[...].astype(F32), 0.0).astype(BF16)
    send_ref[...] = nn(picks, grad_ref[...]).astype(BF16)
    order = order_ref[...]
    both = jnp.concatenate(
        [jnp.broadcast_to(expert, (8, rows)), jnp.broadcast_to(slot, (8, rows))], axis=0
    ).astype(BF16)
    moved = nt(both, order)
    there = moved[0:1] * capacity + moved[8:9]
    row_ref[...] = there.astype(jnp.int32)
    same = iota((rows, rows), 0) == iota((rows, rows), 1)
    col_ref[...] = jnp.sum(jnp.where(same, there, 0.0), axis=1, keepdims=True).astype(jnp.int32)


def bias_kernel(table_ref, targets_ref, bias_ref, spread):
    table = jnp.concatenate(pieces_of(table_ref[...], 3), axis=0)
    for col in range(16):
        part = nn(table, spread_matrix(targets_ref[...], col % WINDOW))
        spread[col] = part[0:HEADS] + part[HEADS : 2 * HEADS] + part[2 * HEADS :]
    for head in range(HEADS):
        rows = spread[:, head, :]
        for row in range(WINDOW):
            start = (WINDOW - 1 - row) * WINDOW
            turned = pltpu.roll(rows, (SPAN - start) % SPAN, 1) if start else rows
            bias_ref[head, row * WINDOW : (row + 1) * WINDOW, :] = turned[:WINDOW, :TOKENS]


def table_kernel(lined, targets_ref, gain_one_ref, gain_two_ref, out_ref):
    grads = jnp.zeros((2 * HEADS, TABLE_PAD), F32)
    for col in range(WINDOW):
        value = jnp.concatenate(pieces_of(lined[:, col, :], 2), axis=0)
        grads = grads + nt(value, spread_matrix(targets_ref[...], col))
    grads = grads[:HEADS] + grads[HEADS:]
    out_ref[...] = jnp.zeros_like(out_ref)
    lines = [grads[head : head + 1, 128 * part : 128 * part + 128] for head in range(HEADS) for part in range(5)]
    for gain_ref in (gain_one_ref, gain_two_ref):
        lines += [gain_ref[:, 128 * part : 128 * part + 128] for part in range(4)]
    for number, line in enumerate(lines):
        high, low = pieces_of(line, 2)
        out_ref[number // 2, number % 2 : number % 2 + 1, :] = high.astype(F32)
        out_ref[number // 2, 2 + number % 2 : 3 + number % 2, :] = low.astype(F32)


def merge_kernel(mine_ref, other_ref, small_ref, out_ref):
    for owner in range(OWNERS):
        both = mine_ref[owner].astype(F32) + other_ref[owner].astype(F32)
        out_ref[owner, :, :512] = both.astype(BF16)
        out_ref[owner, :, 512:] = small_ref[owner].astype(BF16)


def sum_kernel(all_ref, out_ref):
    total = all_ref[0].astype(F32)
    for owner in range(1, OWNERS):
        total = total + all_ref[owner].astype(F32)
    small = total[:, 512:]
    small = small + pltpu.roll(small, 14, 0)
    high = small.astype(BF16).astype(F32)
    low = pltpu.roll(small - high, 2, 0)
    row = iota(small.shape, 0)
    small = jnp.where(row < 2, high, jnp.where(row < 4, low, 0.0))
    total = jnp.concatenate([total[:, :512], small], axis=1).astype(BF16)
    for owner in range(OWNERS):
        out_ref[owner] = total


def unpack_kernel(core_ref, mine_ref, other_ref, qkv_ref, proj_ref, small_ref):
    def place(half_ref, first):
        for row in range(16):
            here = slice(first + 16 * row, first + 16 * row + 16)
            for col in range(4):
                block = half_ref[4 * row + col].astype(F32)
                qkv_ref[here, 384 * col : 384 * col + 384] = block[:, :384]
                proj_ref[here, 128 * col : 128 * col + 128] = block[:, 384:512]

    @pl.when(core_ref[0] == 0)
    def _():
        place(mine_ref, 0)
        place(other_ref, 256)

    @pl.when(core_ref[0] != 0)
    def _():
        place(other_ref, 0)
        place(mine_ref, 256)

    for owner in range(OWNERS):
        small = mine_ref[owner, :, 512:].astype(F32) + other_ref[owner, :, 512:].astype(F32)
        small_ref[owner] = small + pltpu.roll(small, 14, 0)


def attend_kernel(
    image_ref, below_ref, order_ref, gain_ref, w_qkv_ref, w_proj_ref, bias_ref, mask_ref,
    prob_ref, qkv_ref, x_ref, normed_ref, mixed_ref, own_ref, send_ref, blended,
):
    group = pl.program_id(0)
    wins = x_ref.shape[0] // TOKENS
    lanes = iota((TOKENS, 128), 1) // 32

    @pl.when(group == 0)
    def _():
        order = order_ref[...]
        upper = nn(order, image_ref[...])
        lower = nn(order, below_ref[...])
        parts = []
        for win in range(wins):
            parts.append(upper[win * HALF : (win + 1) * HALF])
            parts.append(lower[win * HALF : (win + 1) * HALF])
        x = jnp.concatenate(parts, axis=0)
        x_ref[...] = x.astype(BF16)
        unit, _ = normalised(x)
        normed_ref[...] = (unit * gain_ref[...]).astype(BF16)
        normed = normed_ref[...]
        for pair in range(6):
            act = nn(normed, w_qkv_ref[:, 256 * pair : 256 * pair + 256]).astype(BF16)
            qkv_ref[2 * pair] = act[:, :128]
            qkv_ref[2 * pair + 1] = act[:, 128:]

    def scores_of(win):
        rows = slice(win * TOKENS, (win + 1) * TOKENS)
        query = qkv_ref[group, rows, :]
        key = qkv_ref[4 + group, rows, :]
        return [nt(key, jnp.where(lanes == head, query, jnp.zeros_like(query))) for head in range(4)]

    later = scores_of(0)
    for win in range(wins):
        scores = later
        later = scores_of(win + 1) if win + 1 < wins else None
        rows = slice(win * TOKENS, (win + 1) * TOKENS)
        value_t = jnp.transpose(qkv_ref[8 + group, rows, :].astype(F32)).astype(BF16)
        mask = mask_ref[int(win == wins - 1)]
        mixes = []
        for head in range(4):
            score = scores[head] * SCALE + (bias_ref[head] + mask)
            score = jnp.exp(score - jnp.max(score, axis=0, keepdims=True))
            prob = (score * (1.0 / jnp.sum(score, axis=0, keepdims=True))).astype(BF16)
            prob_ref[head, win] = prob
            mixes.append(nn(value_t[32 * head : 32 * head + 32], prob))
        mix = jnp.transpose(jnp.concatenate(mixes, axis=0))
        blended[group, rows, :] = mix.astype(BF16)

    @pl.when(group == pl.num_programs(0) - 1)
    def _():
        mixed = jnp.concatenate([blended[i] for i in range(4)], axis=1)
        mixed_ref[...] = mixed
        after = x_ref[...].astype(F32) + nn(mixed, w_proj_ref[...])
        kept = [after[win * TOKENS : win * TOKENS + HALF] for win in range(wins)]
        away = [after[win * TOKENS + HALF : (win + 1) * TOKENS] for win in range(wins)]
        own_ref[...] = jnp.concatenate(kept, axis=0)
        send_ref[...] = jnp.concatenate(away, axis=0).astype(BF16)


def weight_kernel(which_ref, pre_ref, hidden_ref, in_ref, grad_ref, *rest):
    step = pl.program_id(0)
    up, down = tn(pre_ref[...], in_ref[...]), tn(hidden_ref[...], grad_ref[...])
    for number, out_ref in enumerate(rest[-4:]):

        @pl.when(step == number)
        def _():
            if len(rest) > 4:
                out_ref[0] = (up + rest[number][0].astype(F32)).astype(BF16)
                out_ref[1] = (down + rest[number][1].astype(F32)).astype(BF16)
            else:
                out_ref[0] = up.astype(BF16)
                out_ref[1] = down.astype(BF16)


def weight_grads(which, grad_pre, hidden, recv_in, recv_grad, added=()):
    slots, ffn = hidden.shape
    width = recv_in.shape[1]
    chunk = ffn // 8
    strip = pl.BlockSpec((slots, chunk), lambda s, which: (0, which[0] * 4 + (which[1] + s) % 4))
    block = whole(2, chunk, width)
    return call(
        weight_kernel,
        (shape((2, chunk, width), BF16),) * 4,
        grid=(4,),
        in_specs=[strip, strip, whole(slots, width), whole(slots, width)] + [block] * len(added),
        out_specs=(block,) * 4,
        scalars=1,
        cost=LIGHT,
        limit=LARGE_LIMIT,
    )(which, grad_pre, hidden, recv_in, recv_grad, *added)


def relay_kernel(next_in_ref, last_in_ref, up_ref, down_ref, next_ref, last_ref):
    next_ref[0] = (next_in_ref[0].astype(F32) + up_ref[...].astype(F32)).astype(BF16)
    next_ref[1] = next_in_ref[1]
    last_ref[0] = last_in_ref[0]
    last_ref[1] = (last_in_ref[1].astype(F32) + down_ref[...].astype(F32)).astype(BF16)


def owned_kernel(own_ref, left_ref, right_ref, out_ref):
    total = own_ref[...].astype(F32) + left_ref[...].astype(F32) + right_ref[...].astype(F32)
    out_ref[...] = total.astype(BF16)


def assemble_kernel(which_ref, *refs):
    up_ref, down_ref = refs[-2:]
    for core in range(2):
        half = which_ref[0] if core == 0 else 1 - which_ref[0]
        own, left, right, far_up, far_down = refs[5 * core : 5 * core + 5]
        for step, up, down in (
            (0, own.at[0], own.at[1]),
            (3, left.at[0], left.at[1]),
            (1, right.at[0], right.at[1]),
            (2, far_up, far_down),
        ):
            chunk = half * 4 + (which_ref[1] + step) % 4
            here = pl.ds(pl.multiple_of(chunk * 256, 256), 256)
            up_ref[:, here] = jnp.transpose(up[...].astype(F32))
            down_ref[here, :] = down[...].astype(F32)


def dispatch_kernel(own_ref, above_ref, gain_ref, row_ref, send_ref, after_ref):
    after = jnp.concatenate([above_ref[...].astype(F32), own_ref[...]], axis=0)
    after_ref[...] = after
    unit, _ = normalised(after)
    normed = (unit * gain_ref[...]).astype(BF16)
    picks = iota((send_ref.shape[0], after.shape[0]), 0) == row_ref[...]
    send_ref[...] = nn(jnp.where(picks, 1.0, 0.0).astype(BF16), normed).astype(BF16)


def expert_kernel(in_ref, back_ref, w_up_ref, hidden_ref, pre_ref, out_ref, total, score):
    step = pl.program_id(0)
    rows = in_ref.shape[0]
    width = out_ref.shape[1] - 128

    @pl.when(step == 0)
    def _():
        total[...] = jnp.zeros_like(total)
        score[...] = jnp.zeros_like(score)

    w_up = w_up_ref[...]
    blocks = rows // EXPERT_ROWS
    places = [slice(block * EXPERT_ROWS, (block + 1) * EXPERT_ROWS) for block in range(blocks)]
    later = nn(in_ref[places[0], :], w_up)
    for block, here in enumerate(places):
        pre = later
        later = nn(in_ref[places[block + 1], :], w_up) if block + 1 < blocks else None
        cumulative, density = normal_of(pre)
        hidden = (pre * cumulative).astype(BF16)
        back = back_ref[here, :].astype(F32)
        grad = (back * (cumulative + pre * density)).astype(BF16)
        hidden_ref[here, :] = hidden
        pre_ref[here, :] = grad
        product = hidden.astype(F32) * back
        score[here, :] += sum(product[:, part : part + 128] for part in range(0, product.shape[1], 128))
        total[here, :] += nt(grad, w_up)

    @pl.when(step == pl.num_programs(0) - 1)
    def _():
        out_ref[:, :width] = total[...].astype(BF16)
        summed = jnp.sum(score[...], axis=1, keepdims=True)
        high = summed.astype(BF16).astype(F32)
        lane = iota((rows, 128), 1)
        tail = jnp.where(lane == 0, high, jnp.where(lane == 1, summed - high, 0.0))
        out_ref[:, width:] = tail.astype(BF16)


def combine_kernel(
    back_ref, col_ref, after_ref, grad_ref, order_ref, gain_ref, send_ref, own_ref, gain_out_ref, score_ref
):
    rows, width = after_ref.shape
    picks = iota((rows, back_ref.shape[0]), 1) == col_ref[...]
    picks = jnp.where(picks, 1.0, 0.0).astype(BF16)
    back = nn(picks, back_ref[...])
    score_ref[...] = back[:, width:]
    unit, scale = normalised(after_ref[...])
    grad, gain_grad = norm_backward(unit, scale, back[:, :width], gain_ref[...])
    gain_out_ref[...] = gain_grad
    order = order_ref[...]
    half = rows // 2
    send_ref[...] = (nn(order, grad_ref[:half, :]) + grad[:half]).astype(BF16)
    own_ref[...] = nn(order, grad_ref[half:, :]) + grad[half:]


def attend_backward_kernel(
    core_ref, own_ref, below_ref, order_t_ref, gain_ref, w_qkv_ref, w_proj_ref, qkv_ref, x_ref, normed_ref, mixed_ref,
    prob_ref, lined_ref, mine_ref, other_ref, kept_ref, send_ref, gain_out_ref, pair, cotangent, grad_mixed, grad_act,
    grad_qkv, grad_proj,
):
    group = pl.program_id(0)
    rows_all = x_ref.shape[0]
    wins = rows_all // TOKENS
    lanes = iota((TOKENS, 128), 1) // 32

    @pl.when(group == 0)
    def _():
        parts = []
        for win in range(wins):
            parts.append(own_ref[win * HALF : (win + 1) * HALF, :])
            parts.append(below_ref[...].astype(F32)[win * HALF : (win + 1) * HALF, :])
        cot = jnp.concatenate(parts, axis=0)
        cotangent[...] = cot
        mixed = nt(cot.astype(BF16), w_proj_ref[...]).astype(BF16)
        for i in range(4):
            grad_mixed[i] = mixed[:, 128 * i : 128 * i + 128]

    pair[...] = jnp.zeros_like(pair)

    def first_part(win):
        rows = slice(win * TOKENS, (win + 1) * TOKENS)
        value = qkv_ref[8 + group, rows, :]
        out = grad_mixed[group, rows, :]
        grad_probs, grad_value = [], None
        for head in range(4):
            own_out = jnp.where(lanes == head, out, jnp.zeros_like(out))
            grad_probs.append(nt(value, own_out))
            part = nn(prob_ref[head, win], own_out)
            grad_value = part if head == 0 else grad_value + part
        grad_act[8 + group, rows, :] = grad_value.astype(BF16)
        return grad_probs

    later = first_part(0)
    for win in range(wins):
        grad_probs = later
        later = first_part(win + 1) if win + 1 < wins else None
        rows = slice(win * TOKENS, (win + 1) * TOKENS)
        query = qkv_ref[group, rows, :]
        key_t = jnp.transpose(qkv_ref[4 + group, rows, :].astype(F32)).astype(BF16)
        grad_query, grad_key = [], None
        for head in range(4):
            own_query = jnp.where(lanes == head, query, jnp.zeros_like(query))
            prob = prob_ref[head, win].astype(F32)
            grad_prob = grad_probs[head].astype(BF16).astype(F32)
            weighted = prob * grad_prob
            grad_score = weighted - prob * jnp.sum(weighted, axis=0, keepdims=True)
            pair[head, :TOKENS, :TOKENS] += grad_score
            half_score = grad_score.astype(BF16)
            part = nn(half_score, own_query)
            grad_key = part if head == 0 else grad_key + part
            grad_query.append(nn(key_t[32 * head : 32 * head + 32], half_score))
        full_query = jnp.transpose(jnp.concatenate(grad_query, axis=0))
        grad_act[group, rows, :] = (full_query * SCALE).astype(BF16)
        grad_act[4 + group, rows, :] = (grad_key * SCALE).astype(BF16)

    for head in range(4):
        total = pair[head, (WINDOW - 1) * WINDOW : (WINDOW - 1) * WINDOW + 16, :]
        for row in range(WINDOW - 1):
            start = (WINDOW - 1 - row) * WINDOW
            total = total + pltpu.roll(pair[head, row * WINDOW : row * WINDOW + 16, :], start, 1)
        lined_ref[head] = total

    @pl.when(group == pl.num_programs(0) - 1)
    def _():
        act = jnp.concatenate([grad_act[i] for i in range(12)], axis=1)
        normed_t = jnp.transpose(normed_ref[...].astype(F32)).astype(BF16)
        mixed_t = jnp.transpose(mixed_ref[...].astype(F32)).astype(BF16)
        cot = cotangent[...]
        grad_proj[...] = nn(mixed_t, cot.astype(BF16)).astype(BF16)
        grad_qkv[...] = nn(normed_t, act).astype(BF16)

        def scatter(half_ref, first):
            for row in range(16):
                here = slice(first + 16 * row, first + 16 * row + 16)
                for col in range(4):
                    half_ref[4 * row + col, :, :384] = grad_qkv[here, 384 * col : 384 * col + 384]
                    half_ref[4 * row + col, :, 384:] = grad_proj[here, 128 * col : 128 * col + 128]

        @pl.when(core_ref[0] == 0)
        def _():
            scatter(mine_ref, 0)
            scatter(other_ref, 256)

        @pl.when(core_ref[0] != 0)
        def _():
            scatter(other_ref, 0)
            scatter(mine_ref, 256)

        grad_normed = nt(act, w_qkv_ref[...])
        unit, scale = normalised(x_ref[...].astype(F32))
        grad, gain_grad = norm_backward(unit, scale, grad_normed, gain_ref[...])
        gain_out_ref[...] = gain_grad
        total = cot + grad
        kept = [total[win * TOKENS : win * TOKENS + HALF] for win in range(wins)]
        away = [total[win * TOKENS + HALF : (win + 1) * TOKENS] for win in range(wins)]
        order_t = order_t_ref[...]
        kept_ref[...] = nn(order_t, jnp.concatenate(kept, axis=0).astype(BF16)).astype(BF16)
        send_ref[...] = nn(order_t, jnp.concatenate(away, axis=0).astype(BF16)).astype(BF16)


def on_device(
    image, grad_out, gate, routes, gain_one, w_qkv, w_proj, table, gain_two, w_fc1, w_fc2
):
    tile_count = lax.axis_size("tile")
    tile_index = lax.axis_index("tile")
    strip_height, columns, channels = image.shape[1:]
    wins = columns // WINDOW
    rows = strip_height * columns
    half = rows // 2
    capacity = 2 * rows // tile_count
    slots = tile_count * capacity
    ffn = w_fc1.shape[2]
    core = lax.axis_index("core").reshape(1).astype(jnp.int32)
    exchange = functools.partial(lax.all_to_all, split_axis=0, concat_axis=0, tiled=True)
    pick = half_order(wins)
    order = jnp.asarray(pick, BF16)
    order_t = jnp.asarray(pick.T, BF16)
    order_all = jnp.asarray(np.kron(np.eye(2), pick), BF16)
    targets = jnp.asarray(bias_targets())
    gain_one = gain_one.reshape(1, channels)
    gain_two = gain_two.reshape(1, channels)
    image_rows = image.reshape(rows, channels)
    grad_rows = grad_out.reshape(rows, channels)
    gate_row = gate.reshape(1, rows)

    below = shifted(image_rows[:half], "tile", -1)
    send_grad, place_row, place_col = call(
        functools.partial(route_kernel, capacity),
        (shape((slots, channels), BF16), shape((1, rows), jnp.int32), shape((rows, 1), jnp.int32)),
        cost=(700000000, 3000000, 0),
    )(routes.reshape(1, rows), gate_row, grad_rows, order_all)
    recv_grad = exchange(send_grad, "tile")
    bias = call(
        bias_kernel,
        shape((HEADS, TOKENS, TOKENS), F32),
        scratch=[pltpu.VMEM((16, HEADS, SPAN), F32)],
        cost=(400000000, 3000000, 0),
    )(jnp.pad(table, ((0, 0), (0, TABLE_PAD - table.shape[1]))), targets)
    mask = window_masks(jnp.reshape(tile_index == tile_count - 1, (1,)), wins)[wins - 2 :]

    head_block = pl.BlockSpec((4, wins, TOKENS, TOKENS), lambda g: (g, 0, 0, 0))
    pair_block = pl.BlockSpec((4, TOKENS, TOKENS), lambda g: (g, 0, 0))
    prob, qkv_act, windows, normed_one, mixed, own_after, send_after = call(
        attend_kernel,
        (
            shape((HEADS, wins, TOKENS, TOKENS), BF16),
            shape((12, rows, 128), BF16),
            shape((rows, channels), BF16),
            shape((rows, channels), BF16),
            shape((rows, channels), BF16),
            shape((half, channels), F32),
            shape((half, channels), BF16),
        ),
        grid=(4,),
        in_specs=[
            pl.BlockSpec((half, channels), lambda g: (1, 0)),
            whole(half, channels),
            whole(half, half),
            whole(1, channels),
            whole(channels, 3 * channels),
            whole(channels, channels),
            pair_block,
            whole(2, TOKENS, TOKENS),
        ],
        out_specs=(
            head_block,
            whole(12, rows, 128),
            whole(rows, channels),
            whole(rows, channels),
            whole(rows, channels),
            whole(half, channels),
            whole(half, channels),
        ),
        scratch=[pltpu.VMEM((4, rows, 128), BF16)],
        cost=(3000000000, 12000000, 2000000),
        limit=LARGE_LIMIT,
    )(image_rows, below, order, gain_one, w_qkv, w_proj, bias, mask)

    above = shifted(send_after, "tile", 1)
    send_in, after = call(
        dispatch_kernel,
        (shape((slots, channels), BF16), shape((rows, channels), F32)),
        cost=(700000000, 4000000, 0),
    )(own_after, above, gain_two, place_row)
    recv_in = exchange(send_in, "tile")

    w_up, w_down = w_fc1[0], w_fc2[0]
    grad_hidden = jnp.dot(recv_grad, w_down.T, preferred_element_type=F32).astype(BF16)
    chunk = 512
    strip = pl.BlockSpec((slots, chunk), lambda f: (0, f))
    hidden, grad_pre, send_back = call(
        expert_kernel,
        (
            shape((slots, ffn), BF16),
            shape((slots, ffn), BF16),
            shape((slots, channels + 128), BF16),
        ),
        grid=(ffn // chunk,),
        in_specs=[whole(slots, channels), strip, pl.BlockSpec((channels, chunk), lambda f: (0, f))],
        out_specs=(strip, strip, whole(slots, channels + 128)),
        scratch=[pltpu.VMEM((slots, channels), F32), pltpu.VMEM((slots, 128), F32)],
        cost=(4800000000, 20000000, 5000000),
        limit=LARGE_LIMIT,
    )(recv_in, grad_hidden, w_up)
    recv_back = exchange(send_back, "tile")
    place_x = lax.axis_index("x").astype(jnp.int32)
    mine_at = jnp.stack([core[0], place_x])
    other_at = jnp.stack([1 - core[0], place_x])
    other_part = weight_grads(other_at, grad_pre, hidden, recv_in, recv_grad)
    other_part = [shifted(part, "core", 1) for part in other_part]
    mine_part = weight_grads(mine_at, grad_pre, hidden, recv_in, recv_grad, other_part)
    recv_back, mine_part = lax.optimization_barrier((recv_back, mine_part))
    chunk = shape(mine_part[0].shape, BF16)
    far_up = shifted(mine_part[2][0], "x", 1)
    far_down = shifted(mine_part[2][1], "x", -1)

    send_cot, own_cot, gain_two_part, score = call(
        combine_kernel,
        (
            shape((half, channels), BF16),
            shape((half, channels), F32),
            shape((1, channels), F32),
            shape((rows, 128), F32),
        ),
        cost=LIGHT,
    )(recv_back, place_col, after, grad_rows, order, gain_two)
    below_cot = shifted(send_cot, "tile", -1)
    to_right, to_left = call(relay_kernel, (chunk, chunk), cost=LIGHT)(mine_part[1], mine_part[3], far_up, far_down)
    below_cot, to_right, to_left = lax.optimization_barrier((below_cot, to_right, to_left))
    from_left, from_right = shifted(to_right, "x", 1), shifted(to_left, "x", -1)
    half_pieces = shape((OWNERS, 16, 512), BF16)
    lined, mine, other, kept, send_up, gain_one_part = call(
        attend_backward_kernel,
        (
            shape((HEADS, 16, SPAN), F32),
            half_pieces,
            half_pieces,
            shape((half, channels), BF16),
            shape((half, channels), BF16),
            shape((1, channels), F32),
        ),
        grid=(4,),
        in_specs=[
            pl.BlockSpec(memory_space=pltpu.SMEM),
            whole(half, channels),
            whole(half, channels),
            whole(half, half),
            whole(1, channels),
            whole(channels, 3 * channels),
            whole(channels, channels),
            whole(12, rows, 128),
            whole(rows, channels),
            whole(rows, channels),
            whole(rows, channels),
            head_block,
        ],
        out_specs=(
            pl.BlockSpec((4, 16, SPAN), lambda g: (g, 0, 0)),
            whole(OWNERS, 16, 512),
            whole(OWNERS, 16, 512),
            whole(half, channels),
            whole(half, channels),
            whole(1, channels),
        ),
        scratch=[
            pltpu.VMEM((4, TOKENS + 16, SPAN), F32),
            pltpu.VMEM((rows, channels), F32),
            pltpu.VMEM((4, rows, 128), BF16),
            pltpu.VMEM((12, rows, 128), BF16),
            pltpu.VMEM((channels, 3 * channels), BF16),
            pltpu.VMEM((channels, channels), BF16),
        ],
        cost=LIGHT,
        limit=LARGE_LIMIT,
    )(core, own_cot, below_cot, order_t, gain_one, w_qkv, w_proj, qkv_act, windows, normed_one, mixed, prob)
    lined, mine, other, send_up, gain_one_part, from_left, from_right = lax.optimization_barrier(
        (lined, mine, other, send_up, gain_one_part, from_left, from_right)
    )
    upper = shifted(send_up, "tile", 1)
    other = shifted(other, "core", 1)
    small = call(
        table_kernel,
        shape((OWNERS, 16, 128), F32),
        cost=LIGHT,
    )(lined, targets, gain_one_part, gain_two_part)
    upper, other, small = lax.optimization_barrier((upper, other, small))
    pieces = shape((OWNERS, 16, 640), BF16)
    merged = call(merge_kernel, pieces, cost=(0, 4000000, 0))(mine, other, small)
    merged, from_left, from_right, score = lax.optimization_barrier((merged, from_left, from_right, score))
    parts = exchange(merged, SAME_CORE)
    owned = call(owned_kernel, chunk, cost=LIGHT)(mine_part[0], from_left, from_right)
    left, right = shifted(owned, "x", 1), shifted(owned, "x", -1)
    score = (score[:, 0] + score[:, 1]).reshape(2, wins, SHIFT, WINDOW)
    score = score.transpose(0, 2, 1, 3).reshape(strip_height, columns)
    grad_gate = jnp.roll(score, SHIFT, axis=1) / gate[0].astype(F32)
    far_up, far_down = shifted(left[0], "x", 1), shifted(right[1], "x", -1)
    parts, far_up, far_down = lax.optimization_barrier((parts, far_up, far_down))
    summed = call(sum_kernel, pieces, cost=LIGHT)(parts)
    chunks = [owned, left, right, far_up, far_down]
    chunks = chunks + [shifted(value, "core", 1) for value in chunks]
    grad_image = jnp.concatenate([upper, kept], axis=0).reshape(image.shape)
    summed_up, summed_down = call(
        assemble_kernel,
        (shape((channels, ffn), F32), shape((ffn, channels), F32)),
        grid=(1,),
        in_specs=[pl.BlockSpec(memory_space=pltpu.SMEM)] + ([whole(*chunk.shape)] * 3 + [whole(*chunk.shape[1:])] * 2) * 2,
        out_specs=(whole(channels, ffn), whole(ffn, channels)),
        cost=LIGHT,
    )(mine_at, *chunks)
    gathered = exchange(summed, SAME_CORE)
    gathered, summed_up, summed_down, grad_image, grad_gate = lax.optimization_barrier(
        (gathered, summed_up, summed_down, grad_image, grad_gate)
    )
    grad_qkv, grad_proj, small_all = call(
        unpack_kernel,
        (
            shape((channels, 3 * channels), F32),
            shape((channels, channels), F32),
            shape((OWNERS, 16, 128), F32),
        ),
        grid=(1,),
        in_specs=[pl.BlockSpec(memory_space=pltpu.SMEM), whole(OWNERS, 16, 640), whole(OWNERS, 16, 640)],
        out_specs=(whole(channels, 3 * channels), whole(channels, channels), whole(OWNERS, 16, 128)),
        cost=(0, 7000000, 0),
    )(core, gathered, shifted(gathered, "core", 1))
    small_all = small_all[:, :2, :].reshape(2 * OWNERS, 128)
    first = HEADS * TABLE_PAD // 128
    grad_table = small_all[:first].reshape(HEADS, TABLE_PAD)[:, : table.shape[1]]
    grad_gain_one = small_all[first : first + 4].reshape(channels)
    grad_gain_two = small_all[first + 4 : first + 8].reshape(channels)
    return (
        grad_image,
        grad_gate.reshape(1, strip_height, columns),
        summed_up.reshape(1, channels, ffn),
        summed_down.reshape(1, ffn, channels),
        grad_qkv,
        grad_proj,
        grad_table,
        grad_gain_one,
        grad_gain_two,
    )


def solution(mesh):
    devices = mesh.devices
    split = jax.sharding.Mesh(devices.reshape(-1, 2, devices.shape[1]), ("x", "core", "tile"))
    return jax.shard_map(
        on_device,
        mesh=split,
        in_specs=(
            P(GROUP, "tile", None, None),
            P(GROUP, "tile", None, None),
            P(GROUP, "tile", None),
            P(GROUP, "tile", None, None),
            P(),
            P(),
            P(),
            P(),
            P(),
            P("tile", None, None),
            P("tile", None, None),
        ),
        out_specs=(
            P(GROUP, "tile", None, None),
            P(GROUP, "tile", None),
            P("tile", None, None),
            P("tile", None, None),
            P(),
            P(),
            P(),
            P(),
            P(),
        ),
        check_vma=False,
    )
```

```python
import functools

import jax
import jax.numpy as jnp
import numpy as np
from jax import lax
from jax.experimental import pallas as pl
from jax.experimental.pallas import tpu as pltpu
from jax.sharding import PartitionSpec as P

HEADS = 16
WINDOW = 12
SHIFT = 6
TOKENS = WINDOW * WINDOW
HALF = TOKENS // 2
SIDE = 2 * WINDOW - 1
SPAN = 384
TABLE_PAD = 640
SCALE = 32**-0.5
EXPERT_ROWS = 384
TAIL_BASE = 2.702702760696411
TAIL = (
    0.398942202,
    1.07827175,
    2.51046658,
    4.81238174,
    1.92840862,
    25.174448,
    -204.768677,
    384.889191,
    -241.165222,
)
VMEM_LIMIT = 40 * 1024 * 1024
LARGE_LIMIT = 60 * 1024 * 1024
F32 = jnp.float32
BF16 = jnp.bfloat16
GROUP = ("x", "core")
SAME_CORE = ("x", "tile")
OWNERS = 64
LIGHT = (1000000, 100000, 0)


def nn(a, b):
    return lax.dot_general(a, b, (((1,), (0,)), ((), ())), preferred_element_type=F32)


def nt(a, b):
    return lax.dot_general(a, b, (((1,), (1,)), ((), ())), preferred_element_type=F32)


def tn(a, b):
    return lax.dot_general(a, b, (((0,), (0,)), ((), ())), preferred_element_type=F32)


def call(kernel, outs, *, grid=None, in_specs=None, out_specs=None, scratch=(), cost=None, limit=VMEM_LIMIT, scalars=0):
    extra = dict(scratch_shapes=list(scratch))
    if scalars:
        spec = pltpu.PrefetchScalarGridSpec(
            num_scalar_prefetch=scalars, grid=grid, in_specs=in_specs, out_specs=out_specs, scratch_shapes=list(scratch)
        )
        extra = dict(grid_spec=spec)
    elif grid is not None:
        extra.update(grid=grid, in_specs=in_specs, out_specs=out_specs)
    if cost is not None:
        extra["cost_estimate"] = pl.CostEstimate(flops=cost[0], bytes_accessed=cost[1], transcendentals=cost[2])
    return pl.pallas_call(
        kernel, out_shape=outs, compiler_params=pltpu.CompilerParams(vmem_limit_bytes=limit), **extra
    )


def shape(dims, dtype):
    return jax.ShapeDtypeStruct(dims, dtype)


def whole(*dims):
    return pl.BlockSpec(dims, lambda *_: (0,) * len(dims))


def shifted(value, axis, steps):
    count = lax.axis_size(axis)
    pairs = [(source, (source + steps) % count) for source in range(count)]
    return lax.ppermute(value, axis, pairs)


def half_order(col_windows):
    columns = col_windows * WINDOW
    pick = np.zeros((SHIFT * columns, SHIFT * columns), np.float32)
    for win in range(col_windows):
        for row in range(SHIFT):
            for col in range(WINDOW):
                source = row * columns + (win * WINDOW + SHIFT + col) % columns
                pick[win * HALF + row * WINDOW + col, source] = 1.0
    return pick


def bias_targets():
    lane = np.arange(SPAN)
    target = (lane // WINDOW) * SIDE + lane % WINDOW + WINDOW - 1
    return np.where(lane < SIDE * WINDOW, target, -1000).astype(np.int32)[None]


def window_masks(row_last, col_windows):
    inner_pos = jnp.arange(TOKENS, dtype=jnp.int32)
    row_in = inner_pos // WINDOW
    col_in = inner_pos % WINDOW
    row_region = jnp.where(row_last[:, None], jnp.where(row_in < SHIFT, 1, 2)[None], 0)
    col_last = jnp.arange(col_windows, dtype=jnp.int32) == col_windows - 1
    col_region = jnp.where(col_last[:, None], jnp.where(col_in < SHIFT, 1, 2)[None], 0)
    region = (row_region[:, None, :] * 3 + col_region[None, :, :]).reshape(-1, TOKENS)
    same = region[:, :, None] == region[:, None, :]
    return jnp.where(same, 0.0, -100.0).astype(F32)


def normalised(values):
    mean = jnp.mean(values, axis=-1, keepdims=True)
    centred = values - mean
    scale = lax.rsqrt(jnp.mean(centred * centred, axis=-1, keepdims=True) + 1e-05)
    return centred * scale, scale


def norm_backward(unit, scale, grad, gain):
    weighted = grad * gain
    along = jnp.mean(weighted * unit, axis=-1, keepdims=True)
    flat = jnp.mean(weighted, axis=-1, keepdims=True)
    return scale * (weighted - flat - unit * along), jnp.sum(grad * unit, axis=0, keepdims=True)


def normal_of(values):
    bell = jnp.exp2(values * values * -0.7213475204444817)
    inverse = pl.reciprocal(TAIL_BASE + jnp.abs(values))
    ratio = inverse * TAIL[-1] + TAIL[-2]
    for factor in TAIL[-3::-1]:
        ratio = ratio * inverse + factor
    tail = bell * (ratio * inverse)
    return jnp.where(values < 0.0, tail, 1.0 - tail), bell * 0.3989422804014327


def iota(dims, axis):
    return lax.broadcasted_iota(jnp.int32, dims, axis)


def spread_matrix(targets, col):
    hit = iota((TABLE_PAD, SPAN), 0) == targets - col
    return jnp.where(hit, 1.0, 0.0).astype(BF16)


def pieces_of(value, count):
    parts = []
    for _ in range(count):
        part = value.astype(BF16)
        parts.append(part)
        value = value - part.astype(F32)
    return parts


def route_kernel(capacity, routes_ref, gate_ref, grad_ref, order_ref, send_ref, row_ref, col_ref):
    rows = grad_ref.shape[0]
    slots = send_ref.shape[0]
    routes = routes_ref[...]
    chosen = jnp.where(iota((HEADS, rows), 0) == routes, 1.0, 0.0)
    upto = jnp.where(iota((rows, rows), 0) <= iota((rows, rows), 1), 1.0, 0.0).astype(BF16)
    running = nn(chosen.astype(BF16), upto)
    slot = jnp.sum(running * chosen, axis=0, keepdims=True) - 1.0
    expert = routes.astype(F32)
    place = (expert * capacity + slot).astype(jnp.int32)
    picks = jnp.where(iota((slots, rows), 0) == place, gate_ref[...].astype(F32), 0.0).astype(BF16)
    send_ref[...] = nn(picks, grad_ref[...]).astype(BF16)
    order = order_ref[...]
    both = jnp.concatenate(
        [jnp.broadcast_to(expert, (8, rows)), jnp.broadcast_to(slot, (8, rows))], axis=0
    ).astype(BF16)
    moved = nt(both, order)
    there = moved[0:1] * capacity + moved[8:9]
    row_ref[...] = there.astype(jnp.int32)
    same = iota((rows, rows), 0) == iota((rows, rows), 1)
    col_ref[...] = jnp.sum(jnp.where(same, there, 0.0), axis=1, keepdims=True).astype(jnp.int32)


def bias_kernel(table_ref, targets_ref, bias_ref, spread):
    table = jnp.concatenate(pieces_of(table_ref[...], 3), axis=0)
    for col in range(16):
        part = nn(table, spread_matrix(targets_ref[...], col % WINDOW))
        spread[col] = part[0:HEADS] + part[HEADS : 2 * HEADS] + part[2 * HEADS :]
    for head in range(HEADS):
        rows = spread[:, head, :]
        for row in range(WINDOW):
            start = (WINDOW - 1 - row) * WINDOW
            turned = pltpu.roll(rows, (SPAN - start) % SPAN, 1) if start else rows
            bias_ref[head, row * WINDOW : (row + 1) * WINDOW, :] = turned[:WINDOW, :TOKENS]


def table_kernel(lined, targets_ref, gain_one_ref, gain_two_ref, out_ref):
    grads = jnp.zeros((2 * HEADS, TABLE_PAD), F32)
    for col in range(WINDOW):
        value = jnp.concatenate(pieces_of(lined[:, col, :], 2), axis=0)
        grads = grads + nt(value, spread_matrix(targets_ref[...], col))
    grads = grads[:HEADS] + grads[HEADS:]
    out_ref[...] = jnp.zeros_like(out_ref)
    lines = [grads[head : head + 1, 128 * part : 128 * part + 128] for head in range(HEADS) for part in range(5)]
    for gain_ref in (gain_one_ref, gain_two_ref):
        lines += [gain_ref[:, 128 * part : 128 * part + 128] for part in range(4)]
    for number, line in enumerate(lines):
        high, low = pieces_of(line, 2)
        out_ref[number // 2, number % 2 : number % 2 + 1, :] = high.astype(F32)
        out_ref[number // 2, 2 + number % 2 : 3 + number % 2, :] = low.astype(F32)


def merge_kernel(mine_ref, other_ref, small_ref, out_ref):
    for owner in range(OWNERS):
        both = mine_ref[owner].astype(F32) + other_ref[owner].astype(F32)
        out_ref[owner, :, :512] = both.astype(BF16)
        out_ref[owner, :, 512:] = small_ref[owner].astype(BF16)


def sum_kernel(all_ref, out_ref):
    total = all_ref[0].astype(F32)
    for owner in range(1, OWNERS):
        total = total + all_ref[owner].astype(F32)
    small = total[:, 512:]
    small = small + pltpu.roll(small, 14, 0)
    high = small.astype(BF16).astype(F32)
    low = pltpu.roll(small - high, 2, 0)
    row = iota(small.shape, 0)
    small = jnp.where(row < 2, high, jnp.where(row < 4, low, 0.0))
    total = jnp.concatenate([total[:, :512], small], axis=1).astype(BF16)
    for owner in range(OWNERS):
        out_ref[owner] = total


def unpack_kernel(core_ref, mine_ref, other_ref, qkv_ref, proj_ref, small_ref):
    def place(half_ref, first):
        for row in range(16):
            here = slice(first + 16 * row, first + 16 * row + 16)
            for col in range(4):
                block = half_ref[4 * row + col].astype(F32)
                qkv_ref[here, 384 * col : 384 * col + 384] = block[:, :384]
                proj_ref[here, 128 * col : 128 * col + 128] = block[:, 384:512]

    @pl.when(core_ref[0] == 0)
    def _():
        place(mine_ref, 0)
        place(other_ref, 256)

    @pl.when(core_ref[0] != 0)
    def _():
        place(other_ref, 0)
        place(mine_ref, 256)

    for owner in range(OWNERS):
        small = mine_ref[owner, :, 512:].astype(F32) + other_ref[owner, :, 512:].astype(F32)
        small_ref[owner] = small + pltpu.roll(small, 14, 0)


def attend_kernel(
    image_ref, below_ref, order_ref, gain_ref, w_qkv_ref, w_proj_ref, bias_ref, mask_ref,
    prob_ref, qkv_ref, x_ref, normed_ref, mixed_ref, own_ref, send_ref, blended,
):
    group = pl.program_id(0)
    wins = x_ref.shape[0] // TOKENS
    lanes = iota((TOKENS, 128), 1) // 32

    @pl.when(group == 0)
    def _():
        order = order_ref[...]
        upper = nn(order, image_ref[...])
        lower = nn(order, below_ref[...])
        parts = []
        for win in range(wins):
            parts.append(upper[win * HALF : (win + 1) * HALF])
            parts.append(lower[win * HALF : (win + 1) * HALF])
        x = jnp.concatenate(parts, axis=0)
        x_ref[...] = x.astype(BF16)
        unit, _ = normalised(x)
        normed_ref[...] = (unit * gain_ref[...]).astype(BF16)
        normed = normed_ref[...]
        for pair in range(6):
            act = nn(normed, w_qkv_ref[:, 256 * pair : 256 * pair + 256]).astype(BF16)
            qkv_ref[2 * pair] = act[:, :128]
            qkv_ref[2 * pair + 1] = act[:, 128:]

    def scores_of(win):
        rows = slice(win * TOKENS, (win + 1) * TOKENS)
        query = qkv_ref[group, rows, :]
        key = qkv_ref[4 + group, rows, :]
        return [nt(key, jnp.where(lanes == head, query, jnp.zeros_like(query))) for head in range(4)]

    later = scores_of(0)
    for win in range(wins):
        scores = later
        later = scores_of(win + 1) if win + 1 < wins else None
        rows = slice(win * TOKENS, (win + 1) * TOKENS)
        value_t = jnp.transpose(qkv_ref[8 + group, rows, :].astype(F32)).astype(BF16)
        mask = mask_ref[int(win == wins - 1)]
        mixes = []
        for head in range(4):
            score = scores[head] * SCALE + (bias_ref[head] + mask)
            score = jnp.exp(score - jnp.max(score, axis=0, keepdims=True))
            prob = (score * (1.0 / jnp.sum(score, axis=0, keepdims=True))).astype(BF16)
            prob_ref[head, win] = prob
            mixes.append(nn(value_t[32 * head : 32 * head + 32], prob))
        mix = jnp.transpose(jnp.concatenate(mixes, axis=0))
        blended[group, rows, :] = mix.astype(BF16)

    @pl.when(group == pl.num_programs(0) - 1)
    def _():
        mixed = jnp.concatenate([blended[i] for i in range(4)], axis=1)
        mixed_ref[...] = mixed
        after = x_ref[...].astype(F32) + nn(mixed, w_proj_ref[...])
        kept = [after[win * TOKENS : win * TOKENS + HALF] for win in range(wins)]
        away = [after[win * TOKENS + HALF : (win + 1) * TOKENS] for win in range(wins)]
        own_ref[...] = jnp.concatenate(kept, axis=0)
        send_ref[...] = jnp.concatenate(away, axis=0).astype(BF16)


def flip_kernel(in_ref, out_ref):
    out_ref[...] = jnp.transpose(in_ref[...].astype(F32)).astype(BF16)


def weight_kernel(which_ref, pre_ref, hidden_ref, in_ref, grad_ref, *rest):
    step = pl.program_id(0)
    added = rest[:-8]
    up, down = nn(in_ref[...], pre_ref[...]), nn(grad_ref[...], hidden_ref[...])
    for number in range(4):

        @pl.when(step == number)
        def _():
            for half, value in ((0, up), (1, down)):
                if added:
                    value = value + added[2 * number + half][...].astype(F32)
                rest[len(added) + 2 * number + half][...] = value.astype(BF16)


def weight_grads(which, grad_pre, hidden, in_t, grad_t, added=()):
    slots, ffn = hidden.shape
    width = in_t.shape[0]
    chunk = ffn // 8
    strip = pl.BlockSpec((slots, chunk), lambda s, which: (0, which[0] * 4 + (which[1] + s) % 4))
    block = whole(width, chunk)
    return call(
        weight_kernel,
        (shape((width, chunk), BF16),) * 8,
        grid=(4,),
        in_specs=[strip, strip, whole(width, slots), whole(width, slots)] + [block] * len(added),
        out_specs=(block,) * 8,
        scalars=1,
        cost=LIGHT,
        limit=LARGE_LIMIT,
    )(which, grad_pre, hidden, in_t, grad_t, *added)


def relay_kernel(next_up, next_down, last_up, last_down, far_up, far_down, next_ref, last_ref):
    next_ref[0] = (next_up[...].astype(F32) + far_up[...].astype(F32)).astype(BF16)
    next_ref[1] = next_down[...]
    last_ref[0] = last_up[...]
    last_ref[1] = (last_down[...].astype(F32) + far_down[...].astype(F32)).astype(BF16)


def owned_kernel(up_ref, down_ref, left_ref, right_ref, out_ref):
    for half, own_ref in ((0, up_ref), (1, down_ref)):
        total = own_ref[...].astype(F32) + left_ref[half].astype(F32) + right_ref[half].astype(F32)
        out_ref[half] = total.astype(BF16)


def assemble_kernel(which_ref, *refs):
    up_ref, down_ref = refs[-2:]
    for core in range(2):
        half = which_ref[0] if core == 0 else 1 - which_ref[0]
        own, left, right, far_up, far_down = refs[5 * core : 5 * core + 5]
        for step, up, down in (
            (0, own.at[0], own.at[1]),
            (3, left.at[0], left.at[1]),
            (1, right.at[0], right.at[1]),
            (2, far_up, far_down),
        ):
            chunk = half * 4 + (which_ref[1] + step) % 4
            here = pl.ds(pl.multiple_of(chunk * 256, 256), 256)
            up_ref[:, here] = up[...].astype(F32)
            down_ref[here, :] = jnp.transpose(down[...].astype(F32))


def dispatch_kernel(own_ref, above_ref, gain_ref, row_ref, send_ref, after_ref):
    after = jnp.concatenate([above_ref[...].astype(F32), own_ref[...]], axis=0)
    after_ref[...] = after
    unit, _ = normalised(after)
    normed = (unit * gain_ref[...]).astype(BF16)
    picks = iota((send_ref.shape[0], after.shape[0]), 0) == row_ref[...]
    send_ref[...] = nn(jnp.where(picks, 1.0, 0.0).astype(BF16), normed).astype(BF16)


def expert_kernel(in_ref, back_ref, w_up_ref, hidden_ref, pre_ref, out_ref, total, score):
    step = pl.program_id(0)
    rows = in_ref.shape[0]
    width = out_ref.shape[1] - 128

    @pl.when(step == 0)
    def _():
        total[...] = jnp.zeros_like(total)
        score[...] = jnp.zeros_like(score)

    w_up = w_up_ref[...]
    blocks = rows // EXPERT_ROWS
    places = [slice(block * EXPERT_ROWS, (block + 1) * EXPERT_ROWS) for block in range(blocks)]
    later = nn(in_ref[places[0], :], w_up)
    for block, here in enumerate(places):
        pre = later
        later = nn(in_ref[places[block + 1], :], w_up) if block + 1 < blocks else None
        cumulative, density = normal_of(pre)
        hidden = pre * cumulative
        back = back_ref[here, :].astype(F32)
        grad = (back * (cumulative + pre * density)).astype(BF16)
        hidden_ref[here, :] = hidden.astype(BF16)
        pre_ref[here, :] = grad
        product = hidden * back
        score[here, :] += sum(product[:, part : part + 128] for part in range(0, product.shape[1], 128))
        total[here, :] += nt(grad, w_up)

    @pl.when(step == pl.num_programs(0) - 1)
    def _():
        out_ref[:, :width] = total[...].astype(BF16)
        summed = jnp.sum(score[...], axis=1, keepdims=True)
        high = summed.astype(BF16).astype(F32)
        lane = iota((rows, 128), 1)
        tail = jnp.where(lane == 0, high, jnp.where(lane == 1, summed - high, 0.0))
        out_ref[:, width:] = tail.astype(BF16)


def combine_kernel(
    back_ref, col_ref, after_ref, grad_ref, order_ref, gain_ref, send_ref, own_ref, gain_out_ref, score_ref
):
    rows, width = after_ref.shape
    picks = iota((rows, back_ref.shape[0]), 1) == col_ref[...]
    picks = jnp.where(picks, 1.0, 0.0).astype(BF16)
    back = nn(picks, back_ref[...])
    score_ref[...] = back[:, width:]
    unit, scale = normalised(after_ref[...])
    grad, gain_grad = norm_backward(unit, scale, back[:, :width], gain_ref[...])
    gain_out_ref[...] = gain_grad
    order = order_ref[...]
    half = rows // 2
    send_ref[...] = (nn(order, grad_ref[:half, :]) + grad[:half]).astype(BF16)
    own_ref[...] = nn(order, grad_ref[half:, :]) + grad[half:]


def attend_backward_kernel(
    core_ref, own_ref, below_ref, order_t_ref, gain_ref, w_qkv_ref, w_proj_ref, qkv_ref, x_ref, normed_ref, mixed_ref,
    prob_ref, lined_ref, mine_ref, other_ref, kept_ref, send_ref, gain_out_ref, pair, cotangent, grad_mixed, grad_act,
    grad_qkv, grad_proj,
):
    group = pl.program_id(0)
    rows_all = x_ref.shape[0]
    wins = rows_all // TOKENS
    lanes = iota((TOKENS, 128), 1) // 32

    @pl.when(group == 0)
    def _():
        parts = []
        for win in range(wins):
            parts.append(own_ref[win * HALF : (win + 1) * HALF, :])
            parts.append(below_ref[...].astype(F32)[win * HALF : (win + 1) * HALF, :])
        cot = jnp.concatenate(parts, axis=0)
        cotangent[...] = cot
        mixed = nt(cot.astype(BF16), w_proj_ref[...]).astype(BF16)
        for i in range(4):
            grad_mixed[i] = mixed[:, 128 * i : 128 * i + 128]

    pair[...] = jnp.zeros_like(pair)

    def first_part(win):
        rows = slice(win * TOKENS, (win + 1) * TOKENS)
        value = qkv_ref[8 + group, rows, :]
        out = grad_mixed[group, rows, :]
        grad_probs, grad_value = [], None
        for head in range(4):
            own_out = jnp.where(lanes == head, out, jnp.zeros_like(out))
            grad_probs.append(nt(value, own_out))
            part = nn(prob_ref[head, win], own_out)
            grad_value = part if head == 0 else grad_value + part
        grad_act[8 + group, rows, :] = grad_value.astype(BF16)
        return grad_probs

    later = first_part(0)
    for win in range(wins):
        grad_probs = later
        later = first_part(win + 1) if win + 1 < wins else None
        rows = slice(win * TOKENS, (win + 1) * TOKENS)
        query = qkv_ref[group, rows, :]
        key_t = jnp.transpose(qkv_ref[4 + group, rows, :].astype(F32)).astype(BF16)
        grad_query, grad_key = [], None
        for head in range(4):
            own_query = jnp.where(lanes == head, query, jnp.zeros_like(query))
            prob = prob_ref[head, win].astype(F32)
            grad_prob = grad_probs[head].astype(BF16).astype(F32)
            weighted = prob * grad_prob
            grad_score = weighted - prob * jnp.sum(weighted, axis=0, keepdims=True)
            pair[head, :TOKENS, :TOKENS] += grad_score
            half_score = grad_score.astype(BF16)
            part = nn(half_score, own_query)
            grad_key = part if head == 0 else grad_key + part
            grad_query.append(nn(key_t[32 * head : 32 * head + 32], half_score))
        full_query = jnp.transpose(jnp.concatenate(grad_query, axis=0))
        grad_act[group, rows, :] = (full_query * SCALE).astype(BF16)
        grad_act[4 + group, rows, :] = (grad_key * SCALE).astype(BF16)

    for head in range(4):
        total = pair[head, (WINDOW - 1) * WINDOW : (WINDOW - 1) * WINDOW + 16, :]
        for row in range(WINDOW - 1):
            start = (WINDOW - 1 - row) * WINDOW
            total = total + pltpu.roll(pair[head, row * WINDOW : row * WINDOW + 16, :], start, 1)
        lined_ref[head] = total

    @pl.when(group == pl.num_programs(0) - 1)
    def _():
        act = jnp.concatenate([grad_act[i] for i in range(12)], axis=1)
        normed_t = jnp.transpose(normed_ref[...].astype(F32)).astype(BF16)
        mixed_t = jnp.transpose(mixed_ref[...].astype(F32)).astype(BF16)
        cot = cotangent[...]
        grad_proj[...] = nn(mixed_t, cot.astype(BF16)).astype(BF16)
        grad_qkv[...] = nn(normed_t, act).astype(BF16)

        def scatter(half_ref, first):
            for row in range(16):
                here = slice(first + 16 * row, first + 16 * row + 16)
                for col in range(4):
                    half_ref[4 * row + col, :, :384] = grad_qkv[here, 384 * col : 384 * col + 384]
                    half_ref[4 * row + col, :, 384:] = grad_proj[here, 128 * col : 128 * col + 128]

        @pl.when(core_ref[0] == 0)
        def _():
            scatter(mine_ref, 0)
            scatter(other_ref, 256)

        @pl.when(core_ref[0] != 0)
        def _():
            scatter(other_ref, 0)
            scatter(mine_ref, 256)

        grad_normed = nt(act, w_qkv_ref[...])
        unit, scale = normalised(x_ref[...].astype(F32))
        grad, gain_grad = norm_backward(unit, scale, grad_normed, gain_ref[...])
        gain_out_ref[...] = gain_grad
        total = cot + grad
        kept = [total[win * TOKENS : win * TOKENS + HALF] for win in range(wins)]
        away = [total[win * TOKENS + HALF : (win + 1) * TOKENS] for win in range(wins)]
        order_t = order_t_ref[...]
        kept_ref[...] = nn(order_t, jnp.concatenate(kept, axis=0).astype(BF16)).astype(BF16)
        send_ref[...] = nn(order_t, jnp.concatenate(away, axis=0).astype(BF16)).astype(BF16)


def on_device(
    image, grad_out, gate, routes, gain_one, w_qkv, w_proj, table, gain_two, w_fc1, w_fc2
):
    tile_count = lax.axis_size("tile")
    tile_index = lax.axis_index("tile")
    strip_height, columns, channels = image.shape[1:]
    wins = columns // WINDOW
    rows = strip_height * columns
    half = rows // 2
    capacity = 2 * rows // tile_count
    slots = tile_count * capacity
    ffn = w_fc1.shape[2]
    core = lax.axis_index("core").reshape(1).astype(jnp.int32)
    exchange = functools.partial(lax.all_to_all, split_axis=0, concat_axis=0, tiled=True)
    pick = half_order(wins)
    order = jnp.asarray(pick, BF16)
    order_t = jnp.asarray(pick.T, BF16)
    order_all = jnp.asarray(np.kron(np.eye(2), pick), BF16)
    targets = jnp.asarray(bias_targets())
    gain_one = gain_one.reshape(1, channels)
    gain_two = gain_two.reshape(1, channels)
    image_rows = image.reshape(rows, channels)
    grad_rows = grad_out.reshape(rows, channels)
    gate_row = gate.reshape(1, rows)

    below = shifted(image_rows[:half], "tile", -1)
    send_grad, place_row, place_col = call(
        functools.partial(route_kernel, capacity),
        (shape((slots, channels), BF16), shape((1, rows), jnp.int32), shape((rows, 1), jnp.int32)),
        cost=(700000000, 3000000, 0),
        limit=LARGE_LIMIT,
    )(routes.reshape(1, rows), gate_row, grad_rows, order_all)
    recv_grad = exchange(send_grad, "tile")
    bias = call(
        bias_kernel,
        shape((HEADS, TOKENS, TOKENS), F32),
        scratch=[pltpu.VMEM((16, HEADS, SPAN), F32)],
        cost=(400000000, 3000000, 0),
    )(jnp.pad(table, ((0, 0), (0, TABLE_PAD - table.shape[1]))), targets)
    mask = window_masks(jnp.reshape(tile_index == tile_count - 1, (1,)), wins)[wins - 2 :]

    head_block = pl.BlockSpec((4, wins, TOKENS, TOKENS), lambda g: (g, 0, 0, 0))
    pair_block = pl.BlockSpec((4, TOKENS, TOKENS), lambda g: (g, 0, 0))
    prob, qkv_act, windows, normed_one, mixed, own_after, send_after = call(
        attend_kernel,
        (
            shape((HEADS, wins, TOKENS, TOKENS), BF16),
            shape((12, rows, 128), BF16),
            shape((rows, channels), BF16),
            shape((rows, channels), BF16),
            shape((rows, channels), BF16),
            shape((half, channels), F32),
            shape((half, channels), BF16),
        ),
        grid=(4,),
        in_specs=[
            pl.BlockSpec((half, channels), lambda g: (1, 0)),
            whole(half, channels),
            whole(half, half),
            whole(1, channels),
            whole(channels, 3 * channels),
            whole(channels, channels),
            pair_block,
            whole(2, TOKENS, TOKENS),
        ],
        out_specs=(
            head_block,
            whole(12, rows, 128),
            whole(rows, channels),
            whole(rows, channels),
            whole(rows, channels),
            whole(half, channels),
            whole(half, channels),
        ),
        scratch=[pltpu.VMEM((4, rows, 128), BF16)],
        cost=(3000000000, 12000000, 2000000),
        limit=LARGE_LIMIT,
    )(image_rows, below, order, gain_one, w_qkv, w_proj, bias, mask)

    above = shifted(send_after, "tile", 1)
    send_in, after = call(
        dispatch_kernel,
        (shape((slots, channels), BF16), shape((rows, channels), F32)),
        cost=(700000000, 4000000, 0),
    )(own_after, above, gain_two, place_row)
    recv_in = exchange(send_in, "tile")

    w_up, w_down = w_fc1[0], w_fc2[0]
    grad_hidden = jnp.dot(recv_grad, w_down.T, preferred_element_type=F32).astype(BF16)
    chunk = 512
    strip = pl.BlockSpec((slots, chunk), lambda f: (0, f))
    hidden, grad_pre, send_back = call(
        expert_kernel,
        (
            shape((slots, ffn), BF16),
            shape((slots, ffn), BF16),
            shape((slots, channels + 128), BF16),
        ),
        grid=(ffn // chunk,),
        in_specs=[whole(slots, channels), strip, pl.BlockSpec((channels, chunk), lambda f: (0, f))],
        out_specs=(strip, strip, whole(slots, channels + 128)),
        scratch=[pltpu.VMEM((slots, channels), F32), pltpu.VMEM((slots, 128), F32)],
        cost=(4800000000, 20000000, 5000000),
        limit=LARGE_LIMIT,
    )(recv_in, grad_hidden, w_up)
    recv_back = exchange(send_back, "tile")
    place_x = lax.axis_index("x").astype(jnp.int32)
    mine_at = jnp.stack([core[0], place_x])
    other_at = jnp.stack([1 - core[0], place_x])
    wide = shape((channels, slots), BF16)
    flip = call(flip_kernel, wide, cost=LIGHT)
    grad_t, in_t = flip(recv_grad), flip(recv_in)
    other_part = weight_grads(other_at, grad_pre, hidden, in_t, grad_t)
    other_part = [shifted(part, "core", 1) for part in other_part]
    mine_part = weight_grads(mine_at, grad_pre, hidden, in_t, grad_t, other_part)
    far_up, far_down = shifted(mine_part[4], "x", 1), shifted(mine_part[5], "x", -1)
    recv_back, mine_part, far_up, far_down = lax.optimization_barrier((recv_back, mine_part, far_up, far_down))
    chunk = shape((2, *mine_part[0].shape), BF16)
    to_right, to_left = call(relay_kernel, (chunk, chunk), cost=LIGHT)(
        mine_part[2], mine_part[3], mine_part[6], mine_part[7], far_up, far_down
    )
    from_left, from_right = shifted(to_right, "x", 1), shifted(to_left, "x", -1)
    recv_back, to_right, to_left = lax.optimization_barrier((recv_back, to_right, to_left))

    send_cot, own_cot, gain_two_part, score = call(
        combine_kernel,
        (
            shape((half, channels), BF16),
            shape((half, channels), F32),
            shape((1, channels), F32),
            shape((rows, 128), F32),
        ),
        cost=LIGHT,
    )(recv_back, place_col, after, grad_rows, order, gain_two)
    below_cot = shifted(send_cot, "tile", -1)
    below_cot, from_left, from_right = lax.optimization_barrier((below_cot, from_left, from_right))
    owned = call(owned_kernel, chunk, cost=LIGHT)(mine_part[0], mine_part[1], from_left, from_right)
    below_cot, owned = lax.optimization_barrier((below_cot, owned))
    left, right = shifted(owned, "x", 1), shifted(owned, "x", -1)

    half_pieces = shape((OWNERS, 16, 512), BF16)
    lined, mine, other, kept, send_up, gain_one_part = call(
        attend_backward_kernel,
        (
            shape((HEADS, 16, SPAN), F32),
            half_pieces,
            half_pieces,
            shape((half, channels), BF16),
            shape((half, channels), BF16),
            shape((1, channels), F32),
        ),
        grid=(4,),
        in_specs=[
            pl.BlockSpec(memory_space=pltpu.SMEM),
            whole(half, channels),
            whole(half, channels),
            whole(half, half),
            whole(1, channels),
            whole(channels, 3 * channels),
            whole(channels, channels),
            whole(12, rows, 128),
            whole(rows, channels),
            whole(rows, channels),
            whole(rows, channels),
            head_block,
        ],
        out_specs=(
            pl.BlockSpec((4, 16, SPAN), lambda g: (g, 0, 0)),
            whole(OWNERS, 16, 512),
            whole(OWNERS, 16, 512),
            whole(half, channels),
            whole(half, channels),
            whole(1, channels),
        ),
        scratch=[
            pltpu.VMEM((4, TOKENS + 16, SPAN), F32),
            pltpu.VMEM((rows, channels), F32),
            pltpu.VMEM((4, rows, 128), BF16),
            pltpu.VMEM((12, rows, 128), BF16),
            pltpu.VMEM((channels, 3 * channels), BF16),
            pltpu.VMEM((channels, channels), BF16),
        ],
        cost=LIGHT,
        limit=LARGE_LIMIT,
    )(core, own_cot, below_cot, order_t, gain_one, w_qkv, w_proj, qkv_act, windows, normed_one, mixed, prob)
    lined, mine, other, send_up, gain_one_part, left, right = lax.optimization_barrier(
        (lined, mine, other, send_up, gain_one_part, left, right)
    )
    upper = shifted(send_up, "tile", 1)
    other = shifted(other, "core", 1)
    small = call(
        table_kernel,
        shape((OWNERS, 16, 128), F32),
        cost=LIGHT,
    )(lined, targets, gain_one_part, gain_two_part)
    upper, other, small = lax.optimization_barrier((upper, other, small))
    pieces = shape((OWNERS, 16, 640), BF16)
    merged = call(merge_kernel, pieces, cost=(0, 4000000, 0))(mine, other, small)
    merged, score = lax.optimization_barrier((merged, score))
    parts = exchange(merged, SAME_CORE)
    score = (score[:, 0] + score[:, 1]).reshape(2, wins, SHIFT, WINDOW)
    score = score.transpose(0, 2, 1, 3).reshape(strip_height, columns)
    grad_gate = jnp.roll(score, SHIFT, axis=1) / gate[0].astype(F32)
    far_up, far_down = shifted(left[0], "x", 1), shifted(right[1], "x", -1)
    parts, far_up, far_down = lax.optimization_barrier((parts, far_up, far_down))
    summed = call(sum_kernel, pieces, cost=LIGHT)(parts)
    chunks = [owned, left, right, far_up, far_down]
    chunks = chunks + [shifted(value, "core", 1) for value in chunks]
    grad_image = jnp.concatenate([upper, kept], axis=0).reshape(image.shape)
    summed_up, summed_down = call(
        assemble_kernel,
        (shape((channels, ffn), F32), shape((ffn, channels), F32)),
        grid=(1,),
        in_specs=[pl.BlockSpec(memory_space=pltpu.SMEM)] + ([whole(*chunk.shape)] * 3 + [whole(*chunk.shape[1:])] * 2) * 2,
        out_specs=(whole(channels, ffn), whole(ffn, channels)),
        cost=LIGHT,
    )(mine_at, *chunks)
    gathered = exchange(summed, SAME_CORE)
    gathered, summed_up, summed_down, grad_image, grad_gate = lax.optimization_barrier(
        (gathered, summed_up, summed_down, grad_image, grad_gate)
    )
    grad_qkv, grad_proj, small_all = call(
        unpack_kernel,
        (
            shape((channels, 3 * channels), F32),
            shape((channels, channels), F32),
            shape((OWNERS, 16, 128), F32),
        ),
        grid=(1,),
        in_specs=[pl.BlockSpec(memory_space=pltpu.SMEM), whole(OWNERS, 16, 640), whole(OWNERS, 16, 640)],
        out_specs=(whole(channels, 3 * channels), whole(channels, channels), whole(OWNERS, 16, 128)),
        cost=(0, 7000000, 0),
    )(core, gathered, shifted(gathered, "core", 1))
    small_all = small_all[:, :2, :].reshape(2 * OWNERS, 128)
    first = HEADS * TABLE_PAD // 128
    grad_table = small_all[:first].reshape(HEADS, TABLE_PAD)[:, : table.shape[1]]
    grad_gain_one = small_all[first : first + 4].reshape(channels)
    grad_gain_two = small_all[first + 4 : first + 8].reshape(channels)
    return (
        grad_image,
        grad_gate.reshape(1, strip_height, columns),
        summed_up.reshape(1, channels, ffn),
        summed_down.reshape(1, ffn, channels),
        grad_qkv,
        grad_proj,
        grad_table,
        grad_gain_one,
        grad_gain_two,
    )


def solution(mesh):
    devices = mesh.devices
    split = jax.sharding.Mesh(devices.reshape(-1, 2, devices.shape[1]), ("x", "core", "tile"))
    return jax.shard_map(
        on_device,
        mesh=split,
        in_specs=(
            P(GROUP, "tile", None, None),
            P(GROUP, "tile", None, None),
            P(GROUP, "tile", None),
            P(GROUP, "tile", None, None),
            P(),
            P(),
            P(),
            P(),
            P(),
            P("tile", None, None),
            P("tile", None, None),
        ),
        out_specs=(
            P(GROUP, "tile", None, None),
            P(GROUP, "tile", None),
            P("tile", None, None),
            P("tile", None, None),
            P(),
            P(),
            P(),
            P(),
            P(),
        ),
        check_vma=False,
    )
```

```python
import functools

import jax
import jax.numpy as jnp
import numpy as np
from jax import lax
from jax.experimental import pallas as pl
from jax.experimental.pallas import tpu as pltpu
from jax.sharding import PartitionSpec as P

HEADS = 16
WINDOW = 12
SHIFT = 6
TOKENS = WINDOW * WINDOW
HALF = TOKENS // 2
SIDE = 2 * WINDOW - 1
SPAN = 384
TABLE_PAD = 640
SCALE = 32**-0.5
EXPERT_ROWS = 384
TAIL_BASE = 2.702702760696411
TAIL = (
    0.398942202,
    1.07827175,
    2.51046658,
    4.81238174,
    1.92840862,
    25.174448,
    -204.768677,
    384.889191,
    -241.165222,
)
VMEM_LIMIT = 40 * 1024 * 1024
LARGE_LIMIT = 60 * 1024 * 1024
F32 = jnp.float32
BF16 = jnp.bfloat16
GROUP = ("x", "core")
SAME_CORE = ("x", "tile")
OWNERS = 64
LIGHT = (1000000, 100000, 0)


def nn(a, b):
    return lax.dot_general(a, b, (((1,), (0,)), ((), ())), preferred_element_type=F32)


def nt(a, b):
    return lax.dot_general(a, b, (((1,), (1,)), ((), ())), preferred_element_type=F32)


def tn(a, b):
    return lax.dot_general(a, b, (((0,), (0,)), ((), ())), preferred_element_type=F32)


def call(kernel, outs, *, grid=None, in_specs=None, out_specs=None, scratch=(), cost=None, limit=VMEM_LIMIT, scalars=0):
    extra = dict(scratch_shapes=list(scratch))
    if scalars:
        spec = pltpu.PrefetchScalarGridSpec(
            num_scalar_prefetch=scalars, grid=grid, in_specs=in_specs, out_specs=out_specs, scratch_shapes=list(scratch)
        )
        extra = dict(grid_spec=spec)
    elif grid is not None:
        extra.update(grid=grid, in_specs=in_specs, out_specs=out_specs)
    if cost is not None:
        extra["cost_estimate"] = pl.CostEstimate(flops=cost[0], bytes_accessed=cost[1], transcendentals=cost[2])
    return pl.pallas_call(
        kernel, out_shape=outs, compiler_params=pltpu.CompilerParams(vmem_limit_bytes=limit), **extra
    )


def shape(dims, dtype):
    return jax.ShapeDtypeStruct(dims, dtype)


def whole(*dims):
    return pl.BlockSpec(dims, lambda *_: (0,) * len(dims))


def shifted(value, axis, steps):
    count = lax.axis_size(axis)
    pairs = [(source, (source + steps) % count) for source in range(count)]
    return lax.ppermute(value, axis, pairs)


def half_order(col_windows):
    columns = col_windows * WINDOW
    pick = np.zeros((SHIFT * columns, SHIFT * columns), np.float32)
    for win in range(col_windows):
        for row in range(SHIFT):
            for col in range(WINDOW):
                source = row * columns + (win * WINDOW + SHIFT + col) % columns
                pick[win * HALF + row * WINDOW + col, source] = 1.0
    return pick


def bias_targets():
    lane = np.arange(SPAN)
    target = (lane // WINDOW) * SIDE + lane % WINDOW + WINDOW - 1
    return np.where(lane < SIDE * WINDOW, target, -1000).astype(np.int32)[None]


def window_masks(row_last, col_windows):
    inner_pos = jnp.arange(TOKENS, dtype=jnp.int32)
    row_in = inner_pos // WINDOW
    col_in = inner_pos % WINDOW
    row_region = jnp.where(row_last[:, None], jnp.where(row_in < SHIFT, 1, 2)[None], 0)
    col_last = jnp.arange(col_windows, dtype=jnp.int32) == col_windows - 1
    col_region = jnp.where(col_last[:, None], jnp.where(col_in < SHIFT, 1, 2)[None], 0)
    region = (row_region[:, None, :] * 3 + col_region[None, :, :]).reshape(-1, TOKENS)
    same = region[:, :, None] == region[:, None, :]
    return jnp.where(same, 0.0, -100.0).astype(F32)


def normalised(values):
    mean = jnp.mean(values, axis=-1, keepdims=True)
    centred = values - mean
    scale = lax.rsqrt(jnp.mean(centred * centred, axis=-1, keepdims=True) + 1e-05)
    return centred * scale, scale


def norm_backward(unit, scale, grad, gain):
    weighted = grad * gain
    along = jnp.mean(weighted * unit, axis=-1, keepdims=True)
    flat = jnp.mean(weighted, axis=-1, keepdims=True)
    return scale * (weighted - flat - unit * along), jnp.sum(grad * unit, axis=0, keepdims=True)


def normal_of(values):
    bell = jnp.exp2(values * values * -0.7213475204444817)
    inverse = pl.reciprocal(TAIL_BASE + jnp.abs(values))
    ratio = inverse * TAIL[-1] + TAIL[-2]
    for factor in TAIL[-3::-1]:
        ratio = ratio * inverse + factor
    tail = bell * (ratio * inverse)
    return jnp.where(values < 0.0, tail, 1.0 - tail), bell * 0.3989422804014327


def iota(dims, axis):
    return lax.broadcasted_iota(jnp.int32, dims, axis)


def spread_matrix(targets, col):
    hit = iota((TABLE_PAD, SPAN), 0) == targets - col
    return jnp.where(hit, 1.0, 0.0).astype(BF16)


def pieces_of(value, count):
    parts = []
    for _ in range(count):
        part = value.astype(BF16)
        parts.append(part)
        value = value - part.astype(F32)
    return parts


def route_kernel(capacity, routes_ref, gate_ref, grad_ref, order_ref, send_ref, row_ref, col_ref):
    rows = grad_ref.shape[0]
    slots = send_ref.shape[0]
    routes = routes_ref[...]
    chosen = jnp.where(iota((HEADS, rows), 0) == routes, 1.0, 0.0)
    upto = jnp.where(iota((rows, rows), 0) <= iota((rows, rows), 1), 1.0, 0.0).astype(BF16)
    running = nn(chosen.astype(BF16), upto)
    slot = jnp.sum(running * chosen, axis=0, keepdims=True) - 1.0
    expert = routes.astype(F32)
    place = (expert * capacity + slot).astype(jnp.int32)
    picks = jnp.where(iota((slots, rows), 0) == place, gate_ref[...].astype(F32), 0.0).astype(BF16)
    send_ref[...] = nn(picks, grad_ref[...]).astype(BF16)
    order = order_ref[...]
    both = jnp.concatenate(
        [jnp.broadcast_to(expert, (8, rows)), jnp.broadcast_to(slot, (8, rows))], axis=0
    ).astype(BF16)
    moved = nt(both, order)
    there = moved[0:1] * capacity + moved[8:9]
    row_ref[...] = there.astype(jnp.int32)
    same = iota((rows, rows), 0) == iota((rows, rows), 1)
    col_ref[...] = jnp.sum(jnp.where(same, there, 0.0), axis=1, keepdims=True).astype(jnp.int32)


def bias_kernel(table_ref, targets_ref, bias_ref, spread):
    table = jnp.concatenate(pieces_of(table_ref[...], 3), axis=0)
    for col in range(16):
        part = nn(table, spread_matrix(targets_ref[...], col % WINDOW))
        spread[col] = part[0:HEADS] + part[HEADS : 2 * HEADS] + part[2 * HEADS :]
    for head in range(HEADS):
        rows = spread[:, head, :]
        for row in range(WINDOW):
            start = (WINDOW - 1 - row) * WINDOW
            turned = pltpu.roll(rows, (SPAN - start) % SPAN, 1) if start else rows
            bias_ref[head, row * WINDOW : (row + 1) * WINDOW, :] = turned[:WINDOW, :TOKENS]


def table_kernel(lined, targets_ref, gain_one_ref, gain_two_ref, out_ref):
    grads = jnp.zeros((2 * HEADS, TABLE_PAD), F32)
    for col in range(WINDOW):
        value = jnp.concatenate(pieces_of(lined[:, col, :], 2), axis=0)
        grads = grads + nt(value, spread_matrix(targets_ref[...], col))
    grads = grads[:HEADS] + grads[HEADS:]
    out_ref[...] = jnp.zeros_like(out_ref)
    lines = [grads[head : head + 1, 128 * part : 128 * part + 128] for head in range(HEADS) for part in range(5)]
    for gain_ref in (gain_one_ref, gain_two_ref):
        lines += [gain_ref[:, 128 * part : 128 * part + 128] for part in range(4)]
    for number, line in enumerate(lines):
        high, low = pieces_of(line, 2)
        out_ref[number // 2, number % 2 : number % 2 + 1, :] = high.astype(F32)
        out_ref[number // 2, 2 + number % 2 : 3 + number % 2, :] = low.astype(F32)


def merge_kernel(mine_ref, other_ref, small_ref, out_ref):
    for owner in range(OWNERS):
        both = mine_ref[owner].astype(F32) + other_ref[owner].astype(F32)
        out_ref[owner, :, :512] = both.astype(BF16)
        out_ref[owner, :, 512:] = small_ref[owner].astype(BF16)


def sum_kernel(all_ref, out_ref):
    total = all_ref[0].astype(F32)
    for owner in range(1, OWNERS):
        total = total + all_ref[owner].astype(F32)
    small = total[:, 512:]
    small = small + pltpu.roll(small, 14, 0)
    high = small.astype(BF16).astype(F32)
    low = pltpu.roll(small - high, 2, 0)
    row = iota(small.shape, 0)
    small = jnp.where(row < 2, high, jnp.where(row < 4, low, 0.0))
    total = jnp.concatenate([total[:, :512], small], axis=1).astype(BF16)
    for owner in range(OWNERS):
        out_ref[owner] = total


def unpack_kernel(core_ref, mine_ref, other_ref, qkv_ref, proj_ref, small_ref):
    def place(half_ref, first):
        for row in range(16):
            here = slice(first + 16 * row, first + 16 * row + 16)
            for col in range(4):
                block = half_ref[4 * row + col].astype(F32)
                qkv_ref[here, 384 * col : 384 * col + 384] = block[:, :384]
                proj_ref[here, 128 * col : 128 * col + 128] = block[:, 384:512]

    @pl.when(core_ref[0] == 0)
    def _():
        place(mine_ref, 0)
        place(other_ref, 256)

    @pl.when(core_ref[0] != 0)
    def _():
        place(other_ref, 0)
        place(mine_ref, 256)

    for owner in range(OWNERS):
        small = mine_ref[owner, :, 512:].astype(F32) + other_ref[owner, :, 512:].astype(F32)
        small_ref[owner] = small + pltpu.roll(small, 14, 0)


def attend_kernel(
    image_ref, below_ref, order_ref, gain_ref, w_qkv_ref, w_proj_ref, bias_ref, mask_ref,
    prob_ref, qkv_ref, x_ref, normed_ref, mixed_ref, own_ref, send_ref, blended,
):
    group = pl.program_id(0)
    wins = x_ref.shape[0] // TOKENS
    lanes = iota((TOKENS, 128), 1) // 32

    @pl.when(group == 0)
    def _():
        order = order_ref[...]
        upper = nn(order, image_ref[...])
        lower = nn(order, below_ref[...])
        parts = []
        for win in range(wins):
            parts.append(upper[win * HALF : (win + 1) * HALF])
            parts.append(lower[win * HALF : (win + 1) * HALF])
        x = jnp.concatenate(parts, axis=0)
        x_ref[...] = x.astype(BF16)
        unit, _ = normalised(x)
        normed_ref[...] = (unit * gain_ref[...]).astype(BF16)
        normed = normed_ref[...]
        for pair in range(6):
            act = nn(normed, w_qkv_ref[:, 256 * pair : 256 * pair + 256]).astype(BF16)
            qkv_ref[2 * pair] = act[:, :128]
            qkv_ref[2 * pair + 1] = act[:, 128:]

    def scores_of(win):
        rows = slice(win * TOKENS, (win + 1) * TOKENS)
        query = qkv_ref[group, rows, :]
        key = qkv_ref[4 + group, rows, :]
        return [nt(key, jnp.where(lanes == head, query, jnp.zeros_like(query))) for head in range(4)]

    later = scores_of(0)
    for win in range(wins):
        scores = later
        later = scores_of(win + 1) if win + 1 < wins else None
        rows = slice(win * TOKENS, (win + 1) * TOKENS)
        value_t = jnp.transpose(qkv_ref[8 + group, rows, :].astype(F32)).astype(BF16)
        mask = mask_ref[int(win == wins - 1)]
        mixes = []
        for head in range(4):
            score = scores[head] * SCALE + (bias_ref[head] + mask)
            score = jnp.exp(score - jnp.max(score, axis=0, keepdims=True))
            prob = (score * (1.0 / jnp.sum(score, axis=0, keepdims=True))).astype(BF16)
            prob_ref[head, win] = prob
            mixes.append(nn(value_t[32 * head : 32 * head + 32], prob))
        mix = jnp.transpose(jnp.concatenate(mixes, axis=0))
        blended[group, rows, :] = mix.astype(BF16)

    @pl.when(group == pl.num_programs(0) - 1)
    def _():
        mixed = jnp.concatenate([blended[i] for i in range(4)], axis=1)
        mixed_ref[...] = mixed
        after = x_ref[...].astype(F32) + nn(mixed, w_proj_ref[...])
        kept = [after[win * TOKENS : win * TOKENS + HALF] for win in range(wins)]
        away = [after[win * TOKENS + HALF : (win + 1) * TOKENS] for win in range(wins)]
        own_ref[...] = jnp.concatenate(kept, axis=0)
        send_ref[...] = jnp.concatenate(away, axis=0).astype(BF16)


def weight_kernel(which_ref, pre_ref, hidden_ref, in_ref, grad_ref, *rest):
    step = pl.program_id(0)
    up, down = tn(pre_ref[0], in_ref[...]), tn(hidden_ref[0], grad_ref[...])
    for number, out_ref in enumerate(rest[-4:]):

        @pl.when(step == number)
        def _():
            if len(rest) > 4:
                out_ref[0] = (up + rest[number][0].astype(F32)).astype(BF16)
                out_ref[1] = (down + rest[number][1].astype(F32)).astype(BF16)
            else:
                out_ref[0] = up.astype(BF16)
                out_ref[1] = down.astype(BF16)


def weight_grads(which, grad_pre, hidden, recv_in, recv_grad, added=()):
    _, slots, chunk = hidden.shape
    width = recv_in.shape[1]
    strip = pl.BlockSpec((1, slots, chunk), lambda s, which: (which[0] * 4 + (which[1] + s) % 4, 0, 0))
    block = whole(2, chunk, width)
    return call(
        weight_kernel,
        (shape((2, chunk, width), BF16),) * 4,
        grid=(4,),
        in_specs=[strip, strip, whole(slots, width), whole(slots, width)] + [block] * len(added),
        out_specs=(block,) * 4,
        scalars=1,
        cost=LIGHT,
        limit=LARGE_LIMIT,
    )(which, grad_pre, hidden, recv_in, recv_grad, *added)


def relay_kernel(next_in_ref, last_in_ref, up_ref, down_ref, next_ref, last_ref):
    next_ref[0] = (next_in_ref[0].astype(F32) + up_ref[...].astype(F32)).astype(BF16)
    next_ref[1] = next_in_ref[1]
    last_ref[0] = last_in_ref[0]
    last_ref[1] = (last_in_ref[1].astype(F32) + down_ref[...].astype(F32)).astype(BF16)


def owned_kernel(own_ref, left_ref, right_ref, out_ref):
    total = own_ref[...].astype(F32) + left_ref[...].astype(F32) + right_ref[...].astype(F32)
    out_ref[...] = total.astype(BF16)


def assemble_kernel(which_ref, *refs):
    up_ref, down_ref = refs[-2:]
    for core in range(2):
        half = which_ref[0] if core == 0 else 1 - which_ref[0]
        own, left, right, far_up, far_down = refs[5 * core : 5 * core + 5]
        for step, up, down in (
            (0, own.at[0], own.at[1]),
            (3, left.at[0], left.at[1]),
            (1, right.at[0], right.at[1]),
            (2, far_up, far_down),
        ):
            chunk = half * 4 + (which_ref[1] + step) % 4
            here = pl.ds(pl.multiple_of(chunk * 256, 256), 256)
            up_ref[:, here] = jnp.transpose(up[...].astype(F32))
            down_ref[here, :] = down[...].astype(F32)


def dispatch_kernel(own_ref, above_ref, gain_ref, row_ref, send_ref, after_ref):
    after = jnp.concatenate([above_ref[...].astype(F32), own_ref[...]], axis=0)
    after_ref[...] = after
    unit, _ = normalised(after)
    normed = (unit * gain_ref[...]).astype(BF16)
    picks = iota((send_ref.shape[0], after.shape[0]), 0) == row_ref[...]
    send_ref[...] = nn(jnp.where(picks, 1.0, 0.0).astype(BF16), normed).astype(BF16)


def expert_kernel(in_ref, back_ref, w_up_ref, hidden_ref, pre_ref, out_ref, total, score):
    step = pl.program_id(0)
    rows = in_ref.shape[0]
    width = out_ref.shape[1] - 128

    @pl.when(step == 0)
    def _():
        total[...] = jnp.zeros_like(total)
        score[...] = jnp.zeros_like(score)

    w_up = w_up_ref[...]
    blocks = rows // EXPERT_ROWS
    places = [slice(block * EXPERT_ROWS, (block + 1) * EXPERT_ROWS) for block in range(blocks)]
    later = nn(in_ref[places[0], :], w_up)
    for block, here in enumerate(places):
        pre = later
        later = nn(in_ref[places[block + 1], :], w_up) if block + 1 < blocks else None
        cumulative, density = normal_of(pre)
        hidden = pre * cumulative
        back = back_ref[here, :].astype(F32)
        grad = (back * (cumulative + pre * density)).astype(BF16)
        for part in range(hidden_ref.shape[0]):
            lanes = slice(256 * part, 256 * part + 256)
            hidden_ref[part, here, :] = hidden[:, lanes].astype(BF16)
            pre_ref[part, here, :] = grad[:, lanes]
        product = hidden * back
        score[here, :] += sum(product[:, part : part + 128] for part in range(0, product.shape[1], 128))
        total[here, :] += nt(grad, w_up)

    @pl.when(step == pl.num_programs(0) - 1)
    def _():
        out_ref[:, :width] = total[...].astype(BF16)
        summed = jnp.sum(score[...], axis=1, keepdims=True)
        high = summed.astype(BF16).astype(F32)
        lane = iota((rows, 128), 1)
        tail = jnp.where(lane == 0, high, jnp.where(lane == 1, summed - high, 0.0))
        out_ref[:, width:] = tail.astype(BF16)


def combine_kernel(
    back_ref, col_ref, after_ref, grad_ref, order_ref, gain_ref, send_ref, own_ref, gain_out_ref, score_ref
):
    rows, width = after_ref.shape
    picks = iota((rows, back_ref.shape[0]), 1) == col_ref[...]
    picks = jnp.where(picks, 1.0, 0.0).astype(BF16)
    back = nn(picks, back_ref[...])
    score_ref[...] = back[:, width:]
    unit, scale = normalised(after_ref[...])
    grad, gain_grad = norm_backward(unit, scale, back[:, :width], gain_ref[...])
    gain_out_ref[...] = gain_grad
    order = order_ref[...]
    half = rows // 2
    send_ref[...] = (nn(order, grad_ref[:half, :]) + grad[:half]).astype(BF16)
    own_ref[...] = nn(order, grad_ref[half:, :]) + grad[half:]


def attend_backward_kernel(
    core_ref, own_ref, below_ref, order_t_ref, gain_ref, w_qkv_ref, w_proj_ref, qkv_ref, x_ref, normed_ref, mixed_ref,
    prob_ref, lined_ref, mine_ref, other_ref, kept_ref, send_ref, gain_out_ref, pair, cotangent, grad_mixed, grad_act,
    grad_qkv, grad_proj,
):
    group = pl.program_id(0)
    rows_all = x_ref.shape[0]
    wins = rows_all // TOKENS
    lanes = iota((TOKENS, 128), 1) // 32

    @pl.when(group == 0)
    def _():
        parts = []
        for win in range(wins):
            parts.append(own_ref[win * HALF : (win + 1) * HALF, :])
            parts.append(below_ref[...].astype(F32)[win * HALF : (win + 1) * HALF, :])
        cot = jnp.concatenate(parts, axis=0)
        cotangent[...] = cot
        mixed = nt(cot.astype(BF16), w_proj_ref[...]).astype(BF16)
        for i in range(4):
            grad_mixed[i] = mixed[:, 128 * i : 128 * i + 128]

    pair[...] = jnp.zeros_like(pair)

    def first_part(win):
        rows = slice(win * TOKENS, (win + 1) * TOKENS)
        value = qkv_ref[8 + group, rows, :]
        out = grad_mixed[group, rows, :]
        grad_probs, grad_value = [], None
        for head in range(4):
            own_out = jnp.where(lanes == head, out, jnp.zeros_like(out))
            grad_probs.append(nt(value, own_out))
            part = nn(prob_ref[head, win], own_out)
            grad_value = part if head == 0 else grad_value + part
        grad_act[8 + group, rows, :] = grad_value.astype(BF16)
        return grad_probs

    later = first_part(0)
    for win in range(wins):
        grad_probs = later
        later = first_part(win + 1) if win + 1 < wins else None
        rows = slice(win * TOKENS, (win + 1) * TOKENS)
        query = qkv_ref[group, rows, :]
        key_t = jnp.transpose(qkv_ref[4 + group, rows, :].astype(F32)).astype(BF16)
        grad_query, grad_key = [], None
        for head in range(4):
            own_query = jnp.where(lanes == head, query, jnp.zeros_like(query))
            prob = prob_ref[head, win].astype(F32)
            grad_prob = grad_probs[head].astype(BF16).astype(F32)
            weighted = prob * grad_prob
            grad_score = weighted - prob * jnp.sum(weighted, axis=0, keepdims=True)
            pair[head, :TOKENS, :TOKENS] += grad_score
            half_score = grad_score.astype(BF16)
            part = nn(half_score, own_query)
            grad_key = part if head == 0 else grad_key + part
            grad_query.append(nn(key_t[32 * head : 32 * head + 32], half_score))
        full_query = jnp.transpose(jnp.concatenate(grad_query, axis=0))
        grad_act[group, rows, :] = (full_query * SCALE).astype(BF16)
        grad_act[4 + group, rows, :] = (grad_key * SCALE).astype(BF16)

    for head in range(4):
        total = pair[head, (WINDOW - 1) * WINDOW : (WINDOW - 1) * WINDOW + 16, :]
        for row in range(WINDOW - 1):
            start = (WINDOW - 1 - row) * WINDOW
            total = total + pltpu.roll(pair[head, row * WINDOW : row * WINDOW + 16, :], start, 1)
        lined_ref[head] = total

    @pl.when(group == pl.num_programs(0) - 1)
    def _():
        act = jnp.concatenate([grad_act[i] for i in range(12)], axis=1)
        normed_t = jnp.transpose(normed_ref[...].astype(F32)).astype(BF16)
        mixed_t = jnp.transpose(mixed_ref[...].astype(F32)).astype(BF16)
        cot = cotangent[...]
        grad_proj[...] = nn(mixed_t, cot.astype(BF16)).astype(BF16)
        grad_qkv[...] = nn(normed_t, act).astype(BF16)

        def scatter(half_ref, first):
            for row in range(16):
                here = slice(first + 16 * row, first + 16 * row + 16)
                for col in range(4):
                    half_ref[4 * row + col, :, :384] = grad_qkv[here, 384 * col : 384 * col + 384]
                    half_ref[4 * row + col, :, 384:] = grad_proj[here, 128 * col : 128 * col + 128]

        @pl.when(core_ref[0] == 0)
        def _():
            scatter(mine_ref, 0)
            scatter(other_ref, 256)

        @pl.when(core_ref[0] != 0)
        def _():
            scatter(other_ref, 0)
            scatter(mine_ref, 256)

        grad_normed = nt(act, w_qkv_ref[...])
        unit, scale = normalised(x_ref[...].astype(F32))
        grad, gain_grad = norm_backward(unit, scale, grad_normed, gain_ref[...])
        gain_out_ref[...] = gain_grad
        total = cot + grad
        kept = [total[win * TOKENS : win * TOKENS + HALF] for win in range(wins)]
        away = [total[win * TOKENS + HALF : (win + 1) * TOKENS] for win in range(wins)]
        order_t = order_t_ref[...]
        kept_ref[...] = nn(order_t, jnp.concatenate(kept, axis=0).astype(BF16)).astype(BF16)
        send_ref[...] = nn(order_t, jnp.concatenate(away, axis=0).astype(BF16)).astype(BF16)


def on_device(
    image, grad_out, gate, routes, gain_one, w_qkv, w_proj, table, gain_two, w_fc1, w_fc2
):
    tile_count = lax.axis_size("tile")
    tile_index = lax.axis_index("tile")
    strip_height, columns, channels = image.shape[1:]
    wins = columns // WINDOW
    rows = strip_height * columns
    half = rows // 2
    capacity = 2 * rows // tile_count
    slots = tile_count * capacity
    ffn = w_fc1.shape[2]
    core = lax.axis_index("core").reshape(1).astype(jnp.int32)
    exchange = functools.partial(lax.all_to_all, split_axis=0, concat_axis=0, tiled=True)
    pick = half_order(wins)
    order = jnp.asarray(pick, BF16)
    order_t = jnp.asarray(pick.T, BF16)
    order_all = jnp.asarray(np.kron(np.eye(2), pick), BF16)
    targets = jnp.asarray(bias_targets())
    gain_one = gain_one.reshape(1, channels)
    gain_two = gain_two.reshape(1, channels)
    image_rows = image.reshape(rows, channels)
    grad_rows = grad_out.reshape(rows, channels)
    gate_row = gate.reshape(1, rows)

    below = shifted(image_rows[:half], "tile", -1)
    send_grad, place_row, place_col = call(
        functools.partial(route_kernel, capacity),
        (shape((slots, channels), BF16), shape((1, rows), jnp.int32), shape((rows, 1), jnp.int32)),
        cost=(700000000, 3000000, 0),
    )(routes.reshape(1, rows), gate_row, grad_rows, order_all)
    recv_grad = exchange(send_grad, "tile")
    bias = call(
        bias_kernel,
        shape((HEADS, TOKENS, TOKENS), F32),
        scratch=[pltpu.VMEM((16, HEADS, SPAN), F32)],
        cost=(400000000, 3000000, 0),
    )(jnp.pad(table, ((0, 0), (0, TABLE_PAD - table.shape[1]))), targets)
    mask = window_masks(jnp.reshape(tile_index == tile_count - 1, (1,)), wins)[wins - 2 :]

    head_block = pl.BlockSpec((4, wins, TOKENS, TOKENS), lambda g: (g, 0, 0, 0))
    pair_block = pl.BlockSpec((4, TOKENS, TOKENS), lambda g: (g, 0, 0))
    prob, qkv_act, windows, normed_one, mixed, own_after, send_after = call(
        attend_kernel,
        (
            shape((HEADS, wins, TOKENS, TOKENS), BF16),
            shape((12, rows, 128), BF16),
            shape((rows, channels), BF16),
            shape((rows, channels), BF16),
            shape((rows, channels), BF16),
            shape((half, channels), F32),
            shape((half, channels), BF16),
        ),
        grid=(4,),
        in_specs=[
            pl.BlockSpec((half, channels), lambda g: (1, 0)),
            whole(half, channels),
            whole(half, half),
            whole(1, channels),
            whole(channels, 3 * channels),
            whole(channels, channels),
            pair_block,
            whole(2, TOKENS, TOKENS),
        ],
        out_specs=(
            head_block,
            whole(12, rows, 128),
            whole(rows, channels),
            whole(rows, channels),
            whole(rows, channels),
            whole(half, channels),
            whole(half, channels),
        ),
        scratch=[pltpu.VMEM((4, rows, 128), BF16)],
        cost=(3000000000, 12000000, 2000000),
        limit=LARGE_LIMIT,
    )(image_rows, below, order, gain_one, w_qkv, w_proj, bias, mask)

    above = shifted(send_after, "tile", 1)
    send_in, after = call(
        dispatch_kernel,
        (shape((slots, channels), BF16), shape((rows, channels), F32)),
        cost=(700000000, 4000000, 0),
    )(own_after, above, gain_two, place_row)
    recv_in = exchange(send_in, "tile")

    w_up, w_down = w_fc1[0], w_fc2[0]
    grad_hidden = jnp.dot(recv_grad, w_down.T, preferred_element_type=F32).astype(BF16)
    chunk = 512
    strip = pl.BlockSpec((slots, chunk), lambda f: (0, f))
    split = pl.BlockSpec((chunk // 256, slots, 256), lambda f: (f, 0, 0))
    hidden, grad_pre, send_back = call(
        expert_kernel,
        (
            shape((ffn // 256, slots, 256), BF16),
            shape((ffn // 256, slots, 256), BF16),
            shape((slots, channels + 128), BF16),
        ),
        grid=(ffn // chunk,),
        in_specs=[whole(slots, channels), strip, pl.BlockSpec((channels, chunk), lambda f: (0, f))],
        out_specs=(split, split, whole(slots, channels + 128)),
        scratch=[pltpu.VMEM((slots, channels), F32), pltpu.VMEM((slots, 128), F32)],
        cost=(4800000000, 20000000, 5000000),
        limit=LARGE_LIMIT,
    )(recv_in, grad_hidden, w_up)
    recv_back = exchange(send_back, "tile")
    place_x = lax.axis_index("x").astype(jnp.int32)
    mine_at = jnp.stack([core[0], place_x])
    other_at = jnp.stack([1 - core[0], place_x])
    other_part = weight_grads(other_at, grad_pre, hidden, recv_in, recv_grad)
    other_part = [shifted(part, "core", 1) for part in other_part]
    mine_part = weight_grads(mine_at, grad_pre, hidden, recv_in, recv_grad, other_part)
    recv_back, mine_part = lax.optimization_barrier((recv_back, mine_part))
    chunk = shape(mine_part[0].shape, BF16)
    far_up = shifted(mine_part[2][0], "x", 1)
    far_down = shifted(mine_part[2][1], "x", -1)

    send_cot, own_cot, gain_two_part, score = call(
        combine_kernel,
        (
            shape((half, channels), BF16),
            shape((half, channels), F32),
            shape((1, channels), F32),
            shape((rows, 128), F32),
        ),
        cost=LIGHT,
    )(recv_back, place_col, after, grad_rows, order, gain_two)
    below_cot = shifted(send_cot, "tile", -1)
    to_right, to_left = call(relay_kernel, (chunk, chunk), cost=LIGHT)(mine_part[1], mine_part[3], far_up, far_down)
    below_cot, to_right, to_left = lax.optimization_barrier((below_cot, to_right, to_left))
    from_left, from_right = shifted(to_right, "x", 1), shifted(to_left, "x", -1)
    half_pieces = shape((OWNERS, 16, 512), BF16)
    lined, mine, other, kept, send_up, gain_one_part = call(
        attend_backward_kernel,
        (
            shape((HEADS, 16, SPAN), F32),
            half_pieces,
            half_pieces,
            shape((half, channels), BF16),
            shape((half, channels), BF16),
            shape((1, channels), F32),
        ),
        grid=(4,),
        in_specs=[
            pl.BlockSpec(memory_space=pltpu.SMEM),
            whole(half, channels),
            whole(half, channels),
            whole(half, half),
            whole(1, channels),
            whole(channels, 3 * channels),
            whole(channels, channels),
            whole(12, rows, 128),
            whole(rows, channels),
            whole(rows, channels),
            whole(rows, channels),
            head_block,
        ],
        out_specs=(
            pl.BlockSpec((4, 16, SPAN), lambda g: (g, 0, 0)),
            whole(OWNERS, 16, 512),
            whole(OWNERS, 16, 512),
            whole(half, channels),
            whole(half, channels),
            whole(1, channels),
        ),
        scratch=[
            pltpu.VMEM((4, TOKENS + 16, SPAN), F32),
            pltpu.VMEM((rows, channels), F32),
            pltpu.VMEM((4, rows, 128), BF16),
            pltpu.VMEM((12, rows, 128), BF16),
            pltpu.VMEM((channels, 3 * channels), BF16),
            pltpu.VMEM((channels, channels), BF16),
        ],
        cost=LIGHT,
        limit=LARGE_LIMIT,
    )(core, own_cot, below_cot, order_t, gain_one, w_qkv, w_proj, qkv_act, windows, normed_one, mixed, prob)
    lined, mine, other, send_up, gain_one_part, from_left, from_right = lax.optimization_barrier(
        (lined, mine, other, send_up, gain_one_part, from_left, from_right)
    )
    owned = call(owned_kernel, chunk, cost=LIGHT)(mine_part[0], from_left, from_right)
    left, right = shifted(owned, "x", 1), shifted(owned, "x", -1)
    upper = shifted(send_up, "tile", 1)
    other = shifted(other, "core", 1)
    small = call(
        table_kernel,
        shape((OWNERS, 16, 128), F32),
        cost=LIGHT,
    )(lined, targets, gain_one_part, gain_two_part)
    upper, other, small = lax.optimization_barrier((upper, other, small))
    pieces = shape((OWNERS, 16, 640), BF16)
    merged = call(merge_kernel, pieces, cost=(0, 4000000, 0))(mine, other, small)
    merged, score = lax.optimization_barrier((merged, score))
    parts = exchange(merged, SAME_CORE)
    score = (score[:, 0] + score[:, 1]).reshape(2, wins, SHIFT, WINDOW)
    score = score.transpose(0, 2, 1, 3).reshape(strip_height, columns)
    grad_gate = jnp.roll(score, SHIFT, axis=1) / gate[0].astype(F32)
    far_up, far_down = shifted(left[0], "x", 1), shifted(right[1], "x", -1)
    parts, far_up, far_down = lax.optimization_barrier((parts, far_up, far_down))
    summed = call(sum_kernel, pieces, cost=LIGHT)(parts)
    chunks = [owned, left, right, far_up, far_down]
    chunks = chunks + [shifted(value, "core", 1) for value in chunks]
    grad_image = jnp.concatenate([upper, kept], axis=0).reshape(image.shape)
    summed_up, summed_down = call(
        assemble_kernel,
        (shape((channels, ffn), F32), shape((ffn, channels), F32)),
        grid=(1,),
        in_specs=[pl.BlockSpec(memory_space=pltpu.SMEM)] + ([whole(*chunk.shape)] * 3 + [whole(*chunk.shape[1:])] * 2) * 2,
        out_specs=(whole(channels, ffn), whole(ffn, channels)),
        cost=LIGHT,
    )(mine_at, *chunks)
    gathered = exchange(summed, SAME_CORE)
    gathered, summed_up, summed_down, grad_image, grad_gate = lax.optimization_barrier(
        (gathered, summed_up, summed_down, grad_image, grad_gate)
    )
    grad_qkv, grad_proj, small_all = call(
        unpack_kernel,
        (
            shape((channels, 3 * channels), F32),
            shape((channels, channels), F32),
            shape((OWNERS, 16, 128), F32),
        ),
        grid=(1,),
        in_specs=[pl.BlockSpec(memory_space=pltpu.SMEM), whole(OWNERS, 16, 640), whole(OWNERS, 16, 640)],
        out_specs=(whole(channels, 3 * channels), whole(channels, channels), whole(OWNERS, 16, 128)),
        cost=(0, 7000000, 0),
    )(core, gathered, shifted(gathered, "core", 1))
    small_all = small_all[:, :2, :].reshape(2 * OWNERS, 128)
    first = HEADS * TABLE_PAD // 128
    grad_table = small_all[:first].reshape(HEADS, TABLE_PAD)[:, : table.shape[1]]
    grad_gain_one = small_all[first : first + 4].reshape(channels)
    grad_gain_two = small_all[first + 4 : first + 8].reshape(channels)
    return (
        grad_image,
        grad_gate.reshape(1, strip_height, columns),
        summed_up.reshape(1, channels, ffn),
        summed_down.reshape(1, ffn, channels),
        grad_qkv,
        grad_proj,
        grad_table,
        grad_gain_one,
        grad_gain_two,
    )


def solution(mesh):
    devices = mesh.devices
    split = jax.sharding.Mesh(devices.reshape(-1, 2, devices.shape[1]), ("x", "core", "tile"))
    return jax.shard_map(
        on_device,
        mesh=split,
        in_specs=(
            P(GROUP, "tile", None, None),
            P(GROUP, "tile", None, None),
            P(GROUP, "tile", None),
            P(GROUP, "tile", None, None),
            P(),
            P(),
            P(),
            P(),
            P(),
            P("tile", None, None),
            P("tile", None, None),
        ),
        out_specs=(
            P(GROUP, "tile", None, None),
            P(GROUP, "tile", None),
            P("tile", None, None),
            P("tile", None, None),
            P(),
            P(),
            P(),
            P(),
            P(),
        ),
        check_vma=False,
    )
```

```python
import functools

import jax
import jax.numpy as jnp
import numpy as np
from jax import lax
from jax.experimental import pallas as pl
from jax.experimental.pallas import tpu as pltpu
from jax.sharding import PartitionSpec as P

HEADS = 16
WINDOW = 12
SHIFT = 6
TOKENS = WINDOW * WINDOW
HALF = TOKENS // 2
SIDE = 2 * WINDOW - 1
SPAN = 384
TABLE_PAD = 640
SCALE = 32**-0.5
EXPERT_ROWS = 384
TAIL_BASE = 2.702702760696411
TAIL = (
    0.398942202,
    1.07827175,
    2.51046658,
    4.81238174,
    1.92840862,
    25.174448,
    -204.768677,
    384.889191,
    -241.165222,
)
VMEM_LIMIT = 40 * 1024 * 1024
LARGE_LIMIT = 60 * 1024 * 1024
F32 = jnp.float32
BF16 = jnp.bfloat16
GROUP = ("x", "core")
SAME_CORE = ("x", "tile")
OWNERS = 64
LIGHT = (1000000, 100000, 0)


def nn(a, b):
    return lax.dot_general(a, b, (((1,), (0,)), ((), ())), preferred_element_type=F32)


def nt(a, b):
    return lax.dot_general(a, b, (((1,), (1,)), ((), ())), preferred_element_type=F32)


def tn(a, b):
    return lax.dot_general(a, b, (((0,), (0,)), ((), ())), preferred_element_type=F32)


def call(kernel, outs, *, grid=None, in_specs=None, out_specs=None, scratch=(), cost=None, limit=VMEM_LIMIT, scalars=0):
    extra = dict(scratch_shapes=list(scratch))
    if scalars:
        spec = pltpu.PrefetchScalarGridSpec(
            num_scalar_prefetch=scalars, grid=grid, in_specs=in_specs, out_specs=out_specs, scratch_shapes=list(scratch)
        )
        extra = dict(grid_spec=spec)
    elif grid is not None:
        extra.update(grid=grid, in_specs=in_specs, out_specs=out_specs)
    if cost is not None:
        extra["cost_estimate"] = pl.CostEstimate(flops=cost[0], bytes_accessed=cost[1], transcendentals=cost[2])
    return pl.pallas_call(
        kernel, out_shape=outs, compiler_params=pltpu.CompilerParams(vmem_limit_bytes=limit), **extra
    )


def shape(dims, dtype):
    return jax.ShapeDtypeStruct(dims, dtype)


def whole(*dims):
    return pl.BlockSpec(dims, lambda *_: (0,) * len(dims))


def shifted(value, axis, steps):
    count = lax.axis_size(axis)
    pairs = [(source, (source + steps) % count) for source in range(count)]
    return lax.ppermute(value, axis, pairs)


def half_order(col_windows):
    columns = col_windows * WINDOW
    pick = np.zeros((SHIFT * columns, SHIFT * columns), np.float32)
    for win in range(col_windows):
        for row in range(SHIFT):
            for col in range(WINDOW):
                source = row * columns + (win * WINDOW + SHIFT + col) % columns
                pick[win * HALF + row * WINDOW + col, source] = 1.0
    return pick


def bias_targets():
    lane = np.arange(SPAN)
    target = (lane // WINDOW) * SIDE + lane % WINDOW + WINDOW - 1
    return np.where(lane < SIDE * WINDOW, target, -1000).astype(np.int32)[None]


def window_masks(row_last, col_windows):
    inner_pos = jnp.arange(TOKENS, dtype=jnp.int32)
    row_in = inner_pos // WINDOW
    col_in = inner_pos % WINDOW
    row_region = jnp.where(row_last[:, None], jnp.where(row_in < SHIFT, 1, 2)[None], 0)
    col_last = jnp.arange(col_windows, dtype=jnp.int32) == col_windows - 1
    col_region = jnp.where(col_last[:, None], jnp.where(col_in < SHIFT, 1, 2)[None], 0)
    region = (row_region[:, None, :] * 3 + col_region[None, :, :]).reshape(-1, TOKENS)
    same = region[:, :, None] == region[:, None, :]
    return jnp.where(same, 0.0, -100.0).astype(F32)


def normalised(values):
    mean = jnp.mean(values, axis=-1, keepdims=True)
    centred = values - mean
    scale = lax.rsqrt(jnp.mean(centred * centred, axis=-1, keepdims=True) + 1e-05)
    return centred * scale, scale


def norm_backward(unit, scale, grad, gain):
    weighted = grad * gain
    along = jnp.mean(weighted * unit, axis=-1, keepdims=True)
    flat = jnp.mean(weighted, axis=-1, keepdims=True)
    return scale * (weighted - flat - unit * along), jnp.sum(grad * unit, axis=0, keepdims=True)


def normal_of(values):
    bell = jnp.exp2(values * values * -0.7213475204444817)
    inverse = pl.reciprocal(TAIL_BASE + jnp.abs(values))
    ratio = inverse * TAIL[-1] + TAIL[-2]
    for factor in TAIL[-3::-1]:
        ratio = ratio * inverse + factor
    tail = bell * (ratio * inverse)
    return jnp.where(values < 0.0, tail, 1.0 - tail), bell * 0.3989422804014327


def iota(dims, axis):
    return lax.broadcasted_iota(jnp.int32, dims, axis)


def spread_matrix(targets, col):
    hit = iota((TABLE_PAD, SPAN), 0) == targets - col
    return jnp.where(hit, 1.0, 0.0).astype(BF16)


def pieces_of(value, count):
    parts = []
    for _ in range(count):
        part = value.astype(BF16)
        parts.append(part)
        value = value - part.astype(F32)
    return parts


def route_kernel(capacity, routes_ref, gate_ref, grad_ref, order_ref, send_ref, row_ref, col_ref):
    rows = grad_ref.shape[0]
    slots = send_ref.shape[0]
    routes = routes_ref[...]
    chosen = jnp.where(iota((HEADS, rows), 0) == routes, 1.0, 0.0)
    upto = jnp.where(iota((rows, rows), 0) <= iota((rows, rows), 1), 1.0, 0.0).astype(BF16)
    running = nn(chosen.astype(BF16), upto)
    slot = jnp.sum(running * chosen, axis=0, keepdims=True) - 1.0
    expert = routes.astype(F32)
    place = (expert * capacity + slot).astype(jnp.int32)
    picks = jnp.where(iota((slots, rows), 0) == place, gate_ref[...].astype(F32), 0.0).astype(BF16)
    send_ref[...] = nn(picks, grad_ref[...]).astype(BF16)
    order = order_ref[...]
    both = jnp.concatenate(
        [jnp.broadcast_to(expert, (8, rows)), jnp.broadcast_to(slot, (8, rows))], axis=0
    ).astype(BF16)
    moved = nt(both, order)
    there = moved[0:1] * capacity + moved[8:9]
    row_ref[...] = there.astype(jnp.int32)
    same = iota((rows, rows), 0) == iota((rows, rows), 1)
    col_ref[...] = jnp.sum(jnp.where(same, there, 0.0), axis=1, keepdims=True).astype(jnp.int32)


def bias_kernel(table_ref, targets_ref, bias_ref, spread):
    table = jnp.concatenate(pieces_of(table_ref[...], 3), axis=0)
    for col in range(16):
        part = nn(table, spread_matrix(targets_ref[...], col % WINDOW))
        spread[col] = part[0:HEADS] + part[HEADS : 2 * HEADS] + part[2 * HEADS :]
    for head in range(HEADS):
        rows = spread[:, head, :]
        for row in range(WINDOW):
            start = (WINDOW - 1 - row) * WINDOW
            turned = pltpu.roll(rows, (SPAN - start) % SPAN, 1) if start else rows
            bias_ref[head, row * WINDOW : (row + 1) * WINDOW, :] = turned[:WINDOW, :TOKENS]


def table_kernel(lined, targets_ref, gain_one_ref, gain_two_ref, out_ref):
    grads = jnp.zeros((2 * HEADS, TABLE_PAD), F32)
    for col in range(WINDOW):
        value = jnp.concatenate(pieces_of(lined[:, col, :], 2), axis=0)
        grads = grads + nt(value, spread_matrix(targets_ref[...], col))
    grads = grads[:HEADS] + grads[HEADS:]
    out_ref[...] = jnp.zeros_like(out_ref)
    lines = [grads[head : head + 1, 128 * part : 128 * part + 128] for head in range(HEADS) for part in range(5)]
    for gain_ref in (gain_one_ref, gain_two_ref):
        lines += [gain_ref[:, 128 * part : 128 * part + 128] for part in range(4)]
    for number, line in enumerate(lines):
        high, low = pieces_of(line, 2)
        out_ref[number // 2, number % 2 : number % 2 + 1, :] = high.astype(F32)
        out_ref[number // 2, 2 + number % 2 : 3 + number % 2, :] = low.astype(F32)


def merge_kernel(mine_ref, other_ref, small_ref, out_ref):
    for owner in range(OWNERS):
        both = mine_ref[owner].astype(F32) + other_ref[owner].astype(F32)
        out_ref[owner, :, :512] = both.astype(BF16)
        out_ref[owner, :, 512:] = small_ref[owner].astype(BF16)


def sum_kernel(all_ref, out_ref):
    total = all_ref[0].astype(F32)
    for owner in range(1, OWNERS):
        total = total + all_ref[owner].astype(F32)
    small = total[:, 512:]
    small = small + pltpu.roll(small, 14, 0)
    high = small.astype(BF16).astype(F32)
    low = pltpu.roll(small - high, 2, 0)
    row = iota(small.shape, 0)
    small = jnp.where(row < 2, high, jnp.where(row < 4, low, 0.0))
    total = jnp.concatenate([total[:, :512], small], axis=1).astype(BF16)
    for owner in range(OWNERS):
        out_ref[owner] = total


def unpack_kernel(core_ref, mine_ref, other_ref, qkv_ref, proj_ref, small_ref):
    def place(half_ref, first):
        for row in range(16):
            here = slice(first + 16 * row, first + 16 * row + 16)
            for col in range(4):
                block = half_ref[4 * row + col].astype(F32)
                qkv_ref[here, 384 * col : 384 * col + 384] = block[:, :384]
                proj_ref[here, 128 * col : 128 * col + 128] = block[:, 384:512]

    @pl.when(core_ref[0] == 0)
    def _():
        place(mine_ref, 0)
        place(other_ref, 256)

    @pl.when(core_ref[0] != 0)
    def _():
        place(other_ref, 0)
        place(mine_ref, 256)

    for owner in range(OWNERS):
        small = mine_ref[owner, :, 512:].astype(F32) + other_ref[owner, :, 512:].astype(F32)
        small_ref[owner] = small + pltpu.roll(small, 14, 0)


def attend_kernel(
    image_ref, below_ref, order_ref, gain_ref, w_qkv_ref, w_proj_ref, bias_ref, mask_ref,
    prob_ref, qkv_ref, x_ref, normed_ref, mixed_ref, own_ref, send_ref, blended,
):
    group = pl.program_id(0)
    wins = x_ref.shape[0] // TOKENS
    lanes = iota((TOKENS, 128), 1) // 32

    @pl.when(group == 0)
    def _():
        order = order_ref[...]
        upper = nn(order, image_ref[...])
        lower = nn(order, below_ref[...])
        parts = []
        for win in range(wins):
            parts.append(upper[win * HALF : (win + 1) * HALF])
            parts.append(lower[win * HALF : (win + 1) * HALF])
        x = jnp.concatenate(parts, axis=0)
        x_ref[...] = x.astype(BF16)
        unit, _ = normalised(x)
        normed_ref[...] = (unit * gain_ref[...]).astype(BF16)
        normed = normed_ref[...]
        for pair in range(6):
            act = nn(normed, w_qkv_ref[:, 256 * pair : 256 * pair + 256]).astype(BF16)
            qkv_ref[2 * pair] = act[:, :128]
            qkv_ref[2 * pair + 1] = act[:, 128:]

    def scores_of(win):
        rows = slice(win * TOKENS, (win + 1) * TOKENS)
        query = qkv_ref[group, rows, :]
        key = qkv_ref[4 + group, rows, :]
        return [nt(key, jnp.where(lanes == head, query, jnp.zeros_like(query))) for head in range(4)]

    later = scores_of(0)
    for win in range(wins):
        scores = later
        later = scores_of(win + 1) if win + 1 < wins else None
        rows = slice(win * TOKENS, (win + 1) * TOKENS)
        value_t = jnp.transpose(qkv_ref[8 + group, rows, :].astype(F32)).astype(BF16)
        mask = mask_ref[int(win == wins - 1)]
        mixes = []
        for head in range(4):
            score = scores[head] * SCALE + (bias_ref[head] + mask)
            score = jnp.exp(score - jnp.max(score, axis=0, keepdims=True))
            prob = (score * (1.0 / jnp.sum(score, axis=0, keepdims=True))).astype(BF16)
            prob_ref[head, win] = prob
            mixes.append(nn(value_t[32 * head : 32 * head + 32], prob))
        mix = jnp.transpose(jnp.concatenate(mixes, axis=0))
        blended[group, rows, :] = mix.astype(BF16)

    @pl.when(group == pl.num_programs(0) - 1)
    def _():
        mixed = jnp.concatenate([blended[i] for i in range(4)], axis=1)
        mixed_ref[...] = mixed
        after = x_ref[...].astype(F32) + nn(mixed, w_proj_ref[...])
        kept = [after[win * TOKENS : win * TOKENS + HALF] for win in range(wins)]
        away = [after[win * TOKENS + HALF : (win + 1) * TOKENS] for win in range(wins)]
        own_ref[...] = jnp.concatenate(kept, axis=0)
        send_ref[...] = jnp.concatenate(away, axis=0).astype(BF16)


def weight_kernel(which_ref, pre_ref, hidden_ref, in_ref, grad_ref, *rest):
    step = pl.program_id(0)
    up, down = tn(pre_ref[0], in_ref[...]), tn(hidden_ref[0], grad_ref[...])
    for number, out_ref in enumerate(rest[-4:]):

        @pl.when(step == number)
        def _():
            if len(rest) > 4:
                out_ref[0] = (up + rest[number][0].astype(F32)).astype(BF16)
                out_ref[1] = (down + rest[number][1].astype(F32)).astype(BF16)
            else:
                out_ref[0] = up.astype(BF16)
                out_ref[1] = down.astype(BF16)


def weight_grads(which, grad_pre, hidden, recv_in, recv_grad, added=()):
    _, slots, chunk = hidden.shape
    width = recv_in.shape[1]
    strip = pl.BlockSpec((1, slots, chunk), lambda s, which: (which[0] * 4 + (which[1] + s) % 4, 0, 0))
    block = whole(2, chunk, width)
    return call(
        weight_kernel,
        (shape((2, chunk, width), BF16),) * 4,
        grid=(4,),
        in_specs=[strip, strip, whole(slots, width), whole(slots, width)] + [block] * len(added),
        out_specs=(block,) * 4,
        scalars=1,
        cost=LIGHT,
        limit=LARGE_LIMIT,
    )(which, grad_pre, hidden, recv_in, recv_grad, *added)


def relay_kernel(next_in_ref, last_in_ref, up_ref, down_ref, next_ref, last_ref):
    next_ref[0] = (next_in_ref[0].astype(F32) + up_ref[...].astype(F32)).astype(BF16)
    next_ref[1] = next_in_ref[1]
    last_ref[0] = last_in_ref[0]
    last_ref[1] = (last_in_ref[1].astype(F32) + down_ref[...].astype(F32)).astype(BF16)


def owned_kernel(own_ref, left_ref, right_ref, out_ref):
    total = own_ref[...].astype(F32) + left_ref[...].astype(F32) + right_ref[...].astype(F32)
    out_ref[...] = total.astype(BF16)


def assemble_kernel(which_ref, *refs):
    up_ref, down_ref = refs[-2:]
    for core in range(2):
        half = which_ref[0] if core == 0 else 1 - which_ref[0]
        own, left, right, far_up, far_down = refs[5 * core : 5 * core + 5]
        for step, up, down in (
            (0, own.at[0], own.at[1]),
            (3, left.at[0], left.at[1]),
            (1, right.at[0], right.at[1]),
            (2, far_up, far_down),
        ):
            chunk = half * 4 + (which_ref[1] + step) % 4
            here = pl.ds(pl.multiple_of(chunk * 256, 256), 256)
            up_ref[:, here] = jnp.transpose(up[...].astype(F32))
            down_ref[here, :] = down[...].astype(F32)


def dispatch_kernel(own_ref, above_ref, gain_ref, row_ref, send_ref, after_ref):
    after = jnp.concatenate([above_ref[...].astype(F32), own_ref[...]], axis=0)
    after_ref[...] = after
    unit, _ = normalised(after)
    normed = (unit * gain_ref[...]).astype(BF16)
    picks = iota((send_ref.shape[0], after.shape[0]), 0) == row_ref[...]
    send_ref[...] = nn(jnp.where(picks, 1.0, 0.0).astype(BF16), normed).astype(BF16)


def expert_kernel(in_ref, back_ref, w_up_ref, hidden_ref, pre_ref, out_ref, total, score):
    step = pl.program_id(0)
    rows = in_ref.shape[0]
    width = out_ref.shape[1] - 128

    @pl.when(step == 0)
    def _():
        total[...] = jnp.zeros_like(total)
        score[...] = jnp.zeros_like(score)

    w_up = w_up_ref[...]
    blocks = rows // EXPERT_ROWS
    places = [slice(block * EXPERT_ROWS, (block + 1) * EXPERT_ROWS) for block in range(blocks)]
    later = nn(in_ref[places[0], :], w_up)
    for block, here in enumerate(places):
        pre = later
        later = nn(in_ref[places[block + 1], :], w_up) if block + 1 < blocks else None
        cumulative, density = normal_of(pre)
        hidden = pre * cumulative
        back = back_ref[here, :].astype(F32)
        grad = (back * (cumulative + pre * density)).astype(BF16)
        for part in range(hidden_ref.shape[0]):
            lanes = slice(256 * part, 256 * part + 256)
            hidden_ref[part, here, :] = hidden[:, lanes].astype(BF16)
            pre_ref[part, here, :] = grad[:, lanes]
        product = hidden * back
        score[here, :] += sum(product[:, part : part + 128] for part in range(0, product.shape[1], 128))
        total[here, :] += nt(grad, w_up)

    @pl.when(step == pl.num_programs(0) - 1)
    def _():
        out_ref[:, :width] = total[...].astype(BF16)
        summed = jnp.sum(score[...], axis=1, keepdims=True)
        high = summed.astype(BF16).astype(F32)
        lane = iota((rows, 128), 1)
        tail = jnp.where(lane == 0, high, jnp.where(lane == 1, summed - high, 0.0))
        out_ref[:, width:] = tail.astype(BF16)


def combine_kernel(
    back_ref, col_ref, after_ref, grad_ref, order_ref, gain_ref, send_ref, own_ref, gain_out_ref, score_ref
):
    rows, width = after_ref.shape
    picks = iota((rows, back_ref.shape[0]), 1) == col_ref[...]
    picks = jnp.where(picks, 1.0, 0.0).astype(BF16)
    back = nn(picks, back_ref[...])
    score_ref[...] = back[:, width:]
    unit, scale = normalised(after_ref[...])
    grad, gain_grad = norm_backward(unit, scale, back[:, :width], gain_ref[...])
    gain_out_ref[...] = gain_grad
    order = order_ref[...]
    half = rows // 2
    send_ref[...] = (nn(order, grad_ref[:half, :]) + grad[:half]).astype(BF16)
    own_ref[...] = nn(order, grad_ref[half:, :]) + grad[half:]


def attend_backward_kernel(
    core_ref, own_ref, below_ref, order_t_ref, gain_ref, w_qkv_ref, w_proj_ref, qkv_ref, x_ref, normed_ref, mixed_ref,
    prob_ref, lined_ref, mine_ref, other_ref, kept_ref, send_ref, gain_out_ref, pair, cotangent, grad_mixed, grad_act,
    grad_qkv, grad_proj,
):
    group = pl.program_id(0)
    rows_all = x_ref.shape[0]
    wins = rows_all // TOKENS
    lanes = iota((TOKENS, 128), 1) // 32

    @pl.when(group == 0)
    def _():
        parts = []
        for win in range(wins):
            parts.append(own_ref[win * HALF : (win + 1) * HALF, :])
            parts.append(below_ref[...].astype(F32)[win * HALF : (win + 1) * HALF, :])
        cot = jnp.concatenate(parts, axis=0)
        cotangent[...] = cot
        mixed = nt(cot.astype(BF16), w_proj_ref[...]).astype(BF16)
        for i in range(4):
            grad_mixed[i] = mixed[:, 128 * i : 128 * i + 128]

    pair[...] = jnp.zeros_like(pair)

    def first_part(win):
        rows = slice(win * TOKENS, (win + 1) * TOKENS)
        value = qkv_ref[8 + group, rows, :]
        out = grad_mixed[group, rows, :]
        grad_probs, grad_value = [], None
        for head in range(4):
            own_out = jnp.where(lanes == head, out, jnp.zeros_like(out))
            grad_probs.append(nt(value, own_out))
            part = nn(prob_ref[head, win], own_out)
            grad_value = part if head == 0 else grad_value + part
        grad_act[8 + group, rows, :] = grad_value.astype(BF16)
        return grad_probs

    later = first_part(0)
    for win in range(wins):
        grad_probs = later
        later = first_part(win + 1) if win + 1 < wins else None
        rows = slice(win * TOKENS, (win + 1) * TOKENS)
        query = qkv_ref[group, rows, :]
        key_t = jnp.transpose(qkv_ref[4 + group, rows, :].astype(F32)).astype(BF16)
        grad_query, grad_key = [], None
        for head in range(4):
            own_query = jnp.where(lanes == head, query, jnp.zeros_like(query))
            prob = prob_ref[head, win].astype(F32)
            grad_prob = grad_probs[head].astype(BF16).astype(F32)
            weighted = prob * grad_prob
            grad_score = weighted - prob * jnp.sum(weighted, axis=0, keepdims=True)
            pair[head, :TOKENS, :TOKENS] += grad_score
            half_score = grad_score.astype(BF16)
            part = nn(half_score, own_query)
            grad_key = part if head == 0 else grad_key + part
            grad_query.append(nn(key_t[32 * head : 32 * head + 32], half_score))
        full_query = jnp.transpose(jnp.concatenate(grad_query, axis=0))
        grad_act[group, rows, :] = (full_query * SCALE).astype(BF16)
        grad_act[4 + group, rows, :] = (grad_key * SCALE).astype(BF16)

    for head in range(4):
        total = pair[head, (WINDOW - 1) * WINDOW : (WINDOW - 1) * WINDOW + 16, :]
        for row in range(WINDOW - 1):
            start = (WINDOW - 1 - row) * WINDOW
            total = total + pltpu.roll(pair[head, row * WINDOW : row * WINDOW + 16, :], start, 1)
        lined_ref[head] = total

    @pl.when(group == pl.num_programs(0) - 1)
    def _():
        act = jnp.concatenate([grad_act[i] for i in range(12)], axis=1)
        normed_t = jnp.transpose(normed_ref[...].astype(F32)).astype(BF16)
        mixed_t = jnp.transpose(mixed_ref[...].astype(F32)).astype(BF16)
        cot = cotangent[...]
        grad_proj[...] = nn(mixed_t, cot.astype(BF16)).astype(BF16)
        grad_qkv[...] = nn(normed_t, act).astype(BF16)

        def scatter(half_ref, first):
            for row in range(16):
                here = slice(first + 16 * row, first + 16 * row + 16)
                for col in range(4):
                    half_ref[4 * row + col, :, :384] = grad_qkv[here, 384 * col : 384 * col + 384]
                    half_ref[4 * row + col, :, 384:] = grad_proj[here, 128 * col : 128 * col + 128]

        @pl.when(core_ref[0] == 0)
        def _():
            scatter(mine_ref, 0)
            scatter(other_ref, 256)

        @pl.when(core_ref[0] != 0)
        def _():
            scatter(other_ref, 0)
            scatter(mine_ref, 256)

        grad_normed = nt(act, w_qkv_ref[...])
        unit, scale = normalised(x_ref[...].astype(F32))
        grad, gain_grad = norm_backward(unit, scale, grad_normed, gain_ref[...])
        gain_out_ref[...] = gain_grad
        total = cot + grad
        kept = [total[win * TOKENS : win * TOKENS + HALF] for win in range(wins)]
        away = [total[win * TOKENS + HALF : (win + 1) * TOKENS] for win in range(wins)]
        order_t = order_t_ref[...]
        kept_ref[...] = nn(order_t, jnp.concatenate(kept, axis=0).astype(BF16)).astype(BF16)
        send_ref[...] = nn(order_t, jnp.concatenate(away, axis=0).astype(BF16)).astype(BF16)


def on_device(
    image, grad_out, gate, routes, gain_one, w_qkv, w_proj, table, gain_two, w_fc1, w_fc2
):
    tile_count = lax.axis_size("tile")
    tile_index = lax.axis_index("tile")
    strip_height, columns, channels = image.shape[1:]
    wins = columns // WINDOW
    rows = strip_height * columns
    half = rows // 2
    capacity = 2 * rows // tile_count
    slots = tile_count * capacity
    ffn = w_fc1.shape[2]
    core = lax.axis_index("core").reshape(1).astype(jnp.int32)
    exchange = functools.partial(lax.all_to_all, split_axis=0, concat_axis=0, tiled=True)
    pick = half_order(wins)
    order = jnp.asarray(pick, BF16)
    order_t = jnp.asarray(pick.T, BF16)
    order_all = jnp.asarray(np.kron(np.eye(2), pick), BF16)
    targets = jnp.asarray(bias_targets())
    gain_one = gain_one.reshape(1, channels)
    gain_two = gain_two.reshape(1, channels)
    image_rows = image.reshape(rows, channels)
    grad_rows = grad_out.reshape(rows, channels)
    gate_row = gate.reshape(1, rows)

    below = shifted(image_rows[:half], "tile", -1)
    send_grad, place_row, place_col = call(
        functools.partial(route_kernel, capacity),
        (shape((slots, channels), BF16), shape((1, rows), jnp.int32), shape((rows, 1), jnp.int32)),
        cost=(700000000, 3000000, 0),
    )(routes.reshape(1, rows), gate_row, grad_rows, order_all)
    recv_grad = exchange(send_grad, "tile")
    bias = call(
        bias_kernel,
        shape((HEADS, TOKENS, TOKENS), F32),
        scratch=[pltpu.VMEM((16, HEADS, SPAN), F32)],
        cost=(400000000, 3000000, 0),
    )(jnp.pad(table, ((0, 0), (0, TABLE_PAD - table.shape[1]))), targets)
    mask = window_masks(jnp.reshape(tile_index == tile_count - 1, (1,)), wins)[wins - 2 :]

    head_block = pl.BlockSpec((4, wins, TOKENS, TOKENS), lambda g: (g, 0, 0, 0))
    pair_block = pl.BlockSpec((4, TOKENS, TOKENS), lambda g: (g, 0, 0))
    prob, qkv_act, windows, normed_one, mixed, own_after, send_after = call(
        attend_kernel,
        (
            shape((HEADS, wins, TOKENS, TOKENS), BF16),
            shape((12, rows, 128), BF16),
            shape((rows, channels), BF16),
            shape((rows, channels), BF16),
            shape((rows, channels), BF16),
            shape((half, channels), F32),
            shape((half, channels), BF16),
        ),
        grid=(4,),
        in_specs=[
            pl.BlockSpec((half, channels), lambda g: (1, 0)),
            whole(half, channels),
            whole(half, half),
            whole(1, channels),
            whole(channels, 3 * channels),
            whole(channels, channels),
            pair_block,
            whole(2, TOKENS, TOKENS),
        ],
        out_specs=(
            head_block,
            whole(12, rows, 128),
            whole(rows, channels),
            whole(rows, channels),
            whole(rows, channels),
            whole(half, channels),
            whole(half, channels),
        ),
        scratch=[pltpu.VMEM((4, rows, 128), BF16)],
        cost=(3000000000, 12000000, 2000000),
        limit=LARGE_LIMIT,
    )(image_rows, below, order, gain_one, w_qkv, w_proj, bias, mask)

    above = shifted(send_after, "tile", 1)
    send_in, after = call(
        dispatch_kernel,
        (shape((slots, channels), BF16), shape((rows, channels), F32)),
        cost=(700000000, 4000000, 0),
    )(own_after, above, gain_two, place_row)
    recv_in = exchange(send_in, "tile")

    w_up, w_down = w_fc1[0], w_fc2[0]
    grad_hidden = jnp.dot(recv_grad, w_down.T, preferred_element_type=F32).astype(BF16)
    chunk = 512
    strip = pl.BlockSpec((slots, chunk), lambda f: (0, f))
    split = pl.BlockSpec((chunk // 256, slots, 256), lambda f: (f, 0, 0))
    hidden, grad_pre, send_back = call(
        expert_kernel,
        (
            shape((ffn // 256, slots, 256), BF16),
            shape((ffn // 256, slots, 256), BF16),
            shape((slots, channels + 128), BF16),
        ),
        grid=(ffn // chunk,),
        in_specs=[whole(slots, channels), strip, pl.BlockSpec((channels, chunk), lambda f: (0, f))],
        out_specs=(split, split, whole(slots, channels + 128)),
        scratch=[pltpu.VMEM((slots, channels), F32), pltpu.VMEM((slots, 128), F32)],
        cost=(4800000000, 20000000, 5000000),
        limit=LARGE_LIMIT,
    )(recv_in, grad_hidden, w_up)
    recv_back = exchange(send_back, "tile")
    place_x = lax.axis_index("x").astype(jnp.int32)
    mine_at = jnp.stack([core[0], place_x])
    other_at = jnp.stack([1 - core[0], place_x])
    other_part = weight_grads(other_at, grad_pre, hidden, recv_in, recv_grad)
    other_part = [shifted(part, "core", 1) for part in other_part]
    mine_part = weight_grads(mine_at, grad_pre, hidden, recv_in, recv_grad, other_part)
    recv_back, mine_part = lax.optimization_barrier((recv_back, mine_part))
    chunk = shape(mine_part[0].shape, BF16)
    far_up = shifted(mine_part[2][0], "x", 1)
    far_down = shifted(mine_part[2][1], "x", -1)

    send_cot, own_cot, gain_two_part, score = call(
        combine_kernel,
        (
            shape((half, channels), BF16),
            shape((half, channels), F32),
            shape((1, channels), F32),
            shape((rows, 128), F32),
        ),
        cost=LIGHT,
    )(recv_back, place_col, after, grad_rows, order, gain_two)
    below_cot = shifted(send_cot, "tile", -1)
    to_right, to_left = call(relay_kernel, (chunk, chunk), cost=LIGHT)(mine_part[1], mine_part[3], far_up, far_down)
    below_cot, to_right, to_left = lax.optimization_barrier((below_cot, to_right, to_left))
    from_left, from_right = shifted(to_right, "x", 1), shifted(to_left, "x", -1)
    half_pieces = shape((OWNERS, 16, 512), BF16)
    lined, mine, other, kept, send_up, gain_one_part = call(
        attend_backward_kernel,
        (
            shape((HEADS, 16, SPAN), F32),
            half_pieces,
            half_pieces,
            shape((half, channels), BF16),
            shape((half, channels), BF16),
            shape((1, channels), F32),
        ),
        grid=(4,),
        in_specs=[
            pl.BlockSpec(memory_space=pltpu.SMEM),
            whole(half, channels),
            whole(half, channels),
            whole(half, half),
            whole(1, channels),
            whole(channels, 3 * channels),
            whole(channels, channels),
            whole(12, rows, 128),
            whole(rows, channels),
            whole(rows, channels),
            whole(rows, channels),
            head_block,
        ],
        out_specs=(
            pl.BlockSpec((4, 16, SPAN), lambda g: (g, 0, 0)),
            whole(OWNERS, 16, 512),
            whole(OWNERS, 16, 512),
            whole(half, channels),
            whole(half, channels),
            whole(1, channels),
        ),
        scratch=[
            pltpu.VMEM((4, TOKENS + 16, SPAN), F32),
            pltpu.VMEM((rows, channels), F32),
            pltpu.VMEM((4, rows, 128), BF16),
            pltpu.VMEM((12, rows, 128), BF16),
            pltpu.VMEM((channels, 3 * channels), BF16),
            pltpu.VMEM((channels, channels), BF16),
        ],
        cost=LIGHT,
        limit=LARGE_LIMIT,
    )(core, own_cot, below_cot, order_t, gain_one, w_qkv, w_proj, qkv_act, windows, normed_one, mixed, prob)
    lined, mine, other, send_up, gain_one_part, from_left, from_right = lax.optimization_barrier(
        (lined, mine, other, send_up, gain_one_part, from_left, from_right)
    )
    owned = call(owned_kernel, chunk, cost=LIGHT)(mine_part[0], from_left, from_right)
    left, right = shifted(owned, "x", 1), shifted(owned, "x", -1)
    upper = shifted(send_up, "tile", 1)
    other = shifted(other, "core", 1)
    small = call(
        table_kernel,
        shape((OWNERS, 16, 128), F32),
        cost=LIGHT,
    )(lined, targets, gain_one_part, gain_two_part)
    upper, other, small, left, right = lax.optimization_barrier((upper, other, small, left, right))
    pieces = shape((OWNERS, 16, 640), BF16)
    merged = call(merge_kernel, pieces, cost=(0, 4000000, 0))(mine, other, small)
    merged, score = lax.optimization_barrier((merged, score))
    parts = exchange(merged, SAME_CORE)
    score = (score[:, 0] + score[:, 1]).reshape(2, wins, SHIFT, WINDOW)
    score = score.transpose(0, 2, 1, 3).reshape(strip_height, columns)
    grad_gate = jnp.roll(score, SHIFT, axis=1) / gate[0].astype(F32)
    far_up, far_down = shifted(left[0], "x", 1), shifted(right[1], "x", -1)
    parts, far_up, far_down = lax.optimization_barrier((parts, far_up, far_down))
    summed = call(sum_kernel, pieces, cost=LIGHT)(parts)
    chunks = [owned, left, right, far_up, far_down]
    chunks = chunks + [shifted(value, "core", 1) for value in chunks]
    grad_image = jnp.concatenate([upper, kept], axis=0).reshape(image.shape)
    summed_up, summed_down = call(
        assemble_kernel,
        (shape((channels, ffn), F32), shape((ffn, channels), F32)),
        grid=(1,),
        in_specs=[pl.BlockSpec(memory_space=pltpu.SMEM)] + ([whole(*chunk.shape)] * 3 + [whole(*chunk.shape[1:])] * 2) * 2,
        out_specs=(whole(channels, ffn), whole(ffn, channels)),
        cost=LIGHT,
    )(mine_at, *chunks)
    gathered = exchange(summed, SAME_CORE)
    gathered, summed_up, summed_down, grad_image, grad_gate = lax.optimization_barrier(
        (gathered, summed_up, summed_down, grad_image, grad_gate)
    )
    grad_qkv, grad_proj, small_all = call(
        unpack_kernel,
        (
            shape((channels, 3 * channels), F32),
            shape((channels, channels), F32),
            shape((OWNERS, 16, 128), F32),
        ),
        grid=(1,),
        in_specs=[pl.BlockSpec(memory_space=pltpu.SMEM), whole(OWNERS, 16, 640), whole(OWNERS, 16, 640)],
        out_specs=(whole(channels, 3 * channels), whole(channels, channels), whole(OWNERS, 16, 128)),
        cost=(0, 7000000, 0),
    )(core, gathered, shifted(gathered, "core", 1))
    small_all = small_all[:, :2, :].reshape(2 * OWNERS, 128)
    first = HEADS * TABLE_PAD // 128
    grad_table = small_all[:first].reshape(HEADS, TABLE_PAD)[:, : table.shape[1]]
    grad_gain_one = small_all[first : first + 4].reshape(channels)
    grad_gain_two = small_all[first + 4 : first + 8].reshape(channels)
    return (
        grad_image,
        grad_gate.reshape(1, strip_height, columns),
        summed_up.reshape(1, channels, ffn),
        summed_down.reshape(1, ffn, channels),
        grad_qkv,
        grad_proj,
        grad_table,
        grad_gain_one,
        grad_gain_two,
    )


def solution(mesh):
    devices = mesh.devices
    split = jax.sharding.Mesh(devices.reshape(-1, 2, devices.shape[1]), ("x", "core", "tile"))
    return jax.shard_map(
        on_device,
        mesh=split,
        in_specs=(
            P(GROUP, "tile", None, None),
            P(GROUP, "tile", None, None),
            P(GROUP, "tile", None),
            P(GROUP, "tile", None, None),
            P(),
            P(),
            P(),
            P(),
            P(),
            P("tile", None, None),
            P("tile", None, None),
        ),
        out_specs=(
            P(GROUP, "tile", None, None),
            P(GROUP, "tile", None),
            P("tile", None, None),
            P("tile", None, None),
            P(),
            P(),
            P(),
            P(),
            P(),
        ),
        check_vma=False,
    )
```

```python
import functools

import jax
import jax.numpy as jnp
import numpy as np
from jax import lax
from jax.experimental import pallas as pl
from jax.experimental.pallas import tpu as pltpu
from jax.sharding import PartitionSpec as P

HEADS = 16
WINDOW = 12
SHIFT = 6
TOKENS = WINDOW * WINDOW
HALF = TOKENS // 2
SIDE = 2 * WINDOW - 1
SPAN = 384
TABLE_PAD = 640
SCALE = 32**-0.5
EXPERT_ROWS = 384
TAIL_BASE = 2.702702760696411
TAIL = (
    0.398942202,
    1.07827175,
    2.51046658,
    4.81238174,
    1.92840862,
    25.174448,
    -204.768677,
    384.889191,
    -241.165222,
)
VMEM_LIMIT = 40 * 1024 * 1024
LARGE_LIMIT = 60 * 1024 * 1024
F32 = jnp.float32
BF16 = jnp.bfloat16
GROUP = ("x", "core")
SAME_CORE = ("x", "tile")
OWNERS = 64
LIGHT = (1000000, 100000, 0)


def nn(a, b):
    return lax.dot_general(a, b, (((1,), (0,)), ((), ())), preferred_element_type=F32)


def nt(a, b):
    return lax.dot_general(a, b, (((1,), (1,)), ((), ())), preferred_element_type=F32)


def tn(a, b):
    return lax.dot_general(a, b, (((0,), (0,)), ((), ())), preferred_element_type=F32)


def call(kernel, outs, *, grid=None, in_specs=None, out_specs=None, scratch=(), cost=None, limit=VMEM_LIMIT, scalars=0):
    extra = dict(scratch_shapes=list(scratch))
    if scalars:
        spec = pltpu.PrefetchScalarGridSpec(
            num_scalar_prefetch=scalars, grid=grid, in_specs=in_specs, out_specs=out_specs, scratch_shapes=list(scratch)
        )
        extra = dict(grid_spec=spec)
    elif grid is not None:
        extra.update(grid=grid, in_specs=in_specs, out_specs=out_specs)
    if cost is not None:
        extra["cost_estimate"] = pl.CostEstimate(flops=cost[0], bytes_accessed=cost[1], transcendentals=cost[2])
    return pl.pallas_call(
        kernel, out_shape=outs, compiler_params=pltpu.CompilerParams(vmem_limit_bytes=limit), **extra
    )


def shape(dims, dtype):
    return jax.ShapeDtypeStruct(dims, dtype)


def whole(*dims):
    return pl.BlockSpec(dims, lambda *_: (0,) * len(dims))


def shifted(value, axis, steps):
    count = lax.axis_size(axis)
    pairs = [(source, (source + steps) % count) for source in range(count)]
    return lax.ppermute(value, axis, pairs)


def half_order(col_windows):
    columns = col_windows * WINDOW
    pick = np.zeros((SHIFT * columns, SHIFT * columns), np.float32)
    for win in range(col_windows):
        for row in range(SHIFT):
            for col in range(WINDOW):
                source = row * columns + (win * WINDOW + SHIFT + col) % columns
                pick[win * HALF + row * WINDOW + col, source] = 1.0
    return pick


def bias_targets():
    lane = np.arange(SPAN)
    target = (lane // WINDOW) * SIDE + lane % WINDOW + WINDOW - 1
    return np.where(lane < SIDE * WINDOW, target, -1000).astype(np.int32)[None]


def window_masks(row_last, col_windows):
    inner_pos = jnp.arange(TOKENS, dtype=jnp.int32)
    row_in = inner_pos // WINDOW
    col_in = inner_pos % WINDOW
    row_region = jnp.where(row_last[:, None], jnp.where(row_in < SHIFT, 1, 2)[None], 0)
    col_last = jnp.arange(col_windows, dtype=jnp.int32) == col_windows - 1
    col_region = jnp.where(col_last[:, None], jnp.where(col_in < SHIFT, 1, 2)[None], 0)
    region = (row_region[:, None, :] * 3 + col_region[None, :, :]).reshape(-1, TOKENS)
    same = region[:, :, None] == region[:, None, :]
    return jnp.where(same, 0.0, -100.0).astype(F32)


def normalised(values):
    mean = jnp.mean(values, axis=-1, keepdims=True)
    centred = values - mean
    scale = lax.rsqrt(jnp.mean(centred * centred, axis=-1, keepdims=True) + 1e-05)
    return centred * scale, scale


def norm_backward(unit, scale, grad, gain):
    weighted = grad * gain
    along = jnp.mean(weighted * unit, axis=-1, keepdims=True)
    flat = jnp.mean(weighted, axis=-1, keepdims=True)
    return scale * (weighted - flat - unit * along), jnp.sum(grad * unit, axis=0, keepdims=True)


def normal_of(values):
    bell = jnp.exp2(values * values * -0.7213475204444817)
    inverse = pl.reciprocal(TAIL_BASE + jnp.abs(values))
    ratio = inverse * TAIL[-1] + TAIL[-2]
    for factor in TAIL[-3::-1]:
        ratio = ratio * inverse + factor
    tail = bell * (ratio * inverse)
    return jnp.where(values < 0.0, tail, 1.0 - tail), bell * 0.3989422804014327


def iota(dims, axis):
    return lax.broadcasted_iota(jnp.int32, dims, axis)


def spread_matrix(targets, col):
    hit = iota((TABLE_PAD, SPAN), 0) == targets - col
    return jnp.where(hit, 1.0, 0.0).astype(BF16)


def pieces_of(value, count):
    parts = []
    for _ in range(count):
        part = value.astype(BF16)
        parts.append(part)
        value = value - part.astype(F32)
    return parts


def route_kernel(capacity, routes_ref, gate_ref, grad_ref, order_ref, send_ref, row_ref, col_ref):
    rows = grad_ref.shape[0]
    slots = send_ref.shape[0]
    routes = routes_ref[...]
    chosen = jnp.where(iota((HEADS, rows), 0) == routes, 1.0, 0.0)
    upto = jnp.where(iota((rows, rows), 0) <= iota((rows, rows), 1), 1.0, 0.0).astype(BF16)
    running = nn(chosen.astype(BF16), upto)
    slot = jnp.sum(running * chosen, axis=0, keepdims=True) - 1.0
    expert = routes.astype(F32)
    place = (expert * capacity + slot).astype(jnp.int32)
    picks = jnp.where(iota((slots, rows), 0) == place, gate_ref[...].astype(F32), 0.0).astype(BF16)
    send_ref[...] = nn(picks, grad_ref[...]).astype(BF16)
    order = order_ref[...]
    both = jnp.concatenate(
        [jnp.broadcast_to(expert, (8, rows)), jnp.broadcast_to(slot, (8, rows))], axis=0
    ).astype(BF16)
    moved = nt(both, order)
    there = moved[0:1] * capacity + moved[8:9]
    row_ref[...] = there.astype(jnp.int32)
    same = iota((rows, rows), 0) == iota((rows, rows), 1)
    col_ref[...] = jnp.sum(jnp.where(same, there, 0.0), axis=1, keepdims=True).astype(jnp.int32)


def bias_kernel(table_ref, targets_ref, bias_ref, spread):
    table = jnp.concatenate(pieces_of(table_ref[...], 3), axis=0)
    for col in range(16):
        part = nn(table, spread_matrix(targets_ref[...], col % WINDOW))
        spread[col] = part[0:HEADS] + part[HEADS : 2 * HEADS] + part[2 * HEADS :]
    for head in range(HEADS):
        rows = spread[:, head, :]
        for row in range(WINDOW):
            start = (WINDOW - 1 - row) * WINDOW
            turned = pltpu.roll(rows, (SPAN - start) % SPAN, 1) if start else rows
            bias_ref[head, row * WINDOW : (row + 1) * WINDOW, :] = turned[:WINDOW, :TOKENS]


def table_kernel(lined, targets_ref, gain_one_ref, gain_two_ref, out_ref):
    grads = jnp.zeros((2 * HEADS, TABLE_PAD), F32)
    for col in range(WINDOW):
        value = jnp.concatenate(pieces_of(lined[:, col, :], 2), axis=0)
        grads = grads + nt(value, spread_matrix(targets_ref[...], col))
    grads = grads[:HEADS] + grads[HEADS:]
    out_ref[...] = jnp.zeros_like(out_ref)
    lines = [grads[head : head + 1, 128 * part : 128 * part + 128] for head in range(HEADS) for part in range(5)]
    for gain_ref in (gain_one_ref, gain_two_ref):
        lines += [gain_ref[:, 128 * part : 128 * part + 128] for part in range(4)]
    for number, line in enumerate(lines):
        high, low = pieces_of(line, 2)
        out_ref[number // 2, number % 2 : number % 2 + 1, :] = high.astype(F32)
        out_ref[number // 2, 2 + number % 2 : 3 + number % 2, :] = low.astype(F32)


def merge_kernel(mine_ref, other_ref, small_ref, out_ref):
    for owner in range(OWNERS):
        both = mine_ref[owner].astype(F32) + other_ref[owner].astype(F32)
        out_ref[owner, :, :512] = both.astype(BF16)
        out_ref[owner, :, 512:] = small_ref[owner].astype(BF16)


def sum_kernel(all_ref, out_ref):
    total = all_ref[0].astype(F32)
    for owner in range(1, OWNERS):
        total = total + all_ref[owner].astype(F32)
    small = total[:, 512:]
    small = small + pltpu.roll(small, 14, 0)
    high = small.astype(BF16).astype(F32)
    low = pltpu.roll(small - high, 2, 0)
    row = iota(small.shape, 0)
    small = jnp.where(row < 2, high, jnp.where(row < 4, low, 0.0))
    total = jnp.concatenate([total[:, :512], small], axis=1).astype(BF16)
    for owner in range(OWNERS):
        out_ref[owner] = total


def unpack_kernel(core_ref, mine_ref, other_ref, qkv_ref, proj_ref, small_ref):
    def place(half_ref, first):
        for row in range(16):
            here = slice(first + 16 * row, first + 16 * row + 16)
            for col in range(4):
                block = half_ref[4 * row + col].astype(F32)
                qkv_ref[here, 384 * col : 384 * col + 384] = block[:, :384]
                proj_ref[here, 128 * col : 128 * col + 128] = block[:, 384:512]

    @pl.when(core_ref[0] == 0)
    def _():
        place(mine_ref, 0)
        place(other_ref, 256)

    @pl.when(core_ref[0] != 0)
    def _():
        place(other_ref, 0)
        place(mine_ref, 256)

    for owner in range(OWNERS):
        small = mine_ref[owner, :, 512:].astype(F32) + other_ref[owner, :, 512:].astype(F32)
        small_ref[owner] = small + pltpu.roll(small, 14, 0)


def attend_kernel(
    image_ref, below_ref, order_ref, gain_ref, w_qkv_ref, w_proj_ref, bias_ref, mask_ref,
    prob_ref, qkv_ref, x_ref, normed_ref, mixed_ref, own_ref, send_ref, blended,
):
    group = pl.program_id(0)
    wins = x_ref.shape[0] // TOKENS
    lanes = iota((TOKENS, 128), 1) // 32

    @pl.when(group == 0)
    def _():
        order = order_ref[...]
        upper = nn(order, image_ref[...])
        lower = nn(order, below_ref[...])
        parts = []
        for win in range(wins):
            parts.append(upper[win * HALF : (win + 1) * HALF])
            parts.append(lower[win * HALF : (win + 1) * HALF])
        x = jnp.concatenate(parts, axis=0)
        x_ref[...] = x.astype(BF16)
        unit, _ = normalised(x)
        normed_ref[...] = (unit * gain_ref[...]).astype(BF16)
        normed = normed_ref[...]
        for pair in range(6):
            act = nn(normed, w_qkv_ref[:, 256 * pair : 256 * pair + 256]).astype(BF16)
            qkv_ref[2 * pair] = act[:, :128]
            qkv_ref[2 * pair + 1] = act[:, 128:]

    def scores_of(win):
        rows = slice(win * TOKENS, (win + 1) * TOKENS)
        query = qkv_ref[group, rows, :]
        key = qkv_ref[4 + group, rows, :]
        return [nt(key, jnp.where(lanes == head, query, jnp.zeros_like(query))) for head in range(4)]

    later = scores_of(0)
    for win in range(wins):
        scores = later
        later = scores_of(win + 1) if win + 1 < wins else None
        rows = slice(win * TOKENS, (win + 1) * TOKENS)
        value_t = jnp.transpose(qkv_ref[8 + group, rows, :].astype(F32)).astype(BF16)
        mask = mask_ref[int(win == wins - 1)]
        mixes = []
        for head in range(4):
            score = scores[head] * SCALE + (bias_ref[head] + mask)
            score = jnp.exp(score - jnp.max(score, axis=0, keepdims=True))
            prob = (score * (1.0 / jnp.sum(score, axis=0, keepdims=True))).astype(BF16)
            prob_ref[head, win] = prob
            mixes.append(nn(value_t[32 * head : 32 * head + 32], prob))
        mix = jnp.transpose(jnp.concatenate(mixes, axis=0))
        blended[group, rows, :] = mix.astype(BF16)

    @pl.when(group == pl.num_programs(0) - 1)
    def _():
        mixed = jnp.concatenate([blended[i] for i in range(4)], axis=1)
        mixed_ref[...] = mixed
        after = x_ref[...].astype(F32) + nn(mixed, w_proj_ref[...])
        kept = [after[win * TOKENS : win * TOKENS + HALF] for win in range(wins)]
        away = [after[win * TOKENS + HALF : (win + 1) * TOKENS] for win in range(wins)]
        own_ref[...] = jnp.concatenate(kept, axis=0)
        send_ref[...] = jnp.concatenate(away, axis=0).astype(BF16)


def weight_kernel(which_ref, pre_ref, hidden_ref, in_ref, grad_ref, *rest):
    step = pl.program_id(0)
    up, down = tn(pre_ref[0], in_ref[...]), tn(hidden_ref[0], grad_ref[...])
    for number, out_ref in enumerate(rest[-4:]):

        @pl.when(step == number)
        def _():
            if len(rest) > 4:
                out_ref[0] = (up + rest[number][0].astype(F32)).astype(BF16)
                out_ref[1] = (down + rest[number][1].astype(F32)).astype(BF16)
            else:
                out_ref[0] = up.astype(BF16)
                out_ref[1] = down.astype(BF16)


def weight_grads(which, grad_pre, hidden, recv_in, recv_grad, added=()):
    _, slots, chunk = hidden.shape
    width = recv_in.shape[1]
    strip = pl.BlockSpec((1, slots, chunk), lambda s, which: (which[0] * 4 + (which[1] + s) % 4, 0, 0))
    block = whole(2, chunk, width)
    return call(
        weight_kernel,
        (shape((2, chunk, width), BF16),) * 4,
        grid=(4,),
        in_specs=[strip, strip, whole(slots, width), whole(slots, width)] + [block] * len(added),
        out_specs=(block,) * 4,
        scalars=1,
        cost=LIGHT,
        limit=LARGE_LIMIT,
    )(which, grad_pre, hidden, recv_in, recv_grad, *added)


def relay_kernel(next_in_ref, next_other_ref, last_in_ref, last_other_ref, up_ref, down_ref, next_ref, last_ref):
    ahead = next_in_ref[...].astype(F32) + next_other_ref[...].astype(F32)
    behind = last_in_ref[...].astype(F32) + last_other_ref[...].astype(F32)
    next_ref[0] = (ahead[0] + up_ref[...].astype(F32)).astype(BF16)
    next_ref[1] = ahead[1].astype(BF16)
    last_ref[0] = behind[0].astype(BF16)
    last_ref[1] = (behind[1] + down_ref[...].astype(F32)).astype(BF16)


def owned_kernel(own_ref, other_ref, left_ref, right_ref, out_ref):
    total = own_ref[...].astype(F32) + other_ref[...].astype(F32)
    total = total + left_ref[...].astype(F32) + right_ref[...].astype(F32)
    out_ref[...] = total.astype(BF16)


def assemble_kernel(which_ref, *refs):
    up_ref, down_ref = refs[-2:]
    for core in range(2):
        half = which_ref[0] if core == 0 else 1 - which_ref[0]
        own, left, right, far_up, far_down = refs[5 * core : 5 * core + 5]
        for step, up, down in (
            (0, own.at[0], own.at[1]),
            (3, left.at[0], left.at[1]),
            (1, right.at[0], right.at[1]),
            (2, far_up, far_down),
        ):
            chunk = half * 4 + (which_ref[1] + step) % 4
            here = pl.ds(pl.multiple_of(chunk * 256, 256), 256)
            up_ref[:, here] = jnp.transpose(up[...].astype(F32))
            down_ref[here, :] = down[...].astype(F32)


def dispatch_kernel(own_ref, above_ref, gain_ref, row_ref, send_ref, after_ref):
    after = jnp.concatenate([above_ref[...].astype(F32), own_ref[...]], axis=0)
    after_ref[...] = after
    unit, _ = normalised(after)
    normed = (unit * gain_ref[...]).astype(BF16)
    picks = iota((send_ref.shape[0], after.shape[0]), 0) == row_ref[...]
    send_ref[...] = nn(jnp.where(picks, 1.0, 0.0).astype(BF16), normed).astype(BF16)


def expert_kernel(in_ref, back_ref, w_up_ref, hidden_ref, pre_ref, out_ref, total, score):
    step = pl.program_id(0)
    rows = in_ref.shape[0]
    width = out_ref.shape[1] - 128

    @pl.when(step == 0)
    def _():
        total[...] = jnp.zeros_like(total)
        score[...] = jnp.zeros_like(score)

    w_up = w_up_ref[...]
    blocks = rows // EXPERT_ROWS
    places = [slice(block * EXPERT_ROWS, (block + 1) * EXPERT_ROWS) for block in range(blocks)]
    later = nn(in_ref[places[0], :], w_up)
    for block, here in enumerate(places):
        pre = later
        later = nn(in_ref[places[block + 1], :], w_up) if block + 1 < blocks else None
        cumulative, density = normal_of(pre)
        hidden = pre * cumulative
        back = back_ref[here, :].astype(F32)
        grad = (back * (cumulative + pre * density)).astype(BF16)
        for part in range(hidden_ref.shape[0]):
            lanes = slice(256 * part, 256 * part + 256)
            hidden_ref[part, here, :] = hidden[:, lanes].astype(BF16)
            pre_ref[part, here, :] = grad[:, lanes]
        product = hidden * back
        score[here, :] += sum(product[:, part : part + 128] for part in range(0, product.shape[1], 128))
        total[here, :] += nt(grad, w_up)

    @pl.when(step == pl.num_programs(0) - 1)
    def _():
        out_ref[:, :width] = total[...].astype(BF16)
        summed = jnp.sum(score[...], axis=1, keepdims=True)
        high = summed.astype(BF16).astype(F32)
        lane = iota((rows, 128), 1)
        tail = jnp.where(lane == 0, high, jnp.where(lane == 1, summed - high, 0.0))
        out_ref[:, width:] = tail.astype(BF16)


def combine_kernel(
    back_ref, col_ref, after_ref, grad_ref, order_ref, gain_ref, send_ref, own_ref, gain_out_ref, score_ref
):
    rows, width = after_ref.shape
    picks = iota((rows, back_ref.shape[0]), 1) == col_ref[...]
    picks = jnp.where(picks, 1.0, 0.0).astype(BF16)
    back = nn(picks, back_ref[...])
    score_ref[...] = back[:, width:]
    unit, scale = normalised(after_ref[...])
    grad, gain_grad = norm_backward(unit, scale, back[:, :width], gain_ref[...])
    gain_out_ref[...] = gain_grad
    order = order_ref[...]
    half = rows // 2
    send_ref[...] = (nn(order, grad_ref[:half, :]) + grad[:half]).astype(BF16)
    own_ref[...] = nn(order, grad_ref[half:, :]) + grad[half:]


def attend_backward_kernel(
    core_ref, own_ref, below_ref, order_t_ref, gain_ref, w_qkv_ref, w_proj_ref, qkv_ref, x_ref, normed_ref, mixed_ref,
    prob_ref, lined_ref, mine_ref, other_ref, kept_ref, send_ref, gain_out_ref, pair, cotangent, grad_mixed, grad_act,
    grad_qkv, grad_proj,
):
    group = pl.program_id(0)
    rows_all = x_ref.shape[0]
    wins = rows_all // TOKENS
    lanes = iota((TOKENS, 128), 1) // 32

    @pl.when(group == 0)
    def _():
        parts = []
        for win in range(wins):
            parts.append(own_ref[win * HALF : (win + 1) * HALF, :])
            parts.append(below_ref[...].astype(F32)[win * HALF : (win + 1) * HALF, :])
        cot = jnp.concatenate(parts, axis=0)
        cotangent[...] = cot
        mixed = nt(cot.astype(BF16), w_proj_ref[...]).astype(BF16)
        for i in range(4):
            grad_mixed[i] = mixed[:, 128 * i : 128 * i + 128]

    pair[...] = jnp.zeros_like(pair)

    def first_part(win):
        rows = slice(win * TOKENS, (win + 1) * TOKENS)
        value = qkv_ref[8 + group, rows, :]
        out = grad_mixed[group, rows, :]
        grad_probs, grad_value = [], None
        for head in range(4):
            own_out = jnp.where(lanes == head, out, jnp.zeros_like(out))
            grad_probs.append(nt(value, own_out))
            part = nn(prob_ref[head, win], own_out)
            grad_value = part if head == 0 else grad_value + part
        grad_act[8 + group, rows, :] = grad_value.astype(BF16)
        return grad_probs

    later = first_part(0)
    for win in range(wins):
        grad_probs = later
        later = first_part(win + 1) if win + 1 < wins else None
        rows = slice(win * TOKENS, (win + 1) * TOKENS)
        query = qkv_ref[group, rows, :]
        key_t = jnp.transpose(qkv_ref[4 + group, rows, :].astype(F32)).astype(BF16)
        grad_query, grad_key = [], None
        for head in range(4):
            own_query = jnp.where(lanes == head, query, jnp.zeros_like(query))
            prob = prob_ref[head, win].astype(F32)
            grad_prob = grad_probs[head].astype(BF16).astype(F32)
            weighted = prob * grad_prob
            grad_score = weighted - prob * jnp.sum(weighted, axis=0, keepdims=True)
            pair[head, :TOKENS, :TOKENS] += grad_score
            half_score = grad_score.astype(BF16)
            part = nn(half_score, own_query)
            grad_key = part if head == 0 else grad_key + part
            grad_query.append(nn(key_t[32 * head : 32 * head + 32], half_score))
        full_query = jnp.transpose(jnp.concatenate(grad_query, axis=0))
        grad_act[group, rows, :] = (full_query * SCALE).astype(BF16)
        grad_act[4 + group, rows, :] = (grad_key * SCALE).astype(BF16)

    for head in range(4):
        total = pair[head, (WINDOW - 1) * WINDOW : (WINDOW - 1) * WINDOW + 16, :]
        for row in range(WINDOW - 1):
            start = (WINDOW - 1 - row) * WINDOW
            total = total + pltpu.roll(pair[head, row * WINDOW : row * WINDOW + 16, :], start, 1)
        lined_ref[head] = total

    @pl.when(group == pl.num_programs(0) - 1)
    def _():
        act = jnp.concatenate([grad_act[i] for i in range(12)], axis=1)
        normed_t = jnp.transpose(normed_ref[...].astype(F32)).astype(BF16)
        mixed_t = jnp.transpose(mixed_ref[...].astype(F32)).astype(BF16)
        cot = cotangent[...]
        grad_proj[...] = nn(mixed_t, cot.astype(BF16)).astype(BF16)
        grad_qkv[...] = nn(normed_t, act).astype(BF16)

        def scatter(half_ref, first):
            for row in range(16):
                here = slice(first + 16 * row, first + 16 * row + 16)
                for col in range(4):
                    half_ref[4 * row + col, :, :384] = grad_qkv[here, 384 * col : 384 * col + 384]
                    half_ref[4 * row + col, :, 384:] = grad_proj[here, 128 * col : 128 * col + 128]

        @pl.when(core_ref[0] == 0)
        def _():
            scatter(mine_ref, 0)
            scatter(other_ref, 256)

        @pl.when(core_ref[0] != 0)
        def _():
            scatter(other_ref, 0)
            scatter(mine_ref, 256)

        grad_normed = nt(act, w_qkv_ref[...])
        unit, scale = normalised(x_ref[...].astype(F32))
        grad, gain_grad = norm_backward(unit, scale, grad_normed, gain_ref[...])
        gain_out_ref[...] = gain_grad
        total = cot + grad
        kept = [total[win * TOKENS : win * TOKENS + HALF] for win in range(wins)]
        away = [total[win * TOKENS + HALF : (win + 1) * TOKENS] for win in range(wins)]
        order_t = order_t_ref[...]
        kept_ref[...] = nn(order_t, jnp.concatenate(kept, axis=0).astype(BF16)).astype(BF16)
        send_ref[...] = nn(order_t, jnp.concatenate(away, axis=0).astype(BF16)).astype(BF16)


def on_device(
    image, grad_out, gate, routes, gain_one, w_qkv, w_proj, table, gain_two, w_fc1, w_fc2
):
    tile_count = lax.axis_size("tile")
    tile_index = lax.axis_index("tile")
    strip_height, columns, channels = image.shape[1:]
    wins = columns // WINDOW
    rows = strip_height * columns
    half = rows // 2
    capacity = 2 * rows // tile_count
    slots = tile_count * capacity
    ffn = w_fc1.shape[2]
    core = lax.axis_index("core").reshape(1).astype(jnp.int32)
    exchange = functools.partial(lax.all_to_all, split_axis=0, concat_axis=0, tiled=True)
    pick = half_order(wins)
    order = jnp.asarray(pick, BF16)
    order_t = jnp.asarray(pick.T, BF16)
    order_all = jnp.asarray(np.kron(np.eye(2), pick), BF16)
    targets = jnp.asarray(bias_targets())
    gain_one = gain_one.reshape(1, channels)
    gain_two = gain_two.reshape(1, channels)
    image_rows = image.reshape(rows, channels)
    grad_rows = grad_out.reshape(rows, channels)
    gate_row = gate.reshape(1, rows)

    below = shifted(image_rows[:half], "tile", -1)
    send_grad, place_row, place_col = call(
        functools.partial(route_kernel, capacity),
        (shape((slots, channels), BF16), shape((1, rows), jnp.int32), shape((rows, 1), jnp.int32)),
        cost=(700000000, 3000000, 0),
    )(routes.reshape(1, rows), gate_row, grad_rows, order_all)
    recv_grad = exchange(send_grad, "tile")
    bias = call(
        bias_kernel,
        shape((HEADS, TOKENS, TOKENS), F32),
        scratch=[pltpu.VMEM((16, HEADS, SPAN), F32)],
        cost=(400000000, 3000000, 0),
    )(jnp.pad(table, ((0, 0), (0, TABLE_PAD - table.shape[1]))), targets)
    mask = window_masks(jnp.reshape(tile_index == tile_count - 1, (1,)), wins)[wins - 2 :]

    head_block = pl.BlockSpec((4, wins, TOKENS, TOKENS), lambda g: (g, 0, 0, 0))
    pair_block = pl.BlockSpec((4, TOKENS, TOKENS), lambda g: (g, 0, 0))
    prob, qkv_act, windows, normed_one, mixed, own_after, send_after = call(
        attend_kernel,
        (
            shape((HEADS, wins, TOKENS, TOKENS), BF16),
            shape((12, rows, 128), BF16),
            shape((rows, channels), BF16),
            shape((rows, channels), BF16),
            shape((rows, channels), BF16),
            shape((half, channels), F32),
            shape((half, channels), BF16),
        ),
        grid=(4,),
        in_specs=[
            pl.BlockSpec((half, channels), lambda g: (1, 0)),
            whole(half, channels),
            whole(half, half),
            whole(1, channels),
            whole(channels, 3 * channels),
            whole(channels, channels),
            pair_block,
            whole(2, TOKENS, TOKENS),
        ],
        out_specs=(
            head_block,
            whole(12, rows, 128),
            whole(rows, channels),
            whole(rows, channels),
            whole(rows, channels),
            whole(half, channels),
            whole(half, channels),
        ),
        scratch=[pltpu.VMEM((4, rows, 128), BF16)],
        cost=(3000000000, 12000000, 2000000),
        limit=LARGE_LIMIT,
    )(image_rows, below, order, gain_one, w_qkv, w_proj, bias, mask)

    above = shifted(send_after, "tile", 1)
    send_in, after = call(
        dispatch_kernel,
        (shape((slots, channels), BF16), shape((rows, channels), F32)),
        cost=(700000000, 4000000, 0),
    )(own_after, above, gain_two, place_row)
    recv_in = exchange(send_in, "tile")

    w_up, w_down = w_fc1[0], w_fc2[0]
    grad_hidden = jnp.dot(recv_grad, w_down.T, preferred_element_type=F32).astype(BF16)
    chunk = 512
    strip = pl.BlockSpec((slots, chunk), lambda f: (0, f))
    split = pl.BlockSpec((chunk // 256, slots, 256), lambda f: (f, 0, 0))
    hidden, grad_pre, send_back = call(
        expert_kernel,
        (
            shape((ffn // 256, slots, 256), BF16),
            shape((ffn // 256, slots, 256), BF16),
            shape((slots, channels + 128), BF16),
        ),
        grid=(ffn // chunk,),
        in_specs=[whole(slots, channels), strip, pl.BlockSpec((channels, chunk), lambda f: (0, f))],
        out_specs=(split, split, whole(slots, channels + 128)),
        scratch=[pltpu.VMEM((slots, channels), F32), pltpu.VMEM((slots, 128), F32)],
        cost=(4800000000, 20000000, 5000000),
        limit=LARGE_LIMIT,
    )(recv_in, grad_hidden, w_up)
    recv_back = exchange(send_back, "tile")
    place_x = lax.axis_index("x").astype(jnp.int32)
    mine_at = jnp.stack([core[0], place_x])
    other_at = jnp.stack([1 - core[0], place_x])
    other_part = weight_grads(other_at, grad_pre, hidden, recv_in, recv_grad)
    other_part = [shifted(part, "core", 1) for part in other_part]
    mine_part = weight_grads(mine_at, grad_pre, hidden, recv_in, recv_grad)
    recv_back, mine_part, other_part = lax.optimization_barrier((recv_back, mine_part, other_part))
    chunk = shape(mine_part[0].shape, BF16)
    far = mine_part[2].astype(F32) + other_part[2].astype(F32)
    far_up = shifted(far[0].astype(BF16), "x", 1)
    far_down = shifted(far[1].astype(BF16), "x", -1)

    send_cot, own_cot, gain_two_part, score = call(
        combine_kernel,
        (
            shape((half, channels), BF16),
            shape((half, channels), F32),
            shape((1, channels), F32),
            shape((rows, 128), F32),
        ),
        cost=LIGHT,
    )(recv_back, place_col, after, grad_rows, order, gain_two)
    below_cot = shifted(send_cot, "tile", -1)
    to_right, to_left = call(relay_kernel, (chunk, chunk), cost=LIGHT, limit=LARGE_LIMIT)(
        mine_part[1], other_part[1], mine_part[3], other_part[3], far_up, far_down
    )
    below_cot, to_right, to_left = lax.optimization_barrier((below_cot, to_right, to_left))
    from_left, from_right = shifted(to_right, "x", 1), shifted(to_left, "x", -1)
    half_pieces = shape((OWNERS, 16, 512), BF16)
    lined, mine, other, kept, send_up, gain_one_part = call(
        attend_backward_kernel,
        (
            shape((HEADS, 16, SPAN), F32),
            half_pieces,
            half_pieces,
            shape((half, channels), BF16),
            shape((half, channels), BF16),
            shape((1, channels), F32),
        ),
        grid=(4,),
        in_specs=[
            pl.BlockSpec(memory_space=pltpu.SMEM),
            whole(half, channels),
            whole(half, channels),
            whole(half, half),
            whole(1, channels),
            whole(channels, 3 * channels),
            whole(channels, channels),
            whole(12, rows, 128),
            whole(rows, channels),
            whole(rows, channels),
            whole(rows, channels),
            head_block,
        ],
        out_specs=(
            pl.BlockSpec((4, 16, SPAN), lambda g: (g, 0, 0)),
            whole(OWNERS, 16, 512),
            whole(OWNERS, 16, 512),
            whole(half, channels),
            whole(half, channels),
            whole(1, channels),
        ),
        scratch=[
            pltpu.VMEM((4, TOKENS + 16, SPAN), F32),
            pltpu.VMEM((rows, channels), F32),
            pltpu.VMEM((4, rows, 128), BF16),
            pltpu.VMEM((12, rows, 128), BF16),
            pltpu.VMEM((channels, 3 * channels), BF16),
            pltpu.VMEM((channels, channels), BF16),
        ],
        cost=LIGHT,
        limit=LARGE_LIMIT,
    )(core, own_cot, below_cot, order_t, gain_one, w_qkv, w_proj, qkv_act, windows, normed_one, mixed, prob)
    lined, mine, other, send_up, gain_one_part, from_left, from_right = lax.optimization_barrier(
        (lined, mine, other, send_up, gain_one_part, from_left, from_right)
    )
    owned = call(owned_kernel, chunk, cost=LIGHT, limit=LARGE_LIMIT)(mine_part[0], other_part[0], from_left, from_right)
    left, right = shifted(owned, "x", 1), shifted(owned, "x", -1)
    upper = shifted(send_up, "tile", 1)
    other = shifted(other, "core", 1)
    small = call(
        table_kernel,
        shape((OWNERS, 16, 128), F32),
        cost=LIGHT,
    )(lined, targets, gain_one_part, gain_two_part)
    upper, other, small, left, right = lax.optimization_barrier((upper, other, small, left, right))
    pieces = shape((OWNERS, 16, 640), BF16)
    merged = call(merge_kernel, pieces, cost=(0, 4000000, 0))(mine, other, small)
    merged, score = lax.optimization_barrier((merged, score))
    parts = exchange(merged, SAME_CORE)
    score = (score[:, 0] + score[:, 1]).reshape(2, wins, SHIFT, WINDOW)
    score = score.transpose(0, 2, 1, 3).reshape(strip_height, columns)
    grad_gate = jnp.roll(score, SHIFT, axis=1) / gate[0].astype(F32)
    far_up, far_down = shifted(left[0], "x", 1), shifted(right[1], "x", -1)
    parts, far_up, far_down = lax.optimization_barrier((parts, far_up, far_down))
    summed = call(sum_kernel, pieces, cost=LIGHT)(parts)
    chunks = [owned, left, right, far_up, far_down]
    chunks = chunks + [shifted(value, "core", 1) for value in chunks]
    grad_image = jnp.concatenate([upper, kept], axis=0).reshape(image.shape)
    summed_up, summed_down = call(
        assemble_kernel,
        (shape((channels, ffn), F32), shape((ffn, channels), F32)),
        grid=(1,),
        in_specs=[pl.BlockSpec(memory_space=pltpu.SMEM)] + ([whole(*chunk.shape)] * 3 + [whole(*chunk.shape[1:])] * 2) * 2,
        out_specs=(whole(channels, ffn), whole(ffn, channels)),
        cost=LIGHT,
    )(mine_at, *chunks)
    gathered = exchange(summed, SAME_CORE)
    gathered, summed_up, summed_down, grad_image, grad_gate = lax.optimization_barrier(
        (gathered, summed_up, summed_down, grad_image, grad_gate)
    )
    grad_qkv, grad_proj, small_all = call(
        unpack_kernel,
        (
            shape((channels, 3 * channels), F32),
            shape((channels, channels), F32),
            shape((OWNERS, 16, 128), F32),
        ),
        grid=(1,),
        in_specs=[pl.BlockSpec(memory_space=pltpu.SMEM), whole(OWNERS, 16, 640), whole(OWNERS, 16, 640)],
        out_specs=(whole(channels, 3 * channels), whole(channels, channels), whole(OWNERS, 16, 128)),
        cost=(0, 7000000, 0),
    )(core, gathered, shifted(gathered, "core", 1))
    small_all = small_all[:, :2, :].reshape(2 * OWNERS, 128)
    first = HEADS * TABLE_PAD // 128
    grad_table = small_all[:first].reshape(HEADS, TABLE_PAD)[:, : table.shape[1]]
    grad_gain_one = small_all[first : first + 4].reshape(channels)
    grad_gain_two = small_all[first + 4 : first + 8].reshape(channels)
    return (
        grad_image,
        grad_gate.reshape(1, strip_height, columns),
        summed_up.reshape(1, channels, ffn),
        summed_down.reshape(1, ffn, channels),
        grad_qkv,
        grad_proj,
        grad_table,
        grad_gain_one,
        grad_gain_two,
    )


def solution(mesh):
    devices = mesh.devices
    split = jax.sharding.Mesh(devices.reshape(-1, 2, devices.shape[1]), ("x", "core", "tile"))
    return jax.shard_map(
        on_device,
        mesh=split,
        in_specs=(
            P(GROUP, "tile", None, None),
            P(GROUP, "tile", None, None),
            P(GROUP, "tile", None),
            P(GROUP, "tile", None, None),
            P(),
            P(),
            P(),
            P(),
            P(),
            P("tile", None, None),
            P("tile", None, None),
        ),
        out_specs=(
            P(GROUP, "tile", None, None),
            P(GROUP, "tile", None),
            P("tile", None, None),
            P("tile", None, None),
            P(),
            P(),
            P(),
            P(),
            P(),
        ),
        check_vma=False,
    )
```
